32 devices in a mesh: dp: 2 (over y), seq: 16 (over z, x, core).
Axes of the slice: x: 2, y: 2, z: 4, core: 2. Of those that a mesh axis runs over, the one named last changes fastest.
Arguments:
- tokens: bfloat16 [2, 4096, 768], P('dp', 'seq'), may hold values from -6 to 6
- segment_ids: int32 [2, 4096], P('dp', 'seq'), may hold values from 0 to 7, never falling along the last dimension, each value on 1 to 2048 neighbouring positions
- features: bfloat16 [12, 64, 256], replicated, may hold values from -6 to 6
- query_weight: bfloat16 [768, 768], replicated, may hold values from -0.15625 to 0.15625
- key_weight: bfloat16 [768, 768], replicated, may hold values from -0.15625 to 0.15625
- value_weight: bfloat16 [768, 768], replicated, may hold values from -0.21875 to 0.21875
- out_weight: bfloat16 [768, 768], replicated, may hold values from -0.875 to 0.875
- up_weight: bfloat16 [768, 3072], replicated, may hold values from -0.21875 to 0.21875
- down_weight: bfloat16 [3072, 768], replicated, may hold values from -0.109375 to 0.109375
- first_gain: float32 [768], replicated, may hold values from 0.1 to 1.9
- first_bias: float32 [768], replicated, may hold values from -3 to 3
- second_gain: float32 [768], replicated, may hold values from 0.1 to 1.9
- second_bias: float32 [768], replicated, may hold values from -3 to 3
- cotangent: bfloat16 [2, 4096, 768], P('dp', 'seq'), may hold values from -6 to 6
Outputs:
- output: bfloat16 [2, 4096, 768], P('dp', 'seq')
- grad_tokens: bfloat16 [2, 4096, 768], P('dp', 'seq')
- grad_query: float32 [768, 768], replicated
- grad_key: float32 [768, 768], replicated
- grad_value: float32 [768, 768], replicated
- grad_out: float32 [768, 768], replicated
- grad_up: float32 [768, 3072], replicated
- grad_down: float32 [3072, 768], replicated
- grad_first_gain: float32 [768], replicated
- grad_first_bias: float32 [768], replicated
- grad_second_gain: float32 [768], replicated
- grad_second_bias: float32 [768], replicated
The draws below stay inside these ranges and needn't reach their ends.
Inputs may be any that keep to these rules, and one draw needn't show every extreme that they name: `segment_ids`: in each row the ids never fall, every id from 0 to 7 occurs, each on 1 to 2048 positions, and one on exactly 2048.
All inputs are finite; a program needn't handle non-finite values.
Results may differ from the reference program's by a relative error of at most 0.02.
Values sent between devices are 32-bit elements; how exact they have to be, the bound alone decides.
No kernel may reach another device: no remote copies, remote signals or barrier semaphores. Data moves between devices by JAX's collectives and lax.ppermute only.
A program may use at most 320 MiB of HBM per device.

```python
import math
import jax
import jax.numpy as jnp
import numpy as np
from jax import lax

D = 768
HEADS = 12
HD = 64
FF = 3072
FEATS = 256
SEGS = 8
LEN = 4096
ROWS = 2
SEG_MOST = 2048


def spiked(values, own_key, source, target, shards_of, factor):
    owner, partner = [(jnp.arange(values.shape[position]) // (values.shape[position] // shards_of)).reshape([-1 if axis == position else 1 for axis in range(values.ndim)]) for position in (source, target)]
    chosen = jax.random.permutation(own_key, shards_of)[partner]
    strong = (owner == chosen) | (owner == (partner + shards_of // 2) % shards_of)
    return jnp.where(strong, factor * values, values)


def shard_levels(stream_key, shape, split, low, largest):
    loudness, own = 1.0, jax.random.fold_in(stream_key, 6)
    for axis_at, parts in split:
        draws = jnp.exp(jax.random.uniform(jax.random.fold_in(own, axis_at), (parts,), jnp.float32, low / len(split), largest / len(split)))
        loudness = loudness * jnp.repeat(draws, shape[axis_at] // parts).reshape([-1 if axis == axis_at else 1 for axis in range(len(shape))])
    return loudness


def split_up(number_of, total, bound, slope):
    loads = [(1 << 20) // math.isqrt(rank ** slope) + 1 for rank in range(2, number_of + 1)]
    rest, counts = total - bound - (number_of - 1), [1] * (number_of - 1)
    while rest > 0:
        candidates = [i for i in range(number_of - 1) if counts[i] < bound]
        whole, left = sum([loads[i] for i in candidates]), rest
        for i in candidates:
            more = min(bound - counts[i], max(1, left * loads[i] // whole), rest)
            counts[i] = counts[i] + more
            rest = rest - more
    return np.array([bound] + counts)


def ragged(rng, amount, total, bound, lean):
    if amount == 2:
        one = jax.random.randint(rng, (), max(1, total - bound), min(bound, total - 1) + 1)
        return jnp.stack([one, total - one])
    lengths = jnp.asarray(split_up(amount, total, bound, lean), jnp.int32)
    pairs = (amount - 1) // 2
    source_of, taker = lengths[1:1 + 2 * pairs:2], lengths[2:2 + 2 * pairs:2]
    slack = jnp.minimum(source_of - 1, bound - taker)
    moved = jax.random.randint(jax.random.fold_in(rng, 1), (pairs,), 0, 1 << 20) % (slack + 1)
    lengths = lengths.at[1:1 + 2 * pairs:2].set(source_of - moved).at[2:2 + 2 * pairs:2].set(taker + moved)
    return lengths[jax.random.permutation(jax.random.fold_in(rng, 2), amount)]


def normal_values(rng, dims, spread, limit, split=(), kind=jnp.bfloat16):
    gain = shard_levels(rng, dims, split, -0.22, 0.18) if split else 1.0
    drawn = jax.random.normal(rng, dims, jnp.float32) * spread * gain
    return jnp.minimum(jnp.maximum(drawn, -limit), limit).astype(kind)


def heavy_noise(rng, extent, deviation, limit, split, heavy, kind=jnp.bfloat16):
    values = deviation * jax.random.normal(rng, extent, jnp.float32)
    if split:
        values = values * shard_levels(rng, extent, split, -0.22, 0.18)
    return jnp.clip(spiked(values, jax.random.fold_in(rng, 3), *heavy), -limit, limit).astype(kind)


def setup_inputs(seed: int = 0) -> dict:
    splits = jax.random.split(jax.random.key(seed), 15)
    return {
        "tokens": normal_values(splits[0], (ROWS, LEN, D), 1.0, 6.0, ((0, 2), (1, 16))),
        "segment_ids": jax.vmap(lambda own: jnp.searchsorted(jnp.cumsum(ragged(own, SEGS, LEN, SEG_MOST, 2)), jnp.arange(LEN), side="right"))(jax.random.split(splits[1], ROWS)).reshape((ROWS, LEN)).astype(jnp.int32),
        "features": normal_values(splits[2], (HEADS, HD, FEATS), 1.0, 6.0),
        "query_weight": normal_values(splits[3], (D, D), (2 * D) ** -0.5, 0.15625),
        "key_weight": normal_values(splits[4], (D, D), (2 * D) ** -0.5, 0.15625),
        "value_weight": normal_values(splits[5], (D, D), D ** -0.5, 0.21875),
        "out_weight": normal_values(splits[6], (D, D), (D // 16) ** -0.5, 0.875),
        "up_weight": normal_values(splits[7], (D, FF), D ** -0.5, 0.21875),
        "down_weight": normal_values(splits[8], (FF, D), FF ** -0.5, 0.109375),
        "first_gain": jnp.clip(1.0 + 0.18 * jax.random.normal(splits[9], (D,), jnp.float32), 0.1, 1.9),
        "first_bias": normal_values(splits[10], (D,), 0.5, 3.0, (), jnp.float32),
        "second_gain": jnp.clip(1.0 + 0.18 * jax.random.normal(splits[11], (D,), jnp.float32), 0.1, 1.9),
        "second_bias": normal_values(splits[12], (D,), 0.5, 3.0, (), jnp.float32),
        "cotangent": heavy_noise(splits[13], (ROWS, LEN, D), 1.0, 6.0, ((0, 2), (1, 16)), (1, 2, 16, 2.0)),
    }


EPSILON = 1e-06
HIGHEST = lax.Precision.HIGHEST

@jax.custom_vjp
def low(v):
    return lax.optimization_barrier(v.astype(jnp.bfloat16)).astype(jnp.float32)

@jax.custom_vjp
def low_back(v):
    return v

def low_keep(v):
    return (low(v), None)

def low_pass(kept, grad):
    return (grad,)

def back_keep(v):
    return (v, None)

def back_low(kept, grad):
    return (low(grad),)
low.defvjp(low_keep, low_pass)
low_back.defvjp(back_keep, back_low)

def layer_norm(hidden, norm_gain, norm_bias):
    row_mean = lax.optimization_barrier(jnp.mean(hidden, -1, keepdims=True))
    centered = hidden - row_mean
    variance = lax.optimization_barrier(jnp.mean(centered * centered, -1, keepdims=True))
    return centered * lax.rsqrt(variance + EPSILON) * norm_gain + norm_bias

def feature_map(projected, features):
    rounded = low(low_back(projected))
    inner_u = low_back(jnp.einsum('the,hem->thm', rounded, features, precision=HIGHEST))
    square = lax.optimization_barrier(jnp.sum(rounded * rounded, -1, keepdims=True))
    return low(jnp.exp(inner_u * HD ** (-0.25) - 0.5 * HD ** (-0.5) * square) * FEATS ** (-0.5))

def forward_row(x_row, onehot, features, query_weight, key_weight, value_weight, out_weight, up_weight, down_weight, first_gain, first_bias, second_gain, second_bias):
    positions = x_row.shape[0]

    def split_heads(weight):
        return jnp.dot(x_row, weight, precision=HIGHEST).reshape(positions, HEADS, HD)
    feat_q = feature_map(split_heads(query_weight), features)
    feat_k = feature_map(split_heads(key_weight), features)
    values_b = low(low_back(split_heads(value_weight)))
    numer = jnp.zeros((positions, HEADS, HD), jnp.float32)
    denom = jnp.zeros((positions, HEADS), jnp.float32)
    for segment in range(SEGS):
        select = onehot[:, segment][:, None, None]
        masked_k = feat_k * select
        kv_sum = jnp.einsum('thm,the->hme', masked_k, values_b, precision=HIGHEST)
        z_sum = lax.optimization_barrier(jnp.sum(masked_k, 0))
        kv_low = low(low_back(kv_sum))
        numer = numer + select * jnp.einsum('thm,hme->the', feat_q, kv_low, precision=HIGHEST)
        denom = denom + select[:, :, 0] * jnp.einsum('thm,hm->th', feat_q, z_sum, precision=HIGHEST)
    numer = low_back(numer)
    attention = low((numer / denom[:, :, None]).reshape(positions, D))
    hidden_one = x_row + low_back(jnp.dot(attention, out_weight, precision=HIGHEST))
    normed_one = layer_norm(hidden_one, first_gain, first_bias)
    inner_f = low_back(jnp.dot(low(normed_one), up_weight, precision=HIGHEST))
    activated = low(jax.nn.gelu(inner_f, approximate=False))
    branch = low_back(jnp.dot(activated, down_weight, precision=HIGHEST))
    return layer_norm(normed_one + branch, second_gain, second_bias)

def reference(tokens, segment_ids, features, query_weight, key_weight, value_weight, out_weight, up_weight, down_weight, first_gain, first_bias, second_gain, second_bias, cotangent):
    weights = (query_weight.astype(jnp.float32), key_weight.astype(jnp.float32), value_weight.astype(jnp.float32), out_weight.astype(jnp.float32), up_weight.astype(jnp.float32), down_weight.astype(jnp.float32), first_gain.astype(jnp.float32), first_bias.astype(jnp.float32), second_gain.astype(jnp.float32), second_bias.astype(jnp.float32))
    feat_mats = features.astype(jnp.float32)
    labels = jnp.arange(SEGS, dtype=jnp.int32)

    def one_row(totals, row_data):
        x_row, seg_row, cot_row = row_data
        onehot = (seg_row[:, None] == labels[None, :]).astype(jnp.float32)

        def run_row(x_in, *params):
            return forward_row(x_in, onehot, feat_mats, *params)
        result, pull_back = jax.vjp(run_row, x_row.astype(jnp.float32), *weights)
        grads = pull_back(cot_row.astype(jnp.float32))
        totals = tuple((acc + new for acc, new in zip(totals, grads[1:])))
        return (totals, (result.astype(jnp.bfloat16), grads[0].astype(jnp.bfloat16)))
    start = tuple((jnp.zeros_like(w) for w in weights))
    totals, (outputs, grad_in) = lax.scan(one_row, start, (tokens, segment_ids, cotangent))
    return (outputs, grad_in, totals[0], totals[1], totals[2], totals[3], totals[4], totals[5], totals[6], totals[7], totals[8], totals[9])
```

```python
from functools import partial

import jax
import jax.numpy as jnp
from jax import lax
from jax.sharding import PartitionSpec as P

SEG_MOST = 2048
EPSILON = 1e-06
AXES = ("dp", "seq")
BF = jnp.bfloat16
F32 = jnp.float32


def mm(a, b):
    return jnp.dot(a, b, preferred_element_type=F32)


def mm_nt(a, b):
    return lax.dot_general(a, b, (((1,), (1,)), ((), ())), preferred_element_type=F32)


def mm_tn(a, b):
    return lax.dot_general(a, b, (((0,), (0,)), ((), ())), preferred_element_type=F32)


def dslice(a, start, size, axis=0):
    return lax.dynamic_slice_in_dim(a, start, size, axis)


class Net:
    def __init__(self, n_dp, n_seq):
        self.n_dp, self.n_seq = n_dp, n_seq
        self.nz = 4
        self.nx = n_seq // 8
        self.fast = n_dp == 2 and n_seq == 16
        seq = lax.axis_index("seq")
        self.y = lax.axis_index("dp")
        self.core = seq % 2
        self.x = (seq // 2) % self.nx
        self.z = seq // (2 * self.nx)
        self.seq = seq
        self.one = jnp.where(seq < 0, 0.5, 1.0).astype(F32)

    def perm(self, move):
        pairs = []
        for y in range(self.n_dp):
            for s in range(self.n_seq):
                target = move(y, s // (2 * self.nx), (s // 2) % self.nx, s % 2)
                if target is not None:
                    ty, tz, tx, tc = target
                    pairs.append((y * self.n_seq + s, ty * self.n_seq + (tz * self.nx + tx) * 2 + tc))
        return pairs

    def send(self, value, move):
        return lax.ppermute(value, AXES, self.perm(move))

    def over_core(self, value):
        return self.send(value, lambda y, z, x, c: (y, z, x, 1 - c))

    def swap_b(self, value):
        got = self.over_core(value.astype(F32))
        return (got * self.one).astype(BF)

    def over_x(self, value, inner=False):
        return self.send(
            value, lambda y, z, x, c: None if inner and z in (0, 3) else (y, z, 1 - x, c)
        )

    def over_y(self, value, inner=False):
        return self.send(
            value, lambda y, z, x, c: None if inner and z in (0, 3) else (1 - y, z, x, c)
        )

    def z_up(self, value):
        return self.send(value, lambda y, z, x, c: (y, z + 1, x, c) if z < 3 else None)

    def z_down(self, value):
        return self.send(value, lambda y, z, x, c: (y, z - 1, x, c) if z > 0 else None)

    def z_in(self, value):
        return self.send(
            value, lambda y, z, x, c: (y, (1, 1, 2, 2)[z], x, c) if z in (0, 3) else None
        )

    def z_out(self, value):
        return self.send(
            value, lambda y, z, x, c: (y, (0, 0, 3, 3)[z], x, c) if z in (1, 2) else None
        )

    def z_swap(self, value):
        return self.send(value, lambda y, z, x, c: (y, 3 - z, x, c) if z in (1, 2) else None)

    def shift(self, value, step):
        chips = self.n_seq // 2
        pairs = []
        for y in range(self.n_dp):
            for s in range(self.n_seq):
                if 0 <= s // 2 + step < chips:
                    pairs.append((y * self.n_seq + s, y * self.n_seq + s + 2 * step))
        return lax.ppermute(value, AXES, pairs)


def keep_if(flag, value):
    return jnp.where(flag[:, None, None], value, 0.0)


def exchange(net, lead, tail, first, last, chip_len):
    rows = first.shape[0]
    if not net.fast:
        before = [jnp.zeros_like(part) for part in lead]
        behind = [jnp.zeros_like(part) for part in lead]
        up = (tail, last)
        down = (lead, first)
        for _ in range(min(net.n_seq // 2 - 1, -(-SEG_MOST // chip_len))):
            up = jax.tree.map(lambda part: net.shift(part, 1), up)
            down = jax.tree.map(lambda part: net.shift(part, -1), down)
            before = [b + keep_if(up[1] == first, part) for b, part in zip(before, up[0])]
            behind = [b + keep_if(down[1] == last, part) for b, part in zip(behind, down[0])]
        return before, behind
    at_one = net.x == 1

    def pick(pair, flag):
        return jnp.where(flag, pair[1], pair[0])

    ids = jnp.stack([first, last])
    ids_other = net.over_x(ids)
    mine = [pick(lead, at_one), pick(tail, at_one)]
    theirs = [net.over_x(pick(lead, ~at_one)), net.over_x(pick(tail, ~at_one))]
    lead0, lead1 = jnp.where(at_one, theirs[0], mine[0]), jnp.where(at_one, mine[0], theirs[0])
    tail0, tail1 = jnp.where(at_one, theirs[1], mine[1]), jnp.where(at_one, mine[1], theirs[1])
    first0, first1 = jnp.where(at_one, ids_other[0], first), jnp.where(at_one, first, ids_other[0])
    last0, last1 = jnp.where(at_one, ids_other[1], last), jnp.where(at_one, last, ids_other[1])
    up = tail1 + keep_if(last0 == last1, tail0)
    down = lead0 + keep_if(first1 == first0, lead1)
    up_id, down_id = last1, first0
    before = jnp.zeros_like(up)
    behind = jnp.zeros_like(up)
    for _ in range(min(net.nz - 1, -(-SEG_MOST // (2 * chip_len)))):
        up, up_id = net.z_up(up), net.z_up(up_id)
        down, down_id = net.z_down(down), net.z_down(down_id)
        before = before + keep_if(up_id == first0, up)
        behind = behind + keep_if(down_id == last1, down)
    before0, behind1 = before, behind
    behind0 = keep_if(last0 == first1, lead1) + keep_if(last0 == last1, behind)
    before1 = keep_if(first1 == last0, tail0) + keep_if(first1 == first0, before)
    own_before = jnp.where(at_one, before1, before0)
    own_behind = jnp.where(at_one, behind1, behind0)
    got_before = net.over_x(jnp.where(at_one, before0, before1))
    got_behind = net.over_x(jnp.where(at_one, behind0, behind1))
    befores = [jnp.where(at_one, got_before, own_before), jnp.where(at_one, own_before, got_before)]
    behinds = [jnp.where(at_one, got_behind, own_behind), jnp.where(at_one, own_behind, got_behind)]
    return befores, behinds


def pair_scatter(value, place, move):
    half = value.shape[0] // 2
    got = move(dslice(value, (1 - place) * half, half))
    return dslice(value, place * half, half) + got


def pair_gather(value, place, move):
    got = move(value)
    flag = place == 0
    return jnp.concatenate([jnp.where(flag, value, got), jnp.where(flag, got, value)], 0)


def all_reduce(net, value, order):
    z_side = jnp.where(net.z >= 2, 1, 0)
    inner = (net.z == 1) | (net.z == 2)
    seen_z = False
    for axis in order:
        if axis == "z":
            value = value + net.z_in(value)
            value = pair_scatter(value, z_side, net.z_swap)
            seen_z = True
        elif axis == "x":
            value = pair_scatter(value, net.x, partial(net.over_x, inner=seen_z))
        else:
            value = pair_scatter(value, net.y, partial(net.over_y, inner=seen_z))
    for axis in order[::-1]:
        if axis == "z":
            value = pair_gather(value, z_side, net.z_swap)
            got = net.z_out(value)
            value = jnp.where(inner, value, got)
            seen_z = False
        elif axis == "x":
            value = pair_gather(value, net.x, partial(net.over_x, inner=seen_z))
        else:
            value = pair_gather(value, net.y, partial(net.over_y, inner=seen_z))
    return value


def small_sum(net, value):
    if not net.fast:
        return lax.psum(value, AXES)
    value = value + net.over_core(value)
    value = value + net.over_x(value)
    value = value + net.over_y(value)
    value = value + net.send(value, lambda y, z, x, c: (y, z ^ 1, x, c))
    return value + net.send(value, lambda y, z, x, c: (y, z ^ 2, x, c))


def join_cores(net, half, axis):
    got = net.over_core(half)
    flag = net.core == 0
    return jnp.concatenate([jnp.where(flag, half, got), jnp.where(flag, got, half)], axis)


def total(net, half, axis, parts):
    if not net.fast:
        size = half.shape[axis]
        shape = tuple(2 * n if i == axis else n for i, n in enumerate(half.shape))
        own = lax.dynamic_update_slice_in_dim(
            jnp.zeros(shape, F32), half, net.core * size, axis
        )
        return lax.psum(own, AXES)
    pieces = []
    at = 0
    for count, order in parts:
        pieces.append(join_cores(net, all_reduce(net, half[at : at + count], order), axis))
        at += count
    if axis == 1:
        return jnp.concatenate(pieces, 0)
    half_rows = half.shape[0]
    low, high = [], []
    for piece in pieces:
        n = piece.shape[0] // 2
        low.append(piece[:n])
        high.append(piece[n:])
    return jnp.concatenate(low + high, 0)


def norm_forward(hidden, norm_gain, norm_bias):
    row_mean = jnp.mean(hidden, -1, keepdims=True)
    centered = hidden - row_mean
    variance = jnp.mean(centered * centered, -1, keepdims=True)
    inv_std = lax.rsqrt(variance + EPSILON)
    normed = centered * inv_std
    return (normed * norm_gain + norm_bias, normed, inv_std)


def norm_backward(upstream, normed, inv_std, norm_gain):
    scaled = upstream * norm_gain
    grad_hidden = inv_std * (
        scaled
        - jnp.mean(scaled, -1, keepdims=True)
        - normed * jnp.mean(scaled * normed, -1, keepdims=True)
    )
    return (grad_hidden, jnp.sum(upstream * normed, 0), jnp.sum(upstream, 0))


def heads_of(flat, heads):
    rows, length, width = flat.shape
    return flat.reshape(rows, length, heads, width // heads)


def feature_map(projected, features):
    head_dim = projected.shape[-1]
    feat_count = features.shape[-1]
    inner_u = jnp.einsum("rthe,hem->rhtm", projected, features, preferred_element_type=F32)
    widened = projected.astype(F32)
    square = jnp.sum(widened * widened, -1).transpose(0, 2, 1)[..., None]
    return jnp.exp(
        inner_u * head_dim ** (-0.25) - 0.5 * head_dim ** (-0.5) * square
    ) * feat_count ** (-0.5)


def feature_back(grad_feat, feat_vals, projected, features):
    head_dim = projected.shape[-1]
    weighted = grad_feat * feat_vals
    grad_inner = (weighted * head_dim ** (-0.25)).astype(BF)
    grad_proj = jnp.einsum("rhtm,hem->rthe", grad_inner, features, preferred_element_type=F32)
    folded = jnp.sum(weighted, -1).transpose(0, 2, 1)[..., None]
    grad_proj = grad_proj - head_dim ** (-0.5) * projected.astype(F32) * folded
    return grad_proj.astype(BF)


def edge_sums(values, weights, feats, lead_mask, tail_mask):
    rows, length, heads, head_dim = values.shape
    feat_count = feats.shape[-1]
    out = []
    for mask in (lead_mask, tail_mask):
        masked = jnp.where(mask[:, :, None, None], values, jnp.zeros((), values.dtype))
        sums = jnp.einsum("rthe,rhtm->rhem", masked, feats, preferred_element_type=F32)
        scaled = jnp.where(mask[:, :, None], weights, 0.0)
        zs = jnp.einsum("rth,rhtm->rhm", scaled, feats.astype(F32), precision=lax.Precision.HIGHEST)
        groups = []
        half = heads // 2
        for g in range(2):
            part = sums[:, g * half : (g + 1) * half].reshape(rows, half * head_dim, feat_count)
            pad = jnp.zeros((rows, 8 - half, feat_count), F32)
            groups.append(jnp.concatenate([part, zs[:, g * half : (g + 1) * half], pad], 1))
        out.append(groups)
    return out


def split_carry(groups, heads, head_dim):
    rows = groups[0].shape[0]
    half = heads // 2
    kv = jnp.concatenate(
        [g[:, : half * head_dim].reshape(rows, half, head_dim, -1) for g in groups], 1
    )
    zs = jnp.concatenate([g[:, half * head_dim : half * head_dim + half] for g in groups], 1)
    return kv, zs


def body(
    tokens,
    segment_ids,
    features,
    query_weight,
    key_weight,
    value_weight,
    out_weight,
    up_weight,
    down_weight,
    first_gain,
    first_bias,
    second_gain,
    second_bias,
    cotangent,
):
    net = Net(lax.axis_size("dp"), lax.axis_size("seq"))
    rows, length, width = tokens.shape
    heads_all, head_dim, feat_count = features.shape
    heads = heads_all // 2
    mine = width // 2
    core = net.core
    chip_len = 2 * length
    count = rows * length

    tokens_other = net.swap_b(tokens)
    x_chip = jnp.concatenate([tokens, tokens_other], 1)
    ids = segment_ids.astype(F32)
    ids_chip = jnp.concatenate([ids, net.over_core(ids)], 1)
    first = jnp.min(ids_chip, 1)
    last = jnp.max(ids_chip, 1)
    lead_mask = ids_chip == first[:, None]
    tail_mask = ids_chip == last[:, None]
    same = (ids_chip[:, :, None] == ids_chip[:, None, :])[:, None]
    lead_f = lead_mask.astype(F32)[:, None, :, None]
    tail_f = tail_mask.astype(F32)[:, None, :, None]

    feats = dslice(features, core * heads, heads)
    wq = dslice(query_weight, core * mine, mine, 1)
    wk = dslice(key_weight, core * mine, mine, 1)
    wv = dslice(value_weight, core * mine, mine, 1)
    wo = dslice(out_weight, core * mine, mine, 0)
    wo_other = dslice(out_weight, (1 - core) * mine, mine, 0)
    x_flat = x_chip.reshape(rows * chip_len, width)

    def project(weight):
        return heads_of(mm(x_flat, weight).astype(BF).reshape(rows, chip_len, mine), heads)

    keys_b = project(wk)
    values_b = project(wv)
    feat_k = feature_map(keys_b, feats)
    feat_k_b = feat_k.astype(BF)
    ones = jnp.ones((rows, chip_len, heads), F32)
    lead, tail = edge_sums(values_b, ones, feat_k_b, lead_mask, tail_mask)
    before, behind = exchange(net, lead, tail, first, last, chip_len)
    queries = project(wq)
    feat_q = feature_map(queries, feats)
    feat_q_b = feat_q.astype(BF)
    scores = jnp.einsum("rhtm,rhsm->rhts", feat_q_b, feat_k_b, preferred_element_type=F32)
    scores = jnp.where(same, scores, 0.0)
    scores_b = scores.astype(BF)
    numer = jnp.einsum("rhts,rshe->rhte", scores_b, values_b, preferred_element_type=F32)
    denom = jnp.sum(scores, -1, keepdims=True)

    kv_before, z_before = split_carry(before, heads, head_dim)
    kv_behind, z_behind = split_carry(behind, heads, head_dim)
    kv_before_b, kv_behind_b = kv_before.astype(BF), kv_behind.astype(BF)
    wide_q = feat_q_b.astype(F32)

    def carried(left, kv):
        return jnp.einsum("rhtm,rhem->rhte", left, kv, preferred_element_type=F32)

    numer = numer + lead_f * carried(feat_q_b, kv_before_b) + tail_f * carried(feat_q_b, kv_behind_b)
    z_picked = lead_f * z_before[:, :, None, :] + tail_f * z_behind[:, :, None, :]
    denom = denom + jnp.sum(wide_q * z_picked, -1, keepdims=True)
    attention = numer / denom
    attention_b = attention.astype(BF).transpose(0, 2, 1, 3).reshape(rows, chip_len, mine)
    attn_mine = attention_b[:, :length].reshape(count, mine)
    attn_got = net.swap_b(attention_b[:, length:]).reshape(count, mine)

    tokens_flat = tokens.reshape(count, width)
    hidden_one = tokens_flat.astype(F32) + mm(attn_mine, wo) + mm(attn_got, wo_other)
    normed_one, unit_one, inv_one = norm_forward(hidden_one, first_gain, first_bias)
    normed_one_b = normed_one.astype(BF)
    y1_other = net.swap_b(normed_one_b)
    inner_f = mm(normed_one_b, up_weight)
    activated, gelu_pull = jax.vjp(partial(jax.nn.gelu, approximate=False), inner_f)
    activated_b = activated.astype(BF)
    ff_half = up_weight.shape[1] // 2
    act_mine = dslice(activated_b, core * ff_half, ff_half, 1)
    act_other = net.swap_b(dslice(activated_b, (1 - core) * ff_half, ff_half, 1))
    hidden_two = normed_one + mm(activated_b, down_weight)
    result, unit_two, inv_two = norm_forward(hidden_two, second_gain, second_bias)
    upstream = cotangent.reshape(count, width).astype(F32)
    grad_two, grad_gain_two, grad_bias_two = norm_backward(upstream, unit_two, inv_two, second_gain)
    grad_branch = grad_two.astype(BF)
    gz_other = net.swap_b(grad_branch)
    grad_act = mm_nt(grad_branch, down_weight)
    (grad_inner,) = gelu_pull(grad_act)
    grad_inner_b = grad_inner.astype(BF)
    gi_mine = dslice(grad_inner_b, core * ff_half, ff_half, 1)
    gi_other = net.swap_b(dslice(grad_inner_b, (1 - core) * ff_half, ff_half, 1))

    def both(a, b):
        return jnp.concatenate([a, b], 0)

    y1_chip = both(normed_one_b, y1_other)
    act_chip = both(act_mine, act_other)
    gz_chip = both(grad_branch, gz_other)
    gi_chip = both(gi_mine, gi_other)
    grad_up_half = mm_tn(y1_chip, gi_chip)
    grad_down_half = mm_tn(act_chip, gz_chip)
    grad_up = total(net, grad_up_half, 1, [(256, "xyz"), (256, "yxz"), (256, "zxy")])
    grad_down = total(
        net, grad_down_half, 0, [(384, "xyz"), (384, "yxz"), (384, "zyx"), (384, "zxy")]
    )

    grad_normed = grad_two + mm_nt(grad_inner_b, up_weight)
    grad_one, grad_gain_one, grad_bias_one = norm_backward(grad_normed, unit_one, inv_one, first_gain)
    grad_o = grad_one.astype(BF).reshape(rows, length, width)
    go_chip = jnp.concatenate([grad_o, net.swap_b(grad_o)], 1)
    go_flat = go_chip.reshape(rows * chip_len, width)
    grad_out_half = mm_tn(attention_b.reshape(rows * chip_len, mine), go_flat)
    grad_out = total(net, grad_out_half, 0, [(384, "zyx")])

    grad_att = mm_nt(go_flat, wo).reshape(rows, chip_len, mine)
    grad_att = heads_of(grad_att, heads).transpose(0, 2, 1, 3)
    grad_numer = (grad_att / denom).astype(BF)
    grad_denom = -jnp.sum(grad_att * attention, -1, keepdims=True) / denom
    lead_d, tail_d = edge_sums(
        grad_numer.transpose(0, 2, 1, 3), grad_denom[..., 0].transpose(0, 2, 1), feat_q_b, lead_mask, tail_mask
    )
    before_d, behind_d = exchange(net, lead_d, tail_d, first, last, chip_len)
    pulls = jnp.einsum("rhte,rshe->rhts", grad_numer, values_b, preferred_element_type=F32)
    pulls_b = jnp.where(same, pulls + grad_denom, 0.0).astype(BF)
    grad_feat_q = jnp.einsum("rhts,rhsm->rhtm", pulls_b, feat_k_b, preferred_element_type=F32)

    def pulled(left, kv):
        return jnp.einsum("rhte,rhem->rhtm", left, kv, preferred_element_type=F32)

    grad_feat_q = (
        grad_feat_q
        + lead_f * pulled(grad_numer, kv_before_b)
        + tail_f * pulled(grad_numer, kv_behind_b)
        + grad_denom * z_picked
    )
    grad_queries = feature_back(grad_feat_q, feat_q, queries, feats).reshape(rows * chip_len, mine)
    grad_query_half = mm_tn(x_flat, grad_queries)
    grad_query = total(net, grad_query_half, 1, [(768, "xyz")])

    dkv_before, dz_before = split_carry(before_d, heads, head_dim)
    dkv_behind, dz_behind = split_carry(behind_d, heads, head_dim)
    dkv_before_b, dkv_behind_b = dkv_before.astype(BF), dkv_behind.astype(BF)
    values_t = values_b.transpose(0, 2, 1, 3)
    grad_feat_k = jnp.einsum("rhts,rhtm->rhsm", pulls_b, feat_q_b, preferred_element_type=F32)
    grad_feat_k = (
        grad_feat_k
        + lead_f * (pulled(values_t, dkv_before_b) + dz_before[:, :, None, :])
        + tail_f * (pulled(values_t, dkv_behind_b) + dz_behind[:, :, None, :])
    )
    grad_values = jnp.einsum("rhts,rhte->rhse", scores_b, grad_numer, preferred_element_type=F32)
    grad_values = (
        grad_values
        + lead_f * carried(feat_k_b, dkv_before_b)
        + tail_f * carried(feat_k_b, dkv_behind_b)
    )
    grad_values = grad_values.astype(BF).transpose(0, 2, 1, 3).reshape(rows * chip_len, mine)
    grad_keys = feature_back(grad_feat_k, feat_k, keys_b, feats).reshape(rows * chip_len, mine)
    grad_key = total(net, mm_tn(x_flat, grad_keys), 1, [(768, "yxz")])
    grad_value = total(net, mm_tn(x_flat, grad_values), 1, [(768, "zxy")])

    shares = mm_nt(grad_queries, wq) + mm_nt(grad_keys, wk) + mm_nt(grad_values, wv)
    shares = shares.reshape(rows, chip_len, width)
    grad_input = (
        grad_one.reshape(rows, length, width)
        + shares[:, :length]
        + net.over_core(shares[:, length:])
    )
    small = small_sum(
        net, jnp.stack([grad_gain_one, grad_bias_one, grad_gain_two, grad_bias_two])
    )
    return (
        result.astype(BF).reshape(rows, length, width),
        grad_input.astype(BF),
        grad_query,
        grad_key,
        grad_value,
        grad_out,
        grad_up,
        grad_down,
        small[0],
        small[1],
        small[2],
        small[3],
    )


def solution(mesh):
    split = P("dp", "seq", None)
    placed = (split, P("dp", "seq")) + (P(),) * 11 + (split,)
    return jax.shard_map(
        body,
        mesh=mesh,
        in_specs=placed,
        out_specs=(split, split) + (P(),) * 10,
        check_vma=False,
    )
```

```python
import jax
import jax.numpy as jnp
from jax import lax
from jax.experimental import pallas as pl
from jax.experimental.pallas import tpu as pltpu
from jax.sharding import PartitionSpec as P

SEG_MOST = 2048
SPARE_ROWS = 128
EPSILON = 1e-06
AXES = ("dp", "seq")
BF = jnp.bfloat16
F32 = jnp.float32
ANY = pl.BlockSpec(memory_space=pl.ANY)
ROOM = 56 << 20


BIG = 150


def cost(us):
    return pl.CostEstimate(flops=int(us * 1e9), bytes_accessed=1, transcendentals=0)


def shaped(*shape, dtype=F32):
    return jax.ShapeDtypeStruct(shape, dtype)


def mm(a, b):
    return jnp.dot(a, b, preferred_element_type=F32)


def mm_nt(a, b):
    return lax.dot_general(a, b, (((1,), (1,)), ((), ())), preferred_element_type=F32)


def mm_tn(a, b):
    return lax.dot_general(a, b, (((0,), (0,)), ((), ())), preferred_element_type=F32)


def dslice(a, start, size, axis=0):
    return lax.dynamic_slice_in_dim(a, start, size, axis)


class Net:
    def __init__(self, n_dp, n_seq):
        self.n_dp, self.n_seq = n_dp, n_seq
        self.nz = 4
        self.nx = n_seq // 8
        self.fast = n_dp == 2 and n_seq == 16
        seq = lax.axis_index("seq")
        self.y = lax.axis_index("dp")
        self.core = seq % 2
        self.x = (seq // 2) % self.nx
        self.z = seq // (2 * self.nx)
        self.seq = seq

    def perm(self, move):
        pairs = []
        for y in range(self.n_dp):
            for s in range(self.n_seq):
                target = move(y, s // (2 * self.nx), (s // 2) % self.nx, s % 2)
                if target is not None:
                    ty, tz, tx, tc = target
                    pairs.append((y * self.n_seq + s, ty * self.n_seq + (tz * self.nx + tx) * 2 + tc))
        return pairs

    def send(self, value, move):
        return lax.ppermute(value, AXES, self.perm(move))

    def over_core(self, value):
        return self.send(value, lambda y, z, x, c: (y, z, x, 1 - c))

    def over_x(self, value):
        return self.send(value, lambda y, z, x, c: (y, z, 1 - x, c))

    def z_up(self, value):
        return self.send(value, lambda y, z, x, c: (y, z + 1, x, c) if z < 3 else None)

    def z_down(self, value):
        return self.send(value, lambda y, z, x, c: (y, z - 1, x, c) if z > 0 else None)

    def shift(self, value, step):
        chips = self.n_seq // 2
        pairs = []
        for y in range(self.n_dp):
            for s in range(self.n_seq):
                if 0 <= s // 2 + step < chips:
                    pairs.append((y * self.n_seq + s, y * self.n_seq + s + 2 * step))
        return lax.ppermute(value, AXES, pairs)


ORDERS = ((("x", "y", "1", "2"), ("y", "x", "2", "1")), (("1", "2", "x", "y"), ("2", "1", "x", "y")))


def stage_move(net, value, stream, stage):
    def move(y, z, x, c):
        axis = ORDERS[stream][c][stage]
        return {
            "x": (y, z, 1 - x, c),
            "y": (1 - y, z, x, c),
            "1": (y, z ^ 1, x, c),
            "2": (y, z ^ 2, x, c),
        }[axis]

    return net.send(value, move)


def stage_bit(net, stream, stage, core):
    place = {"x": net.x, "y": net.y, "1": net.z % 2, "2": net.z // 2}
    zero, one = (place[ORDERS[stream][c][stage]] for c in (0, 1))
    return jnp.where(core == 0, zero, one)


def tie(value, *deps):
    def kernel(*refs):
        pass

    anywhere = pl.BlockSpec(memory_space=pl.ANY)
    return pl.pallas_call(
        kernel,
        in_specs=[anywhere] * (1 + len(deps)),
        out_specs=anywhere,
        out_shape=jax.ShapeDtypeStruct(value.shape, value.dtype),
        input_output_aliases={0: 0},
        cost_estimate=cost(0.1),
        name="tie",
    )(value, *deps)


def moves(net, parts, stage):
    return [stage_move(net, part, i, stage) for i, part in enumerate(parts)]


def stage_bits(net, stage, core=None):
    core = net.core if core is None else core
    return jnp.stack([stage_bit(net, i, stage, core) for i in range(2)]).astype(jnp.int32)


def add_stage(net, keeps, gots, stage, deps=()):
    steps = max(1, keeps[0].shape[0] // 256)

    def kernel(bits_ref, *refs):
        outs = refs[8 + len(deps) :]
        for i in range(4):
            outs[i][...] = refs[2 * i][...] + refs[2 * i + 1][...]

    in_specs, inputs, out_specs, shapes = [], [], [], []
    for side in (0, 1):
        for i, (keep, got) in enumerate(zip(keeps, gots)):
            half, width = keep.shape[0] // 2, keep.shape[1]
            block = (half // steps, width)
            spec = pl.BlockSpec(
                block,
                lambda r, bits, i=i, side=side: (
                    (bits[i] if side else 1 - bits[i]) * steps + r,
                    0,
                ),
            )
            in_specs += [spec, spec]
            inputs += [keep, got]
            out_specs.append(pl.BlockSpec(block, lambda r, bits: (r, 0)))
            shapes.append(shaped(half, width))
    in_specs += [ANY] * len(deps)
    outs = pl.pallas_call(
        kernel,
        grid_spec=pltpu.PrefetchScalarGridSpec(
            num_scalar_prefetch=1, grid=(steps,), in_specs=in_specs, out_specs=out_specs
        ),
        out_shape=shapes,
        cost_estimate=cost(BIG),
        name="add_stage",
    )(stage_bits(net, stage), *inputs, *deps)
    return outs[:2], outs[2:]


def last_add(keeps, gots, deps=()):
    def kernel(*refs):
        outs = refs[4 + len(deps) :]
        for i in range(2):
            outs[i][...] = refs[i][...] + refs[2 + i][...]

    whole = pl.BlockSpec(memory_space=pltpu.VMEM)
    return pl.pallas_call(
        kernel,
        in_specs=[whole] * 4 + [ANY] * len(deps),
        out_specs=[whole] * 2,
        out_shape=[shaped(*k.shape) for k in keeps],
        cost_estimate=cost(BIG),
        name="last_add",
    )(*keeps, *gots, *deps)


def join_stage(net, parts, gots, stage, deps=()):
    steps = max(1, parts[0].shape[0] // 128)

    def kernel(bits_ref, *refs):
        outs = refs[4 + len(deps) :]
        for i in range(2):
            bit = bits_ref[i]
            outs[i][pl.ds(bit, 1)] = refs[2 * i][...][None]
            outs[i][pl.ds(1 - bit, 1)] = refs[2 * i + 1][...][None]

    in_specs, out_specs, shapes = [], [], []
    for part in parts:
        n, width = part.shape
        rows = n // steps
        in_specs += [pl.BlockSpec((rows, width), lambda r, bits: (r, 0))] * 2
        out_specs.append(pl.BlockSpec((2, rows, width), lambda r, bits: (0, r, 0)))
        shapes.append(shaped(2, n, width))
    outs = pl.pallas_call(
        kernel,
        grid_spec=pltpu.PrefetchScalarGridSpec(
            num_scalar_prefetch=1,
            grid=(steps,),
            in_specs=in_specs + [ANY] * len(deps),
            out_specs=out_specs,
        ),
        out_shape=shapes,
        cost_estimate=cost(BIG),
        name="join_stage",
    )(stage_bits(net, stage), *[v for pair in zip(parts, gots) for v in pair], *deps)
    return [out.reshape(2 * out.shape[1], out.shape[2]) for out in outs]


def block_of(i, bits):
    return jnp.where(i < 2, 2 * bits[0] + i, 4 + bits[1])


def stream_specs(rows, width, more=0):
    return [
        pl.BlockSpec((rows, width), lambda i, bits: (jnp.minimum(i, 1), 0)),
        pl.BlockSpec((rows + more, width), lambda i, bits: (0, 0)),
    ]


def tn(a, a_other, b, b_other):
    return mm_tn(a, b) + mm_tn(a_other.astype(BF), b_other.astype(BF))


def ffn_products(bits, y1, y1_other, gi, gi_other, act, act_other, gz, gz_other, deps=()):
    count, width = y1.shape
    ff_half = gi.shape[1]
    u, d = width // 6, ff_half // 6
    rows = ff_half // width * u + d

    def kernel(bits_ref, y1_r, y1o_r, gi_r, gio_r, act_r, acto_r, gz_r, gzo_r, *rest):
        outs = rest[len(deps) :]

        def fill(out):
            y, yo = y1_r[...], y1o_r[...]
            for part in range(ff_half // width):
                cut = slice(part * width, (part + 1) * width)
                out[part * u : (part + 1) * u, :] = tn(y, yo, gi_r[:, cut], gio_r[:, cut])
            out[ff_half // width * u :, :] = tn(act_r[...], acto_r[...], gz_r[...], gzo_r[...])

        pl.when(pl.program_id(0) < 2)(lambda: fill(outs[0]))
        pl.when(pl.program_id(0) == 2)(lambda: fill(outs[1]))

    def picked(size):
        return pl.BlockSpec((count, size), lambda i, bits: (0, block_of(i, bits)))

    def whole(array):
        return pl.BlockSpec(array.shape, lambda i, bits: (0, 0))

    return pl.pallas_call(
        kernel,
        grid_spec=pltpu.PrefetchScalarGridSpec(
            num_scalar_prefetch=1,
            grid=(3,),
            in_specs=[
                picked(u), picked(u), whole(gi), whole(gi_other),
                picked(d), picked(d), whole(gz), whole(gz_other),
            ] + [ANY] * len(deps),
            out_specs=stream_specs(rows, width),
        ),
        out_shape=[shaped(2 * rows, width), shaped(rows, width)],
        compiler_params=pltpu.CompilerParams(vmem_limit_bytes=ROOM),
        cost_estimate=cost(6.5),
        name="ffn_products",
    )(bits, y1, y1_other, gi, gi_other, act, act_other, gz, gz_other, *deps)


def attn_products(bits, x, x_other, dq, dk, dv, attn, go, go_other, small, deps=()):
    count, width = x.shape
    mine = attn.shape[1]
    u = mine // 3
    rows = mine + u

    def kernel(bits_ref, x_r, xo_r, dq_r, dk_r, dv_r, attn_r, go_r, goo_r, small_r, *rest):
        outs = rest[len(deps) :]
        for i, grad in enumerate((dq_r, dk_r, dv_r)):

            @pl.when(pl.program_id(0) == i)
            def _():
                out = outs[i // 2]
                out[:mine, :] = tn(x_r[...], xo_r[...], grad[:count], grad[count:])
                part = attn_r[...].astype(BF)
                out[mine:rows, :] = tn(part[:count], part[count:], go_r[...], goo_r[...])
                if i == 2:
                    out[rows:, :] = jnp.zeros((SPARE_ROWS, mine), F32)
                    out[rows : rows + 8, :] = small_r[...]

    full = pl.BlockSpec((2 * count, mine), lambda i, bits: (0, 0))
    half = pl.BlockSpec((count, mine), lambda i, bits: (0, bits[i // 2]))
    return pl.pallas_call(
        kernel,
        grid_spec=pltpu.PrefetchScalarGridSpec(
            num_scalar_prefetch=1,
            grid=(3,),
            in_specs=[half, half, full, full, full]
            + [pl.BlockSpec((2 * count, u), lambda i, bits: (0, i)), half, half]
            + [pl.BlockSpec(small.shape, lambda i, bits: (0, 0))]
            + [ANY] * len(deps),
            out_specs=stream_specs(rows, mine, SPARE_ROWS),
        ),
        out_shape=[shaped(2 * rows, mine), shaped(rows + SPARE_ROWS, mine)],
        compiler_params=pltpu.CompilerParams(vmem_limit_bytes=ROOM),
        cost_estimate=cost(6),
        name="attn_products",
    )(bits, x, x_other, dq, dk, dv, attn, go, go_other, small, *deps)


def place_pieces(net, pieces, outs, copies, deps=()):
    fresh = isinstance(outs[0], jax.ShapeDtypeStruct)
    n_out, n = len(outs), len(pieces)
    inputs = [part for piece in pieces for part in piece[0]]
    scalars = []
    for _, other_core, other_first, other_second in pieces:
        core = 1 - net.core if other_core else net.core
        scalars.append(core)
        for i in range(2):
            for stage, flip in ((0, other_first), (1, other_second)):
                bit = stage_bit(net, i, stage, core)
                scalars.append(1 - bit if flip else bit)
    where = jnp.stack(scalars).astype(jnp.int32)

    def kernel(where_ref, *refs):
        srcs = refs[: 2 * n]
        dests = refs[-(2 * n + 2 + n_out) : -(2 * n + 2)]
        held, (arrive, sems) = refs[-(2 * n + 2) : -2], refs[-2:]
        loads = [pltpu.make_async_copy(srcs[j], held[j], arrive.at[j]) for j in range(2 * n)]
        for load in loads:
            load.start()

        def each(j, act):
            piece, i = j // 2, j % 2
            core = where_ref[5 * piece]
            first, second = where_ref[5 * piece + 1 + 2 * i], where_ref[5 * piece + 2 + 2 * i]
            for quarter in (0, 1):

                @pl.when(second == quarter)
                def _():
                    for k, (src, dest) in enumerate(copies(i, quarter, core, first, held[j], dests)):
                        act(pltpu.make_async_copy(src, dest, sems.at[j, k]))

        for j in range(2 * n):
            loads[j].wait()
            each(j, lambda copy: copy.start())
        for j in range(2 * n):
            each(j, lambda copy: copy.wait())

    operands = inputs + ([] if fresh else list(outs)) + list(deps)
    return list(pl.pallas_call(
        kernel,
        grid_spec=pltpu.PrefetchScalarGridSpec(
            num_scalar_prefetch=1,
            grid=(1,),
            in_specs=[ANY] * len(operands),
            out_specs=[ANY] * n_out,
            scratch_shapes=[pltpu.VMEM(part.shape, F32) for part in inputs] + [
                pltpu.SemaphoreType.DMA((2 * n,)),
                pltpu.SemaphoreType.DMA((2 * n, 3)),
            ],
        ),
        out_shape=[shaped(*o.shape) for o in outs],
        input_output_aliases={} if fresh else {1 + 2 * n + i: i for i in range(n_out)},
        compiler_params=pltpu.CompilerParams(vmem_limit_bytes=ROOM),
        cost_estimate=cost(BIG),
        name="place_pieces",
    )(where, *operands))


def rows_at(ref, start, size, step, lanes=None):
    start = pl.multiple_of(start, step)
    return ref.at[pl.ds(start, size)] if lanes is None else ref.at[pl.ds(start, size), lanes]


def ffn_copies(width, ff_half):
    u, d = width // 6, ff_half // 6
    parts = ff_half // width

    def copies(i, quarter, c, b, src, dests):
        up, down = dests
        block = 4 + b if i else 2 * b + quarter
        if i == 0 or quarter == 0:
            for part in range(parts):
                lanes = pl.ds(pl.multiple_of(c * ff_half + part * width, 128), width)
                yield src.at[part * u : (part + 1) * u], rows_at(up, block * u, u, 8, lanes)
        if i == 0 or quarter == 1:
            at = 0 if i else parts * u
            yield src.at[at : at + d], rows_at(down, c * ff_half + block * d, d, 8)

    return copies


def attn_copies(mine):
    u = mine // 3
    cut = (mine + u + SPARE_ROWS) // 2

    def copies(i, quarter, c, b, src, dests):
        rows = pl.ds(pl.multiple_of(c * mine, 128), mine)
        lanes = pl.ds(pl.multiple_of(b * mine, 128), mine)
        if i == 0:
            yield src.at[:mine], rows_at(dests[quarter], b * mine, mine, 8, rows)
            yield src.at[mine:], rows_at(dests[3], c * mine + quarter * u, u, 8, lanes)
        elif quarter == 0:
            yield src.at[:cut], rows_at(dests[2], b * mine, cut, 8, rows)
        else:
            rest = mine - cut
            yield src.at[:rest], rows_at(dests[2], b * mine + cut, rest, 8, rows)
            yield src.at[rest : rest + u], rows_at(dests[3], c * mine + 2 * u, u, 8, lanes)

    return copies


def total(net, half, axis):
    size = half.shape[axis]
    shape = tuple(2 * n if i == axis else n for i, n in enumerate(half.shape))
    own = lax.dynamic_update_slice_in_dim(jnp.zeros(shape, F32), half, net.core * size, axis)
    return lax.psum(own, AXES)


def per_row(array):
    rest = array.shape[1:]
    return pl.BlockSpec((1, *rest), lambda r, info: (r, *(0 for _ in rest)))


COSTS = {"keys": 10, "queries": 8, "attend": 6, "grads_one": 10, "grads_two": 12, "grads_three": 8, "shares": 5, "join_plane": 3, "split_plane": 3}


def row_call(kernel, name, info, inputs, in_specs, outs, deps=(), flops=0):
    n_in = len(inputs)
    rows = outs[0].shape[0]

    def run(info_ref, *refs):
        kernel(info_ref, *refs[:n_in], *refs[n_in + len(deps) :])

    size = sum(v.size * v.dtype.itemsize for v in [*inputs, *outs])
    return pl.pallas_call(
        run,
        grid_spec=pltpu.PrefetchScalarGridSpec(
            num_scalar_prefetch=1,
            grid=(rows,),
            in_specs=list(in_specs) + [ANY] * len(deps),
            out_specs=[per_row(o) for o in outs],
        ),
        out_shape=outs,
        compiler_params=pltpu.CompilerParams(vmem_limit_bytes=ROOM),
        cost_estimate=cost(COSTS[name]),
        name=name,
    )(info, *inputs, *deps)


def edges(idc_ref, idr_ref):
    row = idr_ref[0]
    first = jnp.min(row, axis=1, keepdims=True)
    last = jnp.max(row, axis=1, keepdims=True)
    return idc_ref[0] == first, idc_ref[0] == last, first, last


def phi(part, feats):
    head_dim, feat_count = feats.shape
    wide = part.astype(F32)
    square = jnp.sum(wide * wide, -1, keepdims=True)
    inner = mm(part, feats) * head_dim ** (-0.25) - square * (0.5 * head_dim ** (-0.5))
    return (jnp.exp(inner) * feat_count ** (-0.5)).astype(BF)


def put_edges(info_ref, keep, send, h, heads, sums, lead_z, tail_z):
    half = heads // 2
    group, at = h // half, h % half
    e = sums.shape[0] // 2

    def put(ref):
        ref[0, 0, at * e : (at + 1) * e, :] = sums[:e]
        ref[0, 1, at * e : (at + 1) * e, :] = sums[e:]
        ref[0, 0, half * e + at : half * e + at + 1, :] = lead_z
        ref[0, 1, half * e + at : half * e + at + 1, :] = tail_z

    @pl.when(info_ref[1] == group)
    def _():
        put(keep)

    @pl.when(info_ref[1] != group)
    def _():
        put(send)


def put_tags(keep, send, spare, first, last):
    n, m = keep.shape[2:]
    for ref in (keep, send):
        ref[0, 0, spare:, :] = jnp.broadcast_to(first, (n - spare, m))
        ref[0, 1, spare:, :] = jnp.broadcast_to(last, (n - spare, m))


def weight_columns(weight, mine):
    return pl.BlockSpec((weight.shape[0], mine), lambda r, info: (0, info[0]))


def head_features(features, heads):
    return pl.BlockSpec((heads, *features.shape[1:]), lambda r, info: (info[0], 0, 0))


def keys_kernel(info, x, x_got, key_weight, value_weight, features, idc, idr):
    rows, length, width = x.shape
    mine, heads = width // 2, features.shape[0] // 2
    e, m = features.shape[1:]
    n = heads // 2 * e + 8
    spare = heads // 2 * e + heads // 2

    def kernel(info_ref, x_r, xg_r, wk_r, wv_r, f_r, idc_r, idr_r, k_o, v_o, fk_o, keep, send):
        chip = jnp.concatenate([x_r[0], xg_r[0].astype(BF)], 0)
        keys = mm(chip, wk_r[...]).astype(BF)
        values = mm(chip, wv_r[...]).astype(BF)
        k_o[0] = keys
        v_o[0] = values
        lead, tail, first, last = edges(idc_r, idr_r)
        masks = jnp.concatenate([lead.astype(F32), tail.astype(F32)], 1).astype(BF)
        lead_b, tail_b = masks[:, 0:1], masks[:, 1:2]
        for h in range(heads):
            cut = slice(h * e, (h + 1) * e)
            feat = phi(keys[:, cut], f_r[h])
            fk_o[0, h] = feat
            part = values[:, cut]
            sums = mm_tn(jnp.concatenate([part * lead_b, part * tail_b], 1), feat)
            zs = mm_tn(masks, feat)
            put_edges(info_ref, keep, send, h, heads, sums, zs[0:1], zs[1:2])
        put_tags(keep, send, spare, first, last)

    outs = [
        shaped(rows, 2 * length, mine, dtype=BF),
        shaped(rows, 2 * length, mine, dtype=BF),
        shaped(rows, heads, 2 * length, m, dtype=BF),
        shaped(rows, 2, n, m),
        shaped(rows, 2, n, m),
    ]
    specs = [
        per_row(x), per_row(x_got),
        weight_columns(key_weight, mine), weight_columns(value_weight, mine),
        head_features(features, heads), per_row(idc), per_row(idr),
    ]
    return row_call(
        kernel, "keys", info, [x, x_got, key_weight, value_weight, features, idc, idr], specs, outs,
        flops=rows * length * width * mine * 10,
    )


def queries_kernel(info, x, x_got, query_weight, features, fk, values, idc, idr, deps=()):
    rows, length, width = x.shape
    mine, heads = width // 2, features.shape[0] // 2
    e, m = features.shape[1:]

    def kernel(info_ref, x_r, xg_r, wq_r, f_r, fk_r, v_r, idc_r, idr_r, q_o, fq_o, num_o, den_o):
        chip = jnp.concatenate([x_r[0], xg_r[0].astype(BF)], 0)
        queries = mm(chip, wq_r[...]).astype(BF)
        q_o[0] = queries
        same = idc_r[0] == idr_r[0]
        lane = lax.broadcasted_iota(jnp.int32, (2 * length, 128), 1)
        dens = jnp.ones((2 * length, 128), F32)
        for h in range(heads):
            cut = slice(h * e, (h + 1) * e)
            feat = phi(queries[:, cut], f_r[h])
            fq_o[0, h] = feat
            scores = jnp.where(same, mm_nt(feat, fk_r[0, h]), 0.0)
            num_o[0, :, cut] = mm(scores.astype(BF), v_r[0, :, cut])
            dens = jnp.where(lane == h, jnp.sum(scores, -1, keepdims=True), dens)
        den_o[0] = dens

    outs = [
        shaped(rows, 2 * length, mine, dtype=BF),
        shaped(rows, heads, 2 * length, m, dtype=BF),
        shaped(rows, 2 * length, mine),
        shaped(rows, 2 * length, 128),
    ]
    specs = [
        per_row(x), per_row(x_got), weight_columns(query_weight, mine),
        head_features(features, heads), per_row(fk), per_row(values), per_row(idc), per_row(idr),
    ]
    return row_call(
        kernel, "queries", info,
        [x, x_got, query_weight, features, fk, values, idc, idr], specs, outs, deps,
        flops=rows * length * width * mine * 12,
    )


def carry_of(info_ref, own_r, got_r, h, heads, e):
    half = heads // 2
    group, at = h // half, h % half
    flag = info_ref[1] == group

    def picked(k, rows):
        return jnp.where(flag, own_r[0, k, rows, :], got_r[0, k, rows, :])

    kv = slice(at * e, (at + 1) * e)
    z = slice(half * e + at, half * e + at + 1)
    return picked(0, kv), picked(1, kv), picked(0, z), picked(1, z)


def attend_kernel(info, fq, num, den, own, got, idc, idr):
    rows, heads, chip_len, m = fq.shape
    mine = num.shape[2]
    e = mine // heads
    length = chip_len // 2

    def kernel(info_ref, fq_r, num_r, den_r, own_r, got_r, idc_r, idr_r, att_o, den_o, here_o, send_o):
        lead, tail, _, _ = edges(idc_r, idr_r)
        lead, tail = lead.astype(F32), tail.astype(F32)
        lane = lax.broadcasted_iota(jnp.int32, (chip_len, 128), 1)
        dens = den_r[0]
        for h in range(heads):
            cut = slice(h * e, (h + 1) * e)
            before, behind, zb, za = carry_of(info_ref, own_r, got_r, h, heads, e)
            feat = fq_r[0, h]
            more = mm_nt(feat, jnp.concatenate([before, behind], 0).astype(BF))
            numer = num_r[0, :, cut] + lead * more[:, :e] + tail * more[:, e:]
            extra = jnp.sum(feat.astype(F32) * (lead * zb + tail * za), -1, keepdims=True)
            denom = den_r[0, :, h : h + 1] + extra
            dens = jnp.where(lane == h, denom, dens)
            att = numer / denom
            att_o[0, :, cut] = att
            rounded = att.astype(BF)
            here_o[0, :, cut] = rounded[:length]
            send_o[0, :, cut] = rounded[length:].astype(F32)
        den_o[0] = dens

    outs = [
        shaped(rows, chip_len, mine),
        shaped(rows, chip_len, 128),
        shaped(rows, length, mine, dtype=BF),
        shaped(rows, length, mine),
    ]
    inputs = [fq, num, den, own, got, idc, idr]
    return row_call(
        kernel, "attend", info, inputs, [per_row(v) for v in inputs], outs,
        flops=rows * chip_len * mine * m * 6,
    )


def grads_one_kernel(info, go, go_got, out_weight, att, den, fq, idc, idr):
    rows, length, width = go.shape
    heads, m = fq.shape[1], fq.shape[3]
    mine = width // 2
    e = mine // heads
    n = heads // 2 * e + 8
    spare = heads // 2 * e + heads // 2

    def kernel(info_ref, go_r, gog_r, wo_r, att_r, den_r, fq_r, idc_r, idr_r, dn_o, dd_o, keep, send):
        chip = jnp.concatenate([go_r[0], gog_r[0].astype(BF)], 0)
        pulls = mm_nt(chip, wo_r[...])
        lead, tail, first, last = edges(idc_r, idr_r)
        lead, tail = lead.astype(F32), tail.astype(F32)
        lane = lax.broadcasted_iota(jnp.int32, (2 * length, 128), 1)
        dds = jnp.zeros((2 * length, 128), F32)
        for h in range(heads):
            cut = slice(h * e, (h + 1) * e)
            denom = den_r[0, :, h : h + 1]
            pull = pulls[:, cut]
            dn = (pull / denom).astype(BF)
            dn_o[0, :, cut] = dn
            dd = -jnp.sum(pull * att_r[0, :, cut], -1, keepdims=True) / denom
            dds = jnp.where(lane == h, dd, dds)
            wide = dn.astype(F32)
            sums = mm_tn(jnp.concatenate([wide * lead, wide * tail], 1).astype(BF), fq_r[0, h])
            high = dd.astype(BF).astype(F32)
            low = dd - high
            four = jnp.concatenate([high * lead, low * lead, high * tail, low * tail], 1)
            zs = mm_tn(four.astype(BF), fq_r[0, h])
            put_edges(info_ref, keep, send, h, heads, sums, zs[0:1] + zs[1:2], zs[2:3] + zs[3:4])
        dd_o[0] = dds
        put_tags(keep, send, spare, first, last)

    outs = [
        shaped(rows, 2 * length, mine, dtype=BF),
        shaped(rows, 2 * length, 128),
        shaped(rows, 2, n, m),
        shaped(rows, 2, n, m),
    ]
    specs = [
        per_row(go), per_row(go_got),
        pl.BlockSpec((mine, width), lambda r, info: (info[0], 0)),
        per_row(att), per_row(den), per_row(fq), per_row(idc), per_row(idr),
    ]
    return row_call(
        kernel, "grads_one", info, [go, go_got, out_weight, att, den, fq, idc, idr], specs, outs,
        flops=rows * length * width * mine * 6,
    )


def pulled_back(grad_feat, feat, part, feats):
    e = feats.shape[0]
    weighted = grad_feat * feat.astype(F32)
    inner = (weighted * e ** (-0.25)).astype(BF)
    folded = jnp.sum(weighted, -1, keepdims=True) * e ** (-0.5)
    return (mm_nt(inner, feats) - part.astype(F32) * folded).astype(BF)


def grads_two_kernel(info, fq, fk, queries, values, dn, dd, features, own, got, idc, idr, deps=()):
    rows, heads, chip_len, m = fq.shape
    mine = queries.shape[2]
    e = mine // heads

    def kernel(
        info_ref, fq_r, fk_r, q_r, v_r, dn_r, dd_r, f_r, own_r, got_r, idc_r, idr_r, dq_o, dfk_o, dv_o
    ):
        same = idc_r[0] == idr_r[0]
        lead, tail, _, _ = edges(idc_r, idr_r)
        lead, tail = lead.astype(F32), tail.astype(F32)
        for h in range(heads):
            cut = slice(h * e, (h + 1) * e)
            feat_q, feat_k = fq_r[0, h], fk_r[0, h]
            part, value = dn_r[0, :, cut], v_r[0, :, cut]
            denom = dd_r[0, :, h : h + 1]
            scores = jnp.where(same, mm_nt(feat_q, feat_k), 0.0).astype(BF)
            pulls = jnp.where(same, mm_nt(part, value) + denom, 0.0).astype(BF)
            dv_o[0, :, cut] = mm_tn(scores, part)
            dfk_o[0, h] = mm_tn(pulls, feat_q)
            before, behind, zb, za = carry_of(info_ref, own_r, got_r, h, heads, e)
            wide = part.astype(F32)
            both = jnp.concatenate([wide * lead, wide * tail], 1).astype(BF)
            grad = (
                mm(pulls, feat_k)
                + mm(both, jnp.concatenate([before, behind], 0).astype(BF))
                + denom * (lead * zb + tail * za)
            )
            dq_o[0, :, cut] = pulled_back(grad, feat_q, q_r[0, :, cut], f_r[h])

    outs = [
        shaped(rows, chip_len, mine, dtype=BF),
        shaped(rows, heads, chip_len, m),
        shaped(rows, chip_len, mine),
    ]
    inputs = [fq, fk, queries, values, dn, dd, features, own, got, idc, idr]
    specs = [per_row(v) for v in inputs]
    specs[6] = head_features(features, heads)
    return row_call(
        kernel, "grads_two", info, inputs, specs, outs, deps, flops=rows * chip_len * chip_len * mine * 30
    )


def grads_three_kernel(info, fk, keys, values, dfk, dv, features, own, got, idc, idr, deps=()):
    rows, heads, chip_len, m = fk.shape
    mine = keys.shape[2]
    e = mine // heads

    def kernel(
        info_ref, fk_r, k_r, v_r, dfk_r, dv_r, f_r, own_r, got_r, idc_r, idr_r, dk_o, dv_o
    ):
        lead, tail, _, _ = edges(idc_r, idr_r)
        lead, tail = lead.astype(F32), tail.astype(F32)
        for h in range(heads):
            cut = slice(h * e, (h + 1) * e)
            feat = fk_r[0, h]
            before, behind, zb, za = carry_of(info_ref, own_r, got_r, h, heads, e)
            kv = jnp.concatenate([before, behind], 0).astype(BF)
            wide = v_r[0, :, cut].astype(F32)
            both = jnp.concatenate([wide * lead, wide * tail], 1).astype(BF)
            grad = dfk_r[0, h] + mm(both, kv) + (lead * zb + tail * za)
            dk_o[0, :, cut] = pulled_back(grad, feat, k_r[0, :, cut], f_r[h])
            more = mm_nt(feat, kv)
            total_v = dv_r[0, :, cut] + lead * more[:, :e] + tail * more[:, e:]
            dv_o[0, :, cut] = total_v.astype(BF)

    outs = [shaped(rows, chip_len, mine, dtype=BF), shaped(rows, chip_len, mine, dtype=BF)]
    inputs = [fk, keys, values, dfk, dv, features, own, got, idc, idr]
    specs = [per_row(v) for v in inputs]
    specs[5] = head_features(features, heads)
    return row_call(
        kernel, "grads_three", info, inputs, specs, outs, deps, flops=rows * chip_len * m * mine * 8
    )


def shares_kernel(info, dq, dk, dv, query_weight, key_weight, value_weight, deps=()):
    rows, chip_len, mine = dq.shape
    width = query_weight.shape[0]
    length = chip_len // 2

    def kernel(info_ref, dq_r, dk_r, dv_r, wq_r, wk_r, wv_r, here_o, send_o):
        total_x = (
            mm_nt(dq_r[0], wq_r[...]) + mm_nt(dk_r[0], wk_r[...]) + mm_nt(dv_r[0], wv_r[...])
        )
        here_o[0] = total_x[:length]
        send_o[0] = total_x[length:]

    outs = [shaped(rows, length, width), shaped(rows, length, width)]
    specs = [per_row(dq), per_row(dk), per_row(dv)] + [
        weight_columns(w, mine) for w in (query_weight, key_weight, value_weight)
    ]
    return row_call(
        kernel, "shares", info, [dq, dk, dv, query_weight, key_weight, value_weight], specs, outs, deps,
        flops=rows * chip_len * mine * width * 6,
    )


def norm(hidden):
    mean = jnp.mean(hidden, -1, keepdims=True)
    centered = hidden - mean
    variance = jnp.mean(centered * centered, -1, keepdims=True)
    inv_std = lax.rsqrt(variance + EPSILON)
    return centered * inv_std, inv_std


def norm_back(upstream, normed, inv_std, gain):
    scaled = upstream * gain
    return inv_std * (
        scaled
        - jnp.mean(scaled, -1, keepdims=True)
        - normed * jnp.mean(scaled * normed, -1, keepdims=True)
    )


def put_sums(ref, upstream, normed):
    ref[...] = jnp.zeros_like(ref)
    ref[0:1, :] = jnp.sum(upstream * normed, 0, keepdims=True)
    ref[1:2, :] = jnp.sum(upstream, 0, keepdims=True)


def ffn_chunk(j, info, chunks):
    return lax.rem(j + (1 - info[0]) * (chunks // 2), chunks)


def ffn_forward(info, x, att, att_got, out_weight, first, up, down, second, cot, chunks=6):
    count, width = x.shape
    mine = att.shape[1]
    ff = up.shape[1]
    size = ff // chunks
    half = chunks // 2

    def kernel(
        info_ref, x_r, att_r, attg_r, wo_r, wog_r, first_r, up_r, down_r, second_r, cot_r,
        y_o, ys_o, here_o, send_o, slope_o, out_o, dz_o, dzs_o, dh_o, unit_o, inv_o, sums_o, y_s, acc,
    ):
        j = pl.program_id(0)

        @pl.when(j == 0)
        def _():
            hidden = (
                x_r[...].astype(F32)
                + mm(att_r[...], wo_r[...])
                + mm(attg_r[...].astype(BF), wog_r[...])
            )
            normed, inv_std = norm(hidden)
            unit_o[...] = normed
            inv_o[...] = jnp.broadcast_to(inv_std, inv_o.shape)
            y = normed * first_r[0:1, :] + first_r[1:2, :]
            acc[...] = y
            y_s[...] = y.astype(BF)
            y_o[...] = y_s[...]
            ys_o[...] = y_s[...].astype(F32)

        inner = mm(y_s[...], up_r[...])
        bell = 0.5 * (1.0 + lax.erf(inner * 0.7071067811865476))
        slope_o[...] = bell + inner * (jnp.exp(-0.5 * inner * inner) * 0.3989422804014327)
        act = (inner * bell).astype(BF)

        @pl.when(j < half)
        def _():
            send_o[...] = act.astype(F32)

        @pl.when(j >= half)
        def _():
            here_o[...] = act

        acc[...] += mm(act, down_r[...])

        @pl.when(j == chunks - 1)
        def _():
            normed, inv_std = norm(acc[...])
            gain = second_r[0:1, :]
            out_o[...] = (normed * gain + second_r[1:2, :]).astype(BF)
            upstream = cot_r[...].astype(F32)
            put_sums(sums_o, upstream, normed)
            grad = norm_back(upstream, normed, inv_std, gain)
            dh_o[...] = grad
            dz_o[...] = grad.astype(BF)
            dzs_o[...] = grad.astype(BF).astype(F32)

    def whole(array):
        return pl.BlockSpec(array.shape, lambda j, info: (0, 0))

    flat = pl.BlockSpec((count, width), lambda j, info: (0, 0))
    outs = [
        (shaped(count, width, dtype=BF), flat),
        (shaped(count, width), flat),
        (shaped(count, ff // 2, dtype=BF), pl.BlockSpec((count, size), lambda j, info: (0, jnp.maximum(j - half, 0)))),
        (shaped(count, ff // 2), pl.BlockSpec((count, size), lambda j, info: (0, jnp.minimum(j, half - 1)))),
        (shaped(count, ff), pl.BlockSpec((count, size), lambda j, info: (0, j))),
        (shaped(count, width, dtype=BF), flat),
        (shaped(count, width, dtype=BF), flat),
        (shaped(count, width), flat),
        (shaped(count, width), flat),
        (shaped(count, width), flat),
        (shaped(count, 128), pl.BlockSpec((count, 128), lambda j, info: (0, 0))),
        (shaped(8, width), pl.BlockSpec((8, width), lambda j, info: (0, 0))),
    ]
    return pl.pallas_call(
        kernel,
        grid_spec=pltpu.PrefetchScalarGridSpec(
            num_scalar_prefetch=1,
            grid=(chunks,),
            in_specs=[
                whole(x), whole(att), whole(att_got),
                pl.BlockSpec((mine, width), lambda j, info: (info[0], 0)),
                pl.BlockSpec((mine, width), lambda j, info: (1 - info[0], 0)),
                whole(first),
                pl.BlockSpec((width, size), lambda j, info: (0, ffn_chunk(j, info, chunks))),
                pl.BlockSpec((size, width), lambda j, info: (ffn_chunk(j, info, chunks), 0)),
                whole(second), whole(cot),
            ],
            out_specs=[spec for _, spec in outs],
            scratch_shapes=[pltpu.VMEM((count, width), BF), pltpu.VMEM((count, width), F32)],
        ),
        out_shape=[shape for shape, _ in outs],
        compiler_params=pltpu.CompilerParams(vmem_limit_bytes=ROOM),
        cost_estimate=cost(15),
        name="ffn_forward",
    )(info, x, att, att_got, out_weight, out_weight, first, up, down, second, cot)


def ffn_inner(info, dz, down, slope, chunks=6):
    count, width = dz.shape
    ff = down.shape[0]
    size = ff // chunks
    half = chunks // 2

    def kernel(info_ref, dz_r, down_r, slope_r, here_o, send_o):
        j = pl.program_id(0)
        grad = (mm_nt(dz_r[...], down_r[...]) * slope_r[...]).astype(BF)

        @pl.when(j < half)
        def _():
            send_o[...] = grad.astype(F32)

        @pl.when(j >= half)
        def _():
            here_o[...] = grad

    return pl.pallas_call(
        kernel,
        grid_spec=pltpu.PrefetchScalarGridSpec(
            num_scalar_prefetch=1,
            grid=(chunks,),
            in_specs=[
                pl.BlockSpec((count, width), lambda j, info: (0, 0)),
                pl.BlockSpec((size, width), lambda j, info: (ffn_chunk(j, info, chunks), 0)),
                pl.BlockSpec((count, size), lambda j, info: (0, j)),
            ],
            out_specs=[
                pl.BlockSpec((count, size), lambda j, info: (0, jnp.maximum(j - half, 0))),
                pl.BlockSpec((count, size), lambda j, info: (0, jnp.minimum(j, half - 1))),
            ],
        ),
        out_shape=[shaped(count, ff // 2, dtype=BF), shaped(count, ff // 2)],
        compiler_params=pltpu.CompilerParams(vmem_limit_bytes=ROOM),
        cost_estimate=cost(8),
        name="ffn_inner",
    )(info, dz, down, slope)


def ffn_back(info, here, send, up, dh, unit, inv, first, deps=(), chunks=6):
    count, width = dh.shape
    ff = up.shape[1]
    size = ff // chunks
    half = chunks // 2

    def kernel(info_ref, here_r, send_r, up_r, dh_r, unit_r, inv_r, first_r, *rest):
        dh_o, go_o, gos_o, sums_o, acc = rest[len(deps) :]
        j = pl.program_id(0)

        @pl.when(j == 0)
        def _():
            acc[...] = dh_r[...]

        @pl.when(j < half)
        def _():
            acc[...] += mm_nt(send_r[...].astype(BF), up_r[...])

        @pl.when(j >= half)
        def _():
            acc[...] += mm_nt(here_r[...], up_r[...])

        @pl.when(j == chunks - 1)
        def _():
            upstream, normed = acc[...], unit_r[...]
            put_sums(sums_o, upstream, normed)
            grad = norm_back(upstream, normed, inv_r[:, 0:1], first_r[0:1, :])
            dh_o[...] = grad
            go_o[...] = grad.astype(BF)
            gos_o[...] = grad.astype(BF).astype(F32)

    def whole(array):
        return pl.BlockSpec(array.shape, lambda j, info: (0, 0))

    flat = pl.BlockSpec((count, width), lambda j, info: (0, 0))
    return pl.pallas_call(
        kernel,
        grid_spec=pltpu.PrefetchScalarGridSpec(
            num_scalar_prefetch=1,
            grid=(chunks,),
            in_specs=[
                pl.BlockSpec((count, size), lambda j, info: (0, jnp.maximum(j - half, 0))),
                pl.BlockSpec((count, size), lambda j, info: (0, jnp.minimum(j, half - 1))),
                pl.BlockSpec((width, size), lambda j, info: (0, ffn_chunk(j, info, chunks))),
                whole(dh), whole(unit), whole(inv), whole(first),
            ] + [ANY] * len(deps),
            out_specs=[flat, flat, flat, pl.BlockSpec((8, width), lambda j, info: (0, 0))],
            scratch_shapes=[pltpu.VMEM((count, width), F32)],
        ),
        out_shape=[
            shaped(count, width), shaped(count, width, dtype=BF), shaped(count, width), shaped(8, width)
        ],
        compiler_params=pltpu.CompilerParams(vmem_limit_bytes=ROOM),
        cost_estimate=cost(9),
        name="ffn_back",
    )(info, here, send, up, dh, unit, inv, first, *deps)


def tag_of(ref, k, spare):
    return ref[0, k, spare : spare + 1, 0:1]


def ordered(info_ref, mine, theirs):
    one = info_ref[1] == 1

    def chip(at, k):
        here = one if at else jnp.logical_not(one)
        return jnp.where(here, mine[0, k], theirs[0, k])

    return [[chip(at, k) for k in (0, 1)] for at in (0, 1)]


def join_plane(info, mine, theirs, spare):
    rows, _, n, m = mine.shape

    def kernel(info_ref, mine_r, theirs_r, up_o, down_o):
        (lead0, tail0), (lead1, tail1) = ordered(info_ref, mine_r, theirs_r)

        def tag(part):
            return part[spare : spare + 1, 0:1]

        is_sum = lax.broadcasted_iota(jnp.int32, (n, m), 0) < spare
        up_o[0] = tail1 + jnp.where(is_sum & (tag(tail0) == tag(tail1)), tail0, 0.0)
        down_o[0] = lead0 + jnp.where(is_sum & (tag(lead1) == tag(lead0)), lead1, 0.0)

    outs = [shaped(rows, n, m), shaped(rows, n, m)]
    return row_call(kernel, "join_plane", info, [mine, theirs], [per_row(mine)] * 2, outs)


def split_plane(info, mine, theirs, ups, downs, spare):
    rows, _, n, m = mine.shape
    steps = len(ups)

    def kernel(info_ref, mine_r, theirs_r, *refs):
        give_o, own_o = refs[2 * steps :]
        (lead0, tail0), (lead1, tail1) = ordered(info_ref, mine_r, theirs_r)

        def tag(part):
            return part[spare : spare + 1, 0:1]

        before = jnp.zeros((n, m), F32)
        behind = jnp.zeros((n, m), F32)
        for k in range(steps):
            up, down = refs[k][0], refs[steps + k][0]
            before = before + jnp.where(tag(up) == tag(lead0), up, 0.0)
            behind = behind + jnp.where(tag(down) == tag(tail1), down, 0.0)
        behind0 = jnp.where(tag(tail0) == tag(lead1), lead1, 0.0) + jnp.where(
            tag(tail0) == tag(tail1), behind, 0.0
        )
        before1 = jnp.where(tag(lead1) == tag(tail0), tail0, 0.0) + jnp.where(
            tag(lead1) == tag(lead0), before, 0.0
        )
        one = info_ref[1] == 1
        give_o[0, 0] = jnp.where(one, before, before1)
        give_o[0, 1] = jnp.where(one, behind0, behind)
        own_o[0, 0] = jnp.where(one, before1, before)
        own_o[0, 1] = jnp.where(one, behind, behind0)

    inputs = [mine, theirs, *ups, *downs]
    outs = [shaped(rows, 2, n, m), shaped(rows, 2, n, m)]
    return row_call(kernel, "split_plane", info, inputs, [per_row(v) for v in inputs], outs)


def exchange(net, info, keep, send, ids_row, chip_len, spare, late=()):
    if not net.fast:
        first, last = jnp.min(ids_row, 2), jnp.max(ids_row, 2)
        pay = jnp.stack([keep, send], 1)
        up, down = pay[:, :, 1], pay[:, :, 0]
        before = jnp.zeros_like(up)
        behind = jnp.zeros_like(up)
        for _ in range(min(net.n_seq // 2 - 1, -(-SEG_MOST // chip_len))):
            up, down = net.shift(up, 1), net.shift(down, -1)
            reached = up[:, 0, spare, 0:1] == first
            before = before + jnp.where(reached[:, :, None, None], up, 0.0)
            reached = down[:, 0, spare, 0:1] == last
            behind = behind + jnp.where(reached[:, :, None, None], down, 0.0)
        return jnp.stack([before[:, 0], behind[:, 0]], 1), jnp.stack([before[:, 1], behind[:, 1]], 1)
    theirs = net.over_x(send)
    up, down = join_plane(info, keep, theirs, spare)
    if late:
        up, down = tie(up, *late[0]), tie(down, *late[0])
    ups, downs = [], []
    for _ in range(min(net.nz - 1, -(-SEG_MOST // (2 * chip_len)))):
        up, down = net.z_up(up), net.z_down(down)
        ups.append(up)
        downs.append(down)
    give, own = split_plane(info, keep, theirs, ups, downs, spare)
    if late:
        give = tie(give, *late[1])
    return own, net.over_x(give)


def body(
    tokens,
    segment_ids,
    features,
    query_weight,
    key_weight,
    value_weight,
    out_weight,
    up_weight,
    down_weight,
    first_gain,
    first_bias,
    second_gain,
    second_bias,
    cotangent,
):
    net = Net(lax.axis_size("dp"), lax.axis_size("seq"))
    rows, length, width = tokens.shape
    heads_all, head_dim, _ = features.shape
    heads = heads_all // 2
    mine = width // 2
    ff = up_weight.shape[1]
    ff_half = ff // 2
    core = net.core
    fast = net.fast
    chip_len = 2 * length
    count = rows * length
    spare = heads // 2 * head_dim + heads // 2
    side = net.x if fast else jnp.zeros_like(core)
    info = jnp.stack([core, side]).astype(jnp.int32)

    tokens_got = net.over_core(tokens.astype(F32))
    ids = segment_ids.astype(F32)
    ids_chip = jnp.concatenate([ids, net.over_core(ids)], 1)
    idr, idc = ids_chip[:, None, :], ids_chip[:, :, None]

    keys, values, fk, keep, send = keys_kernel(
        info, tokens, tokens_got, key_weight, value_weight, features, idc, idr
    )
    queries, fq, num, den = queries_kernel(
        info, tokens, tokens_got, query_weight, features, fk, values, idc, idr
    )
    own, got = exchange(net, info, keep, send, idr, chip_len, spare)
    att, den, att_here, att_send = attend_kernel(info, fq, num, den, own, got, idc, idr)
    att_got = net.over_core(att_send).reshape(count, mine)

    flat = tokens.reshape(count, width)
    first = jnp.stack([first_gain, first_bias])
    second = jnp.stack([second_gain, second_bias])
    (
        y1, y1_send, act, act_send, slope, result, dz, dz_send, dh2, unit, inv, sums_two
    ) = ffn_forward(
        info, flat, att_here.reshape(count, mine), att_got, out_weight, first,
        up_weight, down_weight, second, cotangent.reshape(count, width),
    )
    y1_got = net.over_core(y1_send)
    act_got = net.over_core(act_send)
    dz_got = net.over_core(dz_send)
    df, df_send = ffn_inner(info, dz, down_weight, slope)
    df_got = net.over_core(df_send)

    one = jnp.where(net.seq < 0, 0.5, 1.0).astype(F32)

    def rounded(wide):
        return (wide * one).astype(BF)

    def both(a, b):
        return jnp.concatenate([a, rounded(b)], 0)

    late = []
    deps = ()
    if fast:
        bits_mine, bits_other = stage_bits(net, 0), stage_bits(net, 0, 1 - core)
        ffn_parts = (y1, y1_got, df, df_got, act, act_got, dz, dz_got)
        f_sends = ffn_products(1 - bits_mine, *ffn_parts)
        f_keeps = ffn_products(bits_mine, *ffn_parts, deps=f_sends)
        f_gots = moves(net, f_sends, 0)
        deps = f_sends
    else:
        grad_up = total(net, mm_tn(both(y1, y1_got), both(df, df_got)), 1)
        grad_down = total(net, mm_tn(both(act, act_got), both(dz, dz_got)), 0)

    dh1, go, go_send, sums_one = ffn_back(
        info, df, df_send, up_weight, dh2, unit, inv, first, deps
    )
    go_got = net.over_core(go_send)
    dn, dd, keep_d, send_d = grads_one_kernel(
        info, go.reshape(rows, length, width), go_got.reshape(rows, length, width), out_weight,
        att, den, fq, idc, idr,
    )
    if fast:
        f_sends, f_keeps = add_stage(net, f_keeps, f_gots, 1, [send_d])
        f_gots = moves(net, f_sends, 1)
        late.append(f_sends)
    dq, dfk, dv = grads_two_kernel(
        info, fq, fk, queries, values, dn, dd, features, own, got, idc, idr, deps=f_sends if fast else ()
    )
    if fast:
        f_sends, f_keeps = add_stage(net, f_keeps, f_gots, 2, [dq])
        f_gots = moves(net, f_sends, 2)
        late.append(f_sends)
    own_d, got_d = exchange(net, info, keep_d, send_d, idr, chip_len, spare, late)
    if fast:
        f_sends, f_keeps = add_stage(net, f_keeps, f_gots, 3)
        f_gots = moves(net, f_sends, 3)
        f_own = last_add(f_keeps, f_gots)
        f_gots = moves(net, f_own, 3)
    dk, dv = grads_three_kernel(
        info, fk, keys, values, dfk, dv, features, own_d, got_d, idc, idr, deps=f_own if fast else ()
    )

    chip_flat = (rows * chip_len, mine)
    if fast:
        sums = jnp.concatenate([sums_one[:2], sums_two[:2]])
        small = (sums + net.over_core(sums)).reshape(8, mine)
        attn_parts = (
            flat, tokens_got.reshape(count, width),
            dq.reshape(chip_flat), dk.reshape(chip_flat), dv.reshape(chip_flat),
            att.reshape(chip_flat), go, go_got, small,
        )

        def over_core(parts):
            return [net.over_core(part) for part in parts]

        a_sends = attn_products(1 - bits_mine, *attn_parts)
        a_gots = moves(net, a_sends, 0)
        a_keeps = attn_products(bits_mine, *attn_parts, deps=a_sends)
        f_own = join_stage(net, f_own, f_gots, 3, a_keeps)
        f_gots = moves(net, f_own, 2)
        a_sends, a_keeps = add_stage(net, a_keeps, a_gots, 1, f_own)
        a_gots = moves(net, a_sends, 1)
        f_one = join_stage(net, f_own, f_gots, 2, a_sends)
        f_two = moves(net, f_one, 1)
        f_one_core = over_core(f_one)
        a_sends, a_keeps = add_stage(net, a_keeps, a_gots, 2, f_one)
        a_gots = moves(net, a_sends, 2)
        shapes = [shaped(*w.shape) for w in (up_weight, down_weight)]
        copies = ffn_copies(width, ff_half)
        outs = place_pieces(
            net, [(f_one, 0, 0, 0), (f_one_core, 1, 0, 0)], shapes, copies, a_sends
        )
        f_three = moves(net, f_one, 0)
        a_sends, a_keeps = add_stage(net, a_keeps, a_gots, 3, [*outs, *f_two])
        a_gots = moves(net, a_sends, 3)
        f_two_core = over_core(f_two)
        outs = place_pieces(
            net, [(f_two, 0, 0, 1), (f_two_core, 1, 0, 1)], outs, copies, a_sends
        )
        f_four = moves(net, f_two, 0)
        a_own = last_add(a_keeps, a_gots, [*outs, *f_three])
        a_gots = moves(net, a_own, 3)
        f_three_core = over_core(f_three)
        outs = place_pieces(
            net, [(f_three, 0, 1, 0), (f_three_core, 1, 1, 0)], outs, copies, a_own
        )
        a_own = join_stage(net, a_own, a_gots, 3, outs)
        a_gots = moves(net, a_own, 2)
        here, share_send = shares_kernel(
            info, dq, dk, dv, query_weight, key_weight, value_weight, deps=a_own
        )
        a_one = join_stage(net, a_own, a_gots, 2, [here, *f_four])
        a_two = moves(net, a_one, 1)
        a_three = moves(net, a_one, 0)
        f_four_core = over_core(f_four)
        a_one_core = over_core(a_one)
        grad_up, grad_down = place_pieces(
            net, [(f_four, 0, 1, 1), (f_four_core, 1, 1, 1)], outs, copies, a_one
        )
        shapes = [shaped(width, width)] * 4
        copies = attn_copies(mine)
        outs = place_pieces(
            net, [(a_one, 0, 0, 0), (a_one_core, 1, 0, 0)], shapes, copies, [grad_up, *a_two]
        )
        a_four = moves(net, a_two, 0)
        a_two_core = over_core(a_two)
        outs = place_pieces(
            net, [(a_two, 0, 0, 1), (a_two_core, 1, 0, 1)], outs, copies, a_three
        )
        a_three_core = over_core(a_three)
        outs = place_pieces(
            net, [(a_three, 0, 1, 0), (a_three_core, 1, 1, 0)], outs, copies
        )
        outs = place_pieces(net, [(a_four, 0, 1, 1)], outs, copies)
        grad_query, grad_key, grad_value, grad_out = place_pieces(
            net, [(over_core(a_four), 1, 1, 1)], outs, copies
        )
        at = mine - (mine + mine // 3 + SPARE_ROWS) // 2 + mine // 3
        one, two = a_one[1][at : at + 8], a_two[1][at : at + 8]
        small = jnp.where(stage_bit(net, 1, 1, core) == 1, one, two).reshape(4, width)
    else:
        x_chip = jnp.concatenate([tokens, rounded(tokens_got)], 1).reshape(rows * chip_len, width)
        go_chip = jnp.concatenate(
            [go.reshape(rows, length, width), rounded(go_got).reshape(rows, length, width)], 1
        ).reshape(rows * chip_len, width)
        grad_query = total(net, mm_tn(x_chip, dq.reshape(chip_flat)), 1)
        grad_key = total(net, mm_tn(x_chip, dk.reshape(chip_flat)), 1)
        grad_value = total(net, mm_tn(x_chip, dv.reshape(chip_flat)), 1)
        grad_out = total(net, mm_tn(att.astype(BF).reshape(chip_flat), go_chip), 0)

        here, share_send = shares_kernel(info, dq, dk, dv, query_weight, key_weight, value_weight)
        small = lax.psum(jnp.concatenate([sums_one[:2], sums_two[:2]]), AXES)

    grad_input = dh1.reshape(rows, length, width) + here + net.over_core(share_send)
    return (
        result.reshape(rows, length, width),
        grad_input.astype(BF),
        grad_query,
        grad_key,
        grad_value,
        grad_out,
        grad_up,
        grad_down,
        small[0],
        small[1],
        small[2],
        small[3],
    )


def solution(mesh):
    split = P("dp", "seq", None)
    placed = (split, P("dp", "seq")) + (P(),) * 11 + (split,)
    return jax.shard_map(
        body,
        mesh=mesh,
        in_specs=placed,
        out_specs=(split, split) + (P(),) * 10,
        check_vma=False,
    )
```

```python
import jax
import jax.numpy as jnp
from jax import lax
from jax.experimental import pallas as pl
from jax.experimental.pallas import tpu as pltpu
from jax.sharding import PartitionSpec as P

SEG_MOST = 2048
SPARE_ROWS = 64
EPSILON = 1e-06
AXES = ("dp", "seq")
BF = jnp.bfloat16
F32 = jnp.float32
ANY = pl.BlockSpec(memory_space=pl.ANY)
HBM = pl.BlockSpec(memory_space=pltpu.HBM)
ROOM = 20 << 20
SMALL = 14 << 20


SCALE = 3


def cost(us):
    return pl.CostEstimate(flops=int(us * 1e9), bytes_accessed=1, transcendentals=0)


def shaped(*shape, dtype=F32):
    return jax.ShapeDtypeStruct(shape, dtype)


def mm(a, b):
    return jnp.dot(a, b, preferred_element_type=F32)


def mm_nt(a, b):
    return lax.dot_general(a, b, (((1,), (1,)), ((), ())), preferred_element_type=F32)


def mm_tn(a, b):
    return lax.dot_general(a, b, (((0,), (0,)), ((), ())), preferred_element_type=F32)


def dslice(a, start, size, axis=0):
    return lax.dynamic_slice_in_dim(a, start, size, axis)


class Net:
    def __init__(self, n_dp, n_seq):
        self.n_dp, self.n_seq = n_dp, n_seq
        self.nz = 4
        self.nx = n_seq // 8
        self.fast = n_dp == 2 and n_seq == 16
        seq = lax.axis_index("seq")
        self.y = lax.axis_index("dp")
        self.core = seq % 2
        self.x = (seq // 2) % self.nx
        self.z = seq // (2 * self.nx)
        self.seq = seq

    def perm(self, move):
        pairs = []
        for y in range(self.n_dp):
            for s in range(self.n_seq):
                target = move(y, s // (2 * self.nx), (s // 2) % self.nx, s % 2)
                if target is not None:
                    ty, tz, tx, tc = target
                    pairs.append((y * self.n_seq + s, ty * self.n_seq + (tz * self.nx + tx) * 2 + tc))
        return pairs

    def send(self, value, move):
        return lax.ppermute(value, AXES, self.perm(move))

    def over_core(self, value):
        return self.send(value, lambda y, z, x, c: (y, z, x, 1 - c))

    def over_x(self, value):
        return self.send(value, lambda y, z, x, c: (y, z, 1 - x, c))

    def z_up(self, value):
        return self.send(value, lambda y, z, x, c: (y, z + 1, x, c) if z < 3 else None)

    def z_down(self, value):
        return self.send(value, lambda y, z, x, c: (y, z - 1, x, c) if z > 0 else None)

    def shift(self, value, step):
        chips = self.n_seq // 2
        pairs = []
        for y in range(self.n_dp):
            for s in range(self.n_seq):
                if 0 <= s // 2 + step < chips:
                    pairs.append((y * self.n_seq + s, y * self.n_seq + s + 2 * step))
        return lax.ppermute(value, AXES, pairs)


ORDERS = ((("x", "y", "1", "2"), ("y", "x", "2", "1")), (("1", "2", "x", "y"), ("2", "1", "x", "y")))


def stage_move(net, value, stream, stage):
    def move(y, z, x, c):
        axis = ORDERS[stream][c][stage]
        return {
            "x": (y, z, 1 - x, c),
            "y": (1 - y, z, x, c),
            "1": (y, z ^ 1, x, c),
            "2": (y, z ^ 2, x, c),
        }[axis]

    return net.send(value, move)


def stage_bit(net, stream, stage, core):
    place = {"x": net.x, "y": net.y, "1": net.z % 2, "2": net.z // 2}
    zero, one = (place[ORDERS[stream][c][stage]] for c in (0, 1))
    return jnp.where(core == 0, zero, one)


def tie(value, *deps):
    def kernel(*refs):
        pass

    anywhere = pl.BlockSpec(memory_space=pl.ANY)
    return pl.pallas_call(
        kernel,
        in_specs=[anywhere] * (1 + len(deps)),
        out_specs=anywhere,
        out_shape=jax.ShapeDtypeStruct(value.shape, value.dtype),
        input_output_aliases={0: 0},
        compiler_params=pltpu.CompilerParams(vmem_limit_bytes=SMALL),
        cost_estimate=cost(0.1),
        name="tie",
    )(value, *deps)


def moves(net, parts, stage):
    return [stage_move(net, part, i, stage) for i, part in enumerate(parts)]


def stage_bits(net, stage, core=None):
    core = net.core if core is None else core
    return jnp.stack([stage_bit(net, i, stage, core) for i in range(2)]).astype(jnp.int32)


def add_stage(net, keeps, gots, stage, deps=()):
    steps = max(1, keeps[0].shape[0] // 288)

    def kernel(bits_ref, *refs):
        outs = refs[8 + len(deps) :]
        for i in range(4):
            outs[i][...] = refs[2 * i][...] + refs[2 * i + 1][...]

    in_specs, inputs, out_specs, shapes = [], [], [], []
    for side in (0, 1):
        for i, (keep, got) in enumerate(zip(keeps, gots)):
            half, width = keep.shape[0] // 2, keep.shape[1]
            block = (half // steps, width)
            spec = pl.BlockSpec(
                block,
                lambda r, bits, i=i, side=side: (
                    (bits[i] if side else 1 - bits[i]) * steps + r,
                    0,
                ),
            )
            in_specs += [spec, spec]
            inputs += [keep, got]
            out_specs.append(pl.BlockSpec(block, lambda r, bits: (r, 0)))
            shapes.append(shaped(half, width))
    in_specs += [ANY] * len(deps)
    outs = pl.pallas_call(
        kernel,
        grid_spec=pltpu.PrefetchScalarGridSpec(
            num_scalar_prefetch=1, grid=(steps,), in_specs=in_specs, out_specs=out_specs
        ),
        out_shape=shapes,
        compiler_params=pltpu.CompilerParams(vmem_limit_bytes=SMALL),
        cost_estimate=cost(4 * SCALE),
        name="add_stage",
    )(stage_bits(net, stage), *inputs, *deps)
    return outs[:2], outs[2:]


def last_add(keeps, gots, deps=()):
    def kernel(*refs):
        outs = refs[4 + len(deps) :]
        for i in range(2):
            outs[i][...] = refs[i][...] + refs[2 + i][...]

    whole = pl.BlockSpec(memory_space=pltpu.VMEM)
    return pl.pallas_call(
        kernel,
        in_specs=[whole] * 4 + [ANY] * len(deps),
        out_specs=[whole] * 2,
        out_shape=[shaped(*k.shape) for k in keeps],
        compiler_params=pltpu.CompilerParams(vmem_limit_bytes=SMALL),
        cost_estimate=cost(1.5 * SCALE),
        name="last_add",
    )(*keeps, *gots, *deps)


def join_stage(net, parts, gots, stage, deps=()):
    steps = max(1, parts[0].shape[0] // 144)

    def kernel(bits_ref, *refs):
        outs = refs[4 + len(deps) :]
        for i in range(2):
            bit = bits_ref[i]
            outs[i][pl.ds(bit, 1)] = refs[2 * i][...][None]
            outs[i][pl.ds(1 - bit, 1)] = refs[2 * i + 1][...][None]

    in_specs, out_specs, shapes = [], [], []
    for part in parts:
        n, width = part.shape
        rows = n // steps
        in_specs += [pl.BlockSpec((rows, width), lambda r, bits: (r, 0))] * 2
        out_specs.append(pl.BlockSpec((2, rows, width), lambda r, bits: (0, r, 0)))
        shapes.append(shaped(2, n, width))
    outs = pl.pallas_call(
        kernel,
        grid_spec=pltpu.PrefetchScalarGridSpec(
            num_scalar_prefetch=1,
            grid=(steps,),
            in_specs=in_specs + [ANY] * len(deps),
            out_specs=out_specs,
        ),
        out_shape=shapes,
        compiler_params=pltpu.CompilerParams(vmem_limit_bytes=SMALL),
        cost_estimate=cost(3 * SCALE),
        name="join_stage",
    )(stage_bits(net, stage), *[v for pair in zip(parts, gots) for v in pair], *deps)
    return [out.reshape(2 * out.shape[1], out.shape[2]) for out in outs]


def tn(a, a_other, b, b_other):
    return mm_tn(a, b) + mm_tn(a_other.astype(BF), b_other.astype(BF))


def picked_columns(count, size, index):
    return pl.BlockSpec((count, size), lambda g, bits: (0, index(bits)))


def whole_of(array):
    return pl.BlockSpec(array.shape, lambda g, bits: (0,) * array.ndim)


def down_products(bits, act, act_other, gz, gz_other, deps=()):
    count, width = gz.shape
    unit = act.shape[1] // 12
    sizes = (5 * unit, unit)

    def kernel(bits_ref, a0, a0o, a1, a1o, gz_r, gzo_r, *rest):
        outs, scratch, sems = rest[len(deps) : -2], rest[-2], rest[-1]
        scratch[: sizes[0], :] = tn(a0[...], a0o[...], gz_r[...], gzo_r[...])
        scratch[sizes[0] :, :] = tn(a1[...], a1o[...], gz_r[...], gzo_r[...])
        copies = [
            pltpu.make_async_copy(
                scratch.at[: sizes[0]], outs[0].at[outs[0].shape[0] - sizes[0] :], sems.at[0]
            ),
            pltpu.make_async_copy(
                scratch.at[sizes[0] :], outs[1].at[outs[1].shape[0] - sizes[1] :], sems.at[1]
            ),
        ]
        for copy in copies:
            copy.start()
        for copy in copies:
            copy.wait()

    first = picked_columns(count, sizes[0], lambda bits: bits[0])
    second = picked_columns(count, sizes[1], lambda bits: 10 + bits[1])
    up_rows = act.shape[1] // width * (width // 6)
    return pl.pallas_call(
        kernel,
        grid_spec=pltpu.PrefetchScalarGridSpec(
            num_scalar_prefetch=1,
            grid=(1,),
            in_specs=[first, first, second, second, whole_of(gz), whole_of(gz_other)]
            + [ANY] * len(deps),
            out_specs=[ANY, ANY],
            scratch_shapes=[
                pltpu.VMEM((6 * unit, width), F32),
                pltpu.SemaphoreType.DMA((2,)),
            ],
        ),
        out_shape=[shaped(2 * up_rows + sizes[0], width), shaped(up_rows + sizes[1], width)],
        compiler_params=pltpu.CompilerParams(vmem_limit_bytes=ROOM),
        cost_estimate=cost(4 * SCALE),
        name="down_products",
    )(bits, act, act_other, act, act_other, gz, gz_other, *deps)


def up_products(bits, y1, y1_other, gi, gi_other, outs, big):
    count, width = y1.shape
    u = width // 6
    parts = gi.shape[1] // width

    def kernel(bits_ref, y1_r, y1o_r, gi_r, gio_r, *rest):
        outs = rest[2:]

        def fill(out):
            y, yo = y1_r[...], y1o_r[...]
            for part in range(parts):
                cut = slice(part * width, (part + 1) * width)
                out[part * u : (part + 1) * u, :] = tn(y, yo, gi_r[:, cut], gio_r[:, cut])

        pl.when(pl.program_id(0) < 2)(lambda: fill(outs[0]))
        pl.when(pl.program_id(0) == 2)(lambda: fill(outs[1]))

    picked = pl.BlockSpec(
        (count, u), lambda i, bits: (0, jnp.where(i < 2, 2 * bits[0] + i, 4 + bits[1]))
    )
    return pl.pallas_call(
        kernel,
        grid_spec=pltpu.PrefetchScalarGridSpec(
            num_scalar_prefetch=1,
            grid=(3,),
            in_specs=[picked, picked, whole_of(gi), whole_of(gi_other), ANY, ANY],
            out_specs=[
                pl.BlockSpec((parts * u, width), lambda i, bits: (jnp.minimum(i, 1), 0)),
                pl.BlockSpec((parts * u, width), lambda i, bits: (0, 0)),
            ],
        ),
        out_shape=[shaped(*o.shape) for o in outs],
        input_output_aliases={5: 0, 6: 1},
        compiler_params=pltpu.CompilerParams(vmem_limit_bytes=ROOM),
        cost_estimate=cost(big),
        name="up_products",
    )(bits, y1, y1_other, gi, gi_other, *outs)


def attn_products(bits, x, x_other, dq, dk, dv, attn, go, go_other, small, deps=()):
    count, width = x.shape
    mine = attn.shape[1]
    cut = 2 * mine // 3

    def kernel(
        bits_ref, x0, x0o, x1, x1o, dq_r, dk_r, dv_r, attn_r, go_r, goo_r, small_r, *rest
    ):
        one, two = rest[len(deps) :]
        x, xo = x0[...], x0o[...].astype(BF)
        one[:mine, :] = tn(x, xo, dq_r[:count], dq_r[count:])
        one[mine : 2 * mine, :] = tn(x, xo, dk_r[:count], dk_r[count:])
        part = attn_r[...].astype(BF)
        one[2 * mine : 3 * mine, :] = tn(part[:count], part[count:], go_r[...], goo_r[...])
        one[3 * mine :, :] = tn(x[:, :cut], xo[:, :cut], dv_r[:count], dv_r[count:])
        rest_rows = mine - cut
        two[:rest_rows, :] = tn(x1[:, cut:], x1o[:, cut:], dv_r[:count], dv_r[count:])
        two[rest_rows:, :] = jnp.zeros((SPARE_ROWS, mine), F32)
        two[rest_rows : rest_rows + 8, :] = small_r[...]

    first = picked_columns(count, mine, lambda bits: bits[0])
    second = picked_columns(count, mine, lambda bits: bits[1])
    return pl.pallas_call(
        kernel,
        grid_spec=pltpu.PrefetchScalarGridSpec(
            num_scalar_prefetch=1,
            grid=(1,),
            in_specs=[first, first, second, second]
            + [whole_of(v) for v in (dq, dk, dv, attn)]
            + [first, first, whole_of(small)]
            + [ANY] * len(deps),
            out_specs=[
                pl.BlockSpec((3 * mine + cut, mine), lambda g, bits: (0, 0)),
                pl.BlockSpec((mine - cut + SPARE_ROWS, mine), lambda g, bits: (0, 0)),
            ],
        ),
        out_shape=[shaped(3 * mine + cut, mine), shaped(mine - cut + SPARE_ROWS, mine)],
        compiler_params=pltpu.CompilerParams(vmem_limit_bytes=ROOM),
        cost_estimate=cost(4 * SCALE),
        name="attn_products",
    )(bits, x, x_other, x, x_other, dq, dk, dv, attn, go, go_other, small, *deps)


def place_pieces(net, pieces, outs, copies, deps=()):
    fresh = isinstance(outs[0], jax.ShapeDtypeStruct)
    n_out, n = len(outs), len(pieces)
    inputs = [part for piece in pieces for part in piece[0]]
    scalars = []
    for _, other_core, other_first, other_second in pieces:
        core = 1 - net.core if other_core else net.core
        scalars.append(core)
        for i in range(2):
            for stage, flip in ((0, other_first), (1, other_second)):
                bit = stage_bit(net, i, stage, core)
                scalars.append(1 - bit if flip else bit)
    where = jnp.stack(scalars).astype(jnp.int32)

    def kernel(where_ref, *refs):
        srcs = refs[: 2 * n]
        dests = refs[-(2 * n + 3 + n_out) : -(2 * n + 3)]
        refs[-(2 * n + 3)][...] = jnp.zeros((8, 128), F32)
        held, (arrive, sems) = refs[-(2 * n + 2) : -2], refs[-2:]
        loads = [pltpu.make_async_copy(srcs[j], held[j], arrive.at[j]) for j in range(2 * n)]
        for load in loads:
            load.start()

        def each(j, act):
            piece, i = j // 2, j % 2
            core = where_ref[5 * piece]
            first, second = where_ref[5 * piece + 1 + 2 * i], where_ref[5 * piece + 2 + 2 * i]
            for quarter in (0, 1):

                @pl.when(second == quarter)
                def _():
                    for k, (src, dest) in enumerate(copies(i, quarter, core, first, held[j], dests)):
                        act(pltpu.make_async_copy(src, dest, sems.at[j, k]))

        for j in range(2 * n):
            loads[j].wait()
            each(j, lambda copy: copy.start())
        for j in range(2 * n):
            each(j, lambda copy: copy.wait())

    operands = inputs + ([] if fresh else list(outs)) + list(deps)
    *outs, done = pl.pallas_call(
        kernel,
        grid_spec=pltpu.PrefetchScalarGridSpec(
            num_scalar_prefetch=1,
            grid=(1,),
            in_specs=[ANY] * len(inputs) + [HBM] * (0 if fresh else n_out) + [ANY] * len(deps),
            out_specs=[HBM] * n_out + [pl.BlockSpec((8, 128), lambda g, where: (0, 0))],
            scratch_shapes=[pltpu.VMEM(part.shape, F32) for part in inputs] + [
                pltpu.SemaphoreType.DMA((2 * n,)),
                pltpu.SemaphoreType.DMA((2 * n, 6)),
            ],
        ),
        out_shape=[shaped(*o.shape) for o in outs] + [shaped(8, 128)],
        input_output_aliases={} if fresh else {1 + 2 * n + i: i for i in range(n_out)},
        compiler_params=pltpu.CompilerParams(vmem_limit_bytes=ROOM),
        cost_estimate=cost(4.5 * SCALE),
        name="place_pieces",
    )(where, *operands)
    return outs, [done]


def rows_at(ref, start, size, step, lanes=None):
    start = pl.multiple_of(start, step)
    return ref.at[pl.ds(start, size)] if lanes is None else ref.at[pl.ds(start, size), lanes]


def spans(sizes, at, length):
    start = 0
    for k, size in enumerate(sizes):
        low, high = max(start, at), min(start + size, at + length)
        if low < high:
            yield k, low - start, low - at, high - low
        start += size


def ffn_copies(width, ff_half):
    u, unit = width // 6, ff_half // 12
    parts = ff_half // width

    def copies(i, quarter, c, b, src, dests):
        up, down = dests
        blocks = 1 if i else 2
        sizes = [u] * (parts * blocks) + [unit if i else 5 * unit]
        length = src.shape[0]
        for k, row, at, n in spans(sizes, quarter * length, length):
            if k < parts * blocks:
                block = 4 + b if i else 2 * b + k // parts
                lanes = pl.ds(pl.multiple_of(c * ff_half + k % parts * width, 128), width)
                dest = rows_at(up, block * u + row, n, 8, lanes)
            else:
                start = 10 * unit + b * unit if i else 5 * unit * b
                dest = rows_at(down, c * ff_half + start + row, n, 8)
            yield src.at[at : at + n], dest

    return copies


def attn_copies(mine):
    def copies(i, quarter, c, b, src, dests):
        own = pl.ds(pl.multiple_of(c * mine, 128), mine)
        half = pl.ds(pl.multiple_of(b * mine, 128), mine)
        cut = 2 * mine // 3
        sizes = [mine - cut] if i else [mine] * 3 + [cut]
        length = src.shape[0]
        for k, row, at, n in spans(sizes, quarter * length, length):
            if i:
                dest = rows_at(dests[2], b * mine + cut + row, n, 8, own)
            elif k != 2:
                dest = rows_at(dests[min(k, 2)], b * mine + row, n, 8, own)
            else:
                dest = rows_at(dests[3], c * mine + row, n, 8, half)
            yield src.at[at : at + n], dest

    return copies


def total(net, half, axis):
    size = half.shape[axis]
    shape = tuple(2 * n if i == axis else n for i, n in enumerate(half.shape))
    own = lax.dynamic_update_slice_in_dim(jnp.zeros(shape, F32), half, net.core * size, axis)
    return lax.psum(own, AXES)


def per_row(array):
    rest = array.shape[1:]
    return pl.BlockSpec((1, *rest), lambda r, info: (r, *(0 for _ in rest)))


COSTS = {"keys": 10, "queries": 8, "attend": 6, "grads_one": 3, "grads_two": 12, "grads_three": 8, "shares": 3 * SCALE, "join_plane": 3, "split_plane": 3}


def row_call(kernel, name, info, inputs, in_specs, outs, deps=(), flops=0):
    n_in = len(inputs)
    rows = outs[0].shape[0]

    def run(info_ref, *refs):
        kernel(info_ref, *refs[:n_in], *refs[n_in + len(deps) :])

    size = sum(v.size * v.dtype.itemsize for v in [*inputs, *outs])
    return pl.pallas_call(
        run,
        grid_spec=pltpu.PrefetchScalarGridSpec(
            num_scalar_prefetch=1,
            grid=(rows,),
            in_specs=list(in_specs) + [ANY] * len(deps),
            out_specs=[per_row(o) for o in outs],
        ),
        out_shape=outs,
        compiler_params=pltpu.CompilerParams(vmem_limit_bytes=ROOM),
        cost_estimate=cost(COSTS[name]),
        name=name,
    )(info, *inputs, *deps)


def edges(idc_ref, idr_ref):
    row = idr_ref[0]
    first = jnp.min(row, axis=1, keepdims=True)
    last = jnp.max(row, axis=1, keepdims=True)
    return idc_ref[0] == first, idc_ref[0] == last, first, last


def phi(part, feats):
    head_dim, feat_count = feats.shape
    wide = part.astype(F32)
    square = jnp.sum(wide * wide, -1, keepdims=True)
    inner = mm(part, feats) * head_dim ** (-0.25) - square * (0.5 * head_dim ** (-0.5))
    return (jnp.exp(inner) * feat_count ** (-0.5)).astype(BF)


def put_edges(info_ref, keep, send, h, heads, sums, lead_z, tail_z):
    half = heads // 2
    group, at = h // half, h % half
    e = sums.shape[0] // 2

    def put(ref):
        ref[0, 0, at * e : (at + 1) * e, :] = sums[:e]
        ref[0, 1, at * e : (at + 1) * e, :] = sums[e:]
        ref[0, 0, half * e + at : half * e + at + 1, :] = lead_z
        ref[0, 1, half * e + at : half * e + at + 1, :] = tail_z

    @pl.when(info_ref[1] == group)
    def _():
        put(keep)

    @pl.when(info_ref[1] != group)
    def _():
        put(send)


def put_tags(keep, send, spare, first, last):
    n, m = keep.shape[2:]
    for ref in (keep, send):
        ref[0, 0, spare:, :] = jnp.broadcast_to(first, (n - spare, m))
        ref[0, 1, spare:, :] = jnp.broadcast_to(last, (n - spare, m))


def weight_columns(weight, mine):
    return pl.BlockSpec((weight.shape[0], mine), lambda r, info: (0, info[0]))


def head_features(features, heads):
    return pl.BlockSpec((heads, *features.shape[1:]), lambda r, info: (info[0], 0, 0))


def keys_kernel(info, x, x_got, key_weight, value_weight, features, idc, idr):
    rows, length, width = x.shape
    mine, heads = width // 2, features.shape[0] // 2
    e, m = features.shape[1:]
    n = heads // 2 * e + 8
    spare = heads // 2 * e + heads // 2

    def kernel(info_ref, x_r, xg_r, wk_r, wv_r, f_r, idc_r, idr_r, k_o, v_o, fk_o, keep, send):
        chip = jnp.concatenate([x_r[0], xg_r[0].astype(BF)], 0)
        keys = mm(chip, wk_r[...]).astype(BF)
        values = mm(chip, wv_r[...]).astype(BF)
        k_o[0] = keys
        v_o[0] = values
        lead, tail, first, last = edges(idc_r, idr_r)
        masks = jnp.concatenate([lead.astype(F32), tail.astype(F32)], 1).astype(BF)
        lead_b, tail_b = masks[:, 0:1], masks[:, 1:2]
        for h in range(heads):
            cut = slice(h * e, (h + 1) * e)
            feat = phi(keys[:, cut], f_r[h])
            fk_o[0, h] = feat
            part = values[:, cut]
            sums = mm_tn(jnp.concatenate([part * lead_b, part * tail_b], 1), feat)
            zs = mm_tn(masks, feat)
            put_edges(info_ref, keep, send, h, heads, sums, zs[0:1], zs[1:2])
        put_tags(keep, send, spare, first, last)

    outs = [
        shaped(rows, 2 * length, mine, dtype=BF),
        shaped(rows, 2 * length, mine, dtype=BF),
        shaped(rows, heads, 2 * length, m, dtype=BF),
        shaped(rows, 2, n, m),
        shaped(rows, 2, n, m),
    ]
    specs = [
        per_row(x), per_row(x_got),
        weight_columns(key_weight, mine), weight_columns(value_weight, mine),
        head_features(features, heads), per_row(idc), per_row(idr),
    ]
    return row_call(
        kernel, "keys", info, [x, x_got, key_weight, value_weight, features, idc, idr], specs, outs,
        flops=rows * length * width * mine * 10,
    )


def queries_kernel(info, x, x_got, query_weight, features, fk, values, idc, idr, deps=()):
    rows, length, width = x.shape
    mine, heads = width // 2, features.shape[0] // 2
    e, m = features.shape[1:]

    def kernel(info_ref, x_r, xg_r, wq_r, f_r, fk_r, v_r, idc_r, idr_r, q_o, fq_o, num_o, den_o):
        chip = jnp.concatenate([x_r[0], xg_r[0].astype(BF)], 0)
        queries = mm(chip, wq_r[...]).astype(BF)
        q_o[0] = queries
        same = idc_r[0] == idr_r[0]
        lane = lax.broadcasted_iota(jnp.int32, (2 * length, 128), 1)
        dens = jnp.ones((2 * length, 128), F32)
        for h in range(heads):
            cut = slice(h * e, (h + 1) * e)
            feat = phi(queries[:, cut], f_r[h])
            fq_o[0, h] = feat
            scores = jnp.where(same, mm_nt(feat, fk_r[0, h]), 0.0)
            num_o[0, :, cut] = mm(scores.astype(BF), v_r[0, :, cut])
            dens = jnp.where(lane == h, jnp.sum(scores, -1, keepdims=True), dens)
        den_o[0] = dens

    outs = [
        shaped(rows, 2 * length, mine, dtype=BF),
        shaped(rows, heads, 2 * length, m, dtype=BF),
        shaped(rows, 2 * length, mine),
        shaped(rows, 2 * length, 128),
    ]
    specs = [
        per_row(x), per_row(x_got), weight_columns(query_weight, mine),
        head_features(features, heads), per_row(fk), per_row(values), per_row(idc), per_row(idr),
    ]
    return row_call(
        kernel, "queries", info,
        [x, x_got, query_weight, features, fk, values, idc, idr], specs, outs, deps,
        flops=rows * length * width * mine * 12,
    )


def carry_of(info_ref, own_r, got_r, h, heads, e):
    half = heads // 2
    group, at = h // half, h % half
    flag = info_ref[1] == group

    def picked(k, rows):
        return jnp.where(flag, own_r[0, k, rows, :], got_r[0, k, rows, :])

    kv = slice(at * e, (at + 1) * e)
    z = slice(half * e + at, half * e + at + 1)
    return picked(0, kv), picked(1, kv), picked(0, z), picked(1, z)


def attend_kernel(info, fq, num, den, own, got, idc, idr):
    rows, heads, chip_len, m = fq.shape
    mine = num.shape[2]
    e = mine // heads
    length = chip_len // 2

    def kernel(info_ref, fq_r, num_r, den_r, own_r, got_r, idc_r, idr_r, att_o, den_o, here_o, send_o):
        lead, tail, _, _ = edges(idc_r, idr_r)
        lead, tail = lead.astype(F32), tail.astype(F32)
        lane = lax.broadcasted_iota(jnp.int32, (chip_len, 128), 1)
        dens = den_r[0]
        for h in range(heads):
            cut = slice(h * e, (h + 1) * e)
            before, behind, zb, za = carry_of(info_ref, own_r, got_r, h, heads, e)
            feat = fq_r[0, h]
            more = mm_nt(feat, jnp.concatenate([before, behind], 0).astype(BF))
            numer = num_r[0, :, cut] + lead * more[:, :e] + tail * more[:, e:]
            extra = jnp.sum(feat.astype(F32) * (lead * zb + tail * za), -1, keepdims=True)
            denom = den_r[0, :, h : h + 1] + extra
            dens = jnp.where(lane == h, denom, dens)
            att = numer / denom
            att_o[0, :, cut] = att
            rounded = att.astype(BF)
            here_o[0, :, cut] = rounded[:length]
            send_o[0, :, cut] = rounded[length:].astype(F32)
        den_o[0] = dens

    outs = [
        shaped(rows, chip_len, mine),
        shaped(rows, chip_len, 128),
        shaped(rows, length, mine, dtype=BF),
        shaped(rows, length, mine),
    ]
    inputs = [fq, num, den, own, got, idc, idr]
    return row_call(
        kernel, "attend", info, inputs, [per_row(v) for v in inputs], outs,
        flops=rows * chip_len * mine * m * 6,
    )


def grads_one_kernel(info, go, go_got, out_weight, att, den, fq, idc, idr):
    rows, length, width = go.shape
    heads, m = fq.shape[1], fq.shape[3]
    mine = width // 2
    e = mine // heads
    n = heads // 2 * e + 8
    spare = heads // 2 * e + heads // 2

    def kernel(info_ref, go_r, gog_r, wo_r, att_r, den_r, fq_r, idc_r, idr_r, dn_o, dd_o, keep, send):
        chip = jnp.concatenate([go_r[0], gog_r[0].astype(BF)], 0)
        pulls = mm_nt(chip, wo_r[...])
        lead, tail, first, last = edges(idc_r, idr_r)
        lead, tail = lead.astype(F32), tail.astype(F32)
        lane = lax.broadcasted_iota(jnp.int32, (2 * length, 128), 1)
        dds = jnp.zeros((2 * length, 128), F32)
        for h in range(heads):
            cut = slice(h * e, (h + 1) * e)
            denom = den_r[0, :, h : h + 1]
            pull = pulls[:, cut]
            dn = (pull / denom).astype(BF)
            dn_o[0, :, cut] = dn
            dd = -jnp.sum(pull * att_r[0, :, cut], -1, keepdims=True) / denom
            dds = jnp.where(lane == h, dd, dds)
            wide = dn.astype(F32)
            sums = mm_tn(jnp.concatenate([wide * lead, wide * tail], 1).astype(BF), fq_r[0, h])
            high = dd.astype(BF).astype(F32)
            low = dd - high
            four = jnp.concatenate([high * lead, low * lead, high * tail, low * tail], 1)
            zs = mm_tn(four.astype(BF), fq_r[0, h])
            put_edges(info_ref, keep, send, h, heads, sums, zs[0:1] + zs[1:2], zs[2:3] + zs[3:4])
        dd_o[0] = dds
        put_tags(keep, send, spare, first, last)

    outs = [
        shaped(rows, 2 * length, mine, dtype=BF),
        shaped(rows, 2 * length, 128),
        shaped(rows, 2, n, m),
        shaped(rows, 2, n, m),
    ]
    specs = [
        per_row(go), per_row(go_got),
        pl.BlockSpec((mine, width), lambda r, info: (info[0], 0)),
        per_row(att), per_row(den), per_row(fq), per_row(idc), per_row(idr),
    ]
    return row_call(
        kernel, "grads_one", info, [go, go_got, out_weight, att, den, fq, idc, idr], specs, outs,
        flops=rows * length * width * mine * 6,
    )


def pulled_back(grad_feat, feat, part, feats):
    e = feats.shape[0]
    weighted = grad_feat * feat.astype(F32)
    inner = (weighted * e ** (-0.25)).astype(BF)
    folded = jnp.sum(weighted, -1, keepdims=True) * e ** (-0.5)
    return (mm_nt(inner, feats) - part.astype(F32) * folded).astype(BF)


def grads_two_kernel(info, fq, fk, queries, values, dn, dd, features, own, got, idc, idr, deps=()):
    rows, heads, chip_len, m = fq.shape
    mine = queries.shape[2]
    e = mine // heads

    def kernel(
        info_ref, fq_r, fk_r, q_r, v_r, dn_r, dd_r, f_r, own_r, got_r, idc_r, idr_r, dq_o, dfk_o, dv_o
    ):
        same = idc_r[0] == idr_r[0]
        lead, tail, _, _ = edges(idc_r, idr_r)
        lead, tail = lead.astype(F32), tail.astype(F32)
        for h in range(heads):
            cut = slice(h * e, (h + 1) * e)
            feat_q, feat_k = fq_r[0, h], fk_r[0, h]
            part, value = dn_r[0, :, cut], v_r[0, :, cut]
            denom = dd_r[0, :, h : h + 1]
            scores = jnp.where(same, mm_nt(feat_q, feat_k), 0.0).astype(BF)
            pulls = jnp.where(same, mm_nt(part, value) + denom, 0.0).astype(BF)
            dv_o[0, :, cut] = mm_tn(scores, part)
            dfk_o[0, h] = mm_tn(pulls, feat_q)
            before, behind, zb, za = carry_of(info_ref, own_r, got_r, h, heads, e)
            wide = part.astype(F32)
            both = jnp.concatenate([wide * lead, wide * tail], 1).astype(BF)
            grad = (
                mm(pulls, feat_k)
                + mm(both, jnp.concatenate([before, behind], 0).astype(BF))
                + denom * (lead * zb + tail * za)
            )
            dq_o[0, :, cut] = pulled_back(grad, feat_q, q_r[0, :, cut], f_r[h])

    outs = [
        shaped(rows, chip_len, mine, dtype=BF),
        shaped(rows, heads, chip_len, m),
        shaped(rows, chip_len, mine),
    ]
    inputs = [fq, fk, queries, values, dn, dd, features, own, got, idc, idr]
    specs = [per_row(v) for v in inputs]
    specs[6] = head_features(features, heads)
    return row_call(
        kernel, "grads_two", info, inputs, specs, outs, deps, flops=rows * chip_len * chip_len * mine * 30
    )


def grads_three_kernel(info, fk, keys, values, dfk, dv, features, own, got, idc, idr, deps=()):
    rows, heads, chip_len, m = fk.shape
    mine = keys.shape[2]
    e = mine // heads

    def kernel(
        info_ref, fk_r, k_r, v_r, dfk_r, dv_r, f_r, own_r, got_r, idc_r, idr_r, dk_o, dv_o
    ):
        lead, tail, _, _ = edges(idc_r, idr_r)
        lead, tail = lead.astype(F32), tail.astype(F32)
        for h in range(heads):
            cut = slice(h * e, (h + 1) * e)
            feat = fk_r[0, h]
            before, behind, zb, za = carry_of(info_ref, own_r, got_r, h, heads, e)
            kv = jnp.concatenate([before, behind], 0).astype(BF)
            wide = v_r[0, :, cut].astype(F32)
            both = jnp.concatenate([wide * lead, wide * tail], 1).astype(BF)
            grad = dfk_r[0, h] + mm(both, kv) + (lead * zb + tail * za)
            dk_o[0, :, cut] = pulled_back(grad, feat, k_r[0, :, cut], f_r[h])
            more = mm_nt(feat, kv)
            total_v = dv_r[0, :, cut] + lead * more[:, :e] + tail * more[:, e:]
            dv_o[0, :, cut] = total_v.astype(BF)

    outs = [shaped(rows, chip_len, mine, dtype=BF), shaped(rows, chip_len, mine, dtype=BF)]
    inputs = [fk, keys, values, dfk, dv, features, own, got, idc, idr]
    specs = [per_row(v) for v in inputs]
    specs[5] = head_features(features, heads)
    return row_call(
        kernel, "grads_three", info, inputs, specs, outs, deps, flops=rows * chip_len * m * mine * 8
    )


def shares_kernel(info, dq, dk, dv, query_weight, key_weight, value_weight, deps=()):
    rows, chip_len, mine = dq.shape
    width = query_weight.shape[0]
    length = chip_len // 2

    def kernel(info_ref, dq_r, dk_r, dv_r, wq_r, wk_r, wv_r, here_o, send_o):
        total_x = (
            mm_nt(dq_r[0], wq_r[...]) + mm_nt(dk_r[0], wk_r[...]) + mm_nt(dv_r[0], wv_r[...])
        )
        here_o[0] = total_x[:length]
        send_o[0] = total_x[length:]

    outs = [shaped(rows, length, width), shaped(rows, length, width)]
    specs = [per_row(dq), per_row(dk), per_row(dv)] + [
        weight_columns(w, mine) for w in (query_weight, key_weight, value_weight)
    ]
    return row_call(
        kernel, "shares", info, [dq, dk, dv, query_weight, key_weight, value_weight], specs, outs, deps,
        flops=rows * chip_len * mine * width * 6,
    )


def norm(hidden):
    mean = jnp.mean(hidden, -1, keepdims=True)
    centered = hidden - mean
    variance = jnp.mean(centered * centered, -1, keepdims=True)
    inv_std = lax.rsqrt(variance + EPSILON)
    return centered * inv_std, inv_std


def norm_back(upstream, normed, inv_std, gain):
    scaled = upstream * gain
    return inv_std * (
        scaled
        - jnp.mean(scaled, -1, keepdims=True)
        - normed * jnp.mean(scaled * normed, -1, keepdims=True)
    )


def put_sums(ref, upstream, normed):
    ref[...] = jnp.zeros_like(ref)
    ref[0:1, :] = jnp.sum(upstream * normed, 0, keepdims=True)
    ref[1:2, :] = jnp.sum(upstream, 0, keepdims=True)


def ffn_chunk(j, info, chunks):
    return lax.rem(j + (1 - info[0]) * (chunks // 2), chunks)


def ffn_forward(info, x, att, att_got, out_weight, first, up, down, second, cot, chunks=2):
    count, width = x.shape
    mine = att.shape[1]
    ff = up.shape[1]
    size = ff // chunks
    half = chunks // 2

    def kernel(
        info_ref, x_r, att_r, attg_r, wo_r, wog_r, first_r, up_r, down_r, second_r, cot_r,
        y_o, ys_o, here_o, send_o, slope_o, out_o, dz_o, dzs_o, dh_o, unit_o, inv_o, sums_o, y_s, acc,
    ):
        j = pl.program_id(0)

        @pl.when(j == 0)
        def _():
            hidden = (
                x_r[...].astype(F32)
                + mm(att_r[...], wo_r[...])
                + mm(attg_r[...].astype(BF), wog_r[...])
            )
            normed, inv_std = norm(hidden)
            unit_o[...] = normed
            inv_o[...] = jnp.broadcast_to(inv_std, inv_o.shape)
            y = normed * first_r[0:1, :] + first_r[1:2, :]
            acc[...] = y
            y_s[...] = y.astype(BF)
            y_o[...] = y_s[...]
            ys_o[...] = y_s[...].astype(F32)

        inner = mm(y_s[...], up_r[...])
        bell = 0.5 * (1.0 + lax.erf(inner * 0.7071067811865476))
        slope_o[...] = bell + inner * (jnp.exp(-0.5 * inner * inner) * 0.3989422804014327)
        act = (inner * bell).astype(BF)

        @pl.when(j < half)
        def _():
            send_o[...] = act.astype(F32)

        @pl.when(j >= half)
        def _():
            here_o[...] = act

        acc[...] += mm(act, down_r[...])

        @pl.when(j == chunks - 1)
        def _():
            normed, inv_std = norm(acc[...])
            gain = second_r[0:1, :]
            out_o[...] = (normed * gain + second_r[1:2, :]).astype(BF)
            upstream = cot_r[...].astype(F32)
            put_sums(sums_o, upstream, normed)
            grad = norm_back(upstream, normed, inv_std, gain)
            dh_o[...] = grad
            dz_o[...] = grad.astype(BF)
            dzs_o[...] = grad.astype(BF).astype(F32)

    def whole(array):
        return pl.BlockSpec(array.shape, lambda j, info: (0, 0))

    flat = pl.BlockSpec((count, width), lambda j, info: (0, 0))
    outs = [
        (shaped(count, width, dtype=BF), flat),
        (shaped(count, width), flat),
        (shaped(count, ff // 2, dtype=BF), pl.BlockSpec((count, size), lambda j, info: (0, jnp.maximum(j - half, 0)))),
        (shaped(count, ff // 2), pl.BlockSpec((count, size), lambda j, info: (0, jnp.minimum(j, half - 1)))),
        (shaped(count, ff), pl.BlockSpec((count, size), lambda j, info: (0, j))),
        (shaped(count, width, dtype=BF), flat),
        (shaped(count, width, dtype=BF), flat),
        (shaped(count, width), flat),
        (shaped(count, width), flat),
        (shaped(count, width), flat),
        (shaped(count, 128), pl.BlockSpec((count, 128), lambda j, info: (0, 0))),
        (shaped(8, width), pl.BlockSpec((8, width), lambda j, info: (0, 0))),
    ]
    return pl.pallas_call(
        kernel,
        grid_spec=pltpu.PrefetchScalarGridSpec(
            num_scalar_prefetch=1,
            grid=(chunks,),
            in_specs=[
                whole(x), whole(att), whole(att_got),
                pl.BlockSpec((mine, width), lambda j, info: (info[0], 0)),
                pl.BlockSpec((mine, width), lambda j, info: (1 - info[0], 0)),
                whole(first),
                pl.BlockSpec((width, size), lambda j, info: (0, ffn_chunk(j, info, chunks))),
                pl.BlockSpec((size, width), lambda j, info: (ffn_chunk(j, info, chunks), 0)),
                whole(second), whole(cot),
            ],
            out_specs=[spec for _, spec in outs],
            scratch_shapes=[pltpu.VMEM((count, width), BF), pltpu.VMEM((count, width), F32)],
        ),
        out_shape=[shape for shape, _ in outs],
        compiler_params=pltpu.CompilerParams(vmem_limit_bytes=ROOM),
        cost_estimate=cost(15),
        name="ffn_forward",
    )(info, x, att, att_got, out_weight, out_weight, first, up, down, second, cot)


def ffn_inner(info, dz, down, slope, chunks=2):
    count, width = dz.shape
    ff = down.shape[0]
    size = ff // chunks
    half = chunks // 2

    def kernel(info_ref, dz_r, down_r, slope_r, here_o, send_o):
        j = pl.program_id(0)
        grad = (mm_nt(dz_r[...], down_r[...]) * slope_r[...]).astype(BF)

        @pl.when(j < half)
        def _():
            send_o[...] = grad.astype(F32)

        @pl.when(j >= half)
        def _():
            here_o[...] = grad

    return pl.pallas_call(
        kernel,
        grid_spec=pltpu.PrefetchScalarGridSpec(
            num_scalar_prefetch=1,
            grid=(chunks,),
            in_specs=[
                pl.BlockSpec((count, width), lambda j, info: (0, 0)),
                pl.BlockSpec((size, width), lambda j, info: (ffn_chunk(j, info, chunks), 0)),
                pl.BlockSpec((count, size), lambda j, info: (0, j)),
            ],
            out_specs=[
                pl.BlockSpec((count, size), lambda j, info: (0, jnp.maximum(j - half, 0))),
                pl.BlockSpec((count, size), lambda j, info: (0, jnp.minimum(j, half - 1))),
            ],
        ),
        out_shape=[shaped(count, ff // 2, dtype=BF), shaped(count, ff // 2)],
        compiler_params=pltpu.CompilerParams(vmem_limit_bytes=ROOM),
        cost_estimate=cost(8),
        name="ffn_inner",
    )(info, dz, down, slope)


def ffn_back(info, here, send, up, dh, unit, inv, first, deps=(), chunks=2):
    count, width = dh.shape
    ff = up.shape[1]
    size = ff // chunks
    half = chunks // 2

    def kernel(info_ref, here_r, send_r, up_r, dh_r, unit_r, inv_r, first_r, *rest):
        dh_o, go_o, gos_o, sums_o, acc = rest[len(deps) :]
        j = pl.program_id(0)

        @pl.when(j == 0)
        def _():
            acc[...] = dh_r[...]

        @pl.when(j < half)
        def _():
            acc[...] += mm_nt(send_r[...].astype(BF), up_r[...])

        @pl.when(j >= half)
        def _():
            acc[...] += mm_nt(here_r[...], up_r[...])

        @pl.when(j == chunks - 1)
        def _():
            upstream, normed = acc[...], unit_r[...]
            put_sums(sums_o, upstream, normed)
            grad = norm_back(upstream, normed, inv_r[:, 0:1], first_r[0:1, :])
            dh_o[...] = grad
            go_o[...] = grad.astype(BF)
            gos_o[...] = grad.astype(BF).astype(F32)

    def whole(array):
        return pl.BlockSpec(array.shape, lambda j, info: (0, 0))

    flat = pl.BlockSpec((count, width), lambda j, info: (0, 0))
    return pl.pallas_call(
        kernel,
        grid_spec=pltpu.PrefetchScalarGridSpec(
            num_scalar_prefetch=1,
            grid=(chunks,),
            in_specs=[
                pl.BlockSpec((count, size), lambda j, info: (0, jnp.maximum(j - half, 0))),
                pl.BlockSpec((count, size), lambda j, info: (0, jnp.minimum(j, half - 1))),
                pl.BlockSpec((width, size), lambda j, info: (0, ffn_chunk(j, info, chunks))),
                whole(dh), whole(unit), whole(inv), whole(first),
            ] + [ANY] * len(deps),
            out_specs=[flat, flat, flat, pl.BlockSpec((8, width), lambda j, info: (0, 0))],
            scratch_shapes=[pltpu.VMEM((count, width), F32)],
        ),
        out_shape=[
            shaped(count, width), shaped(count, width, dtype=BF), shaped(count, width), shaped(8, width)
        ],
        compiler_params=pltpu.CompilerParams(vmem_limit_bytes=ROOM),
        cost_estimate=cost(3),
        name="ffn_back",
    )(info, here, send, up, dh, unit, inv, first, *deps)


def tag_of(ref, k, spare):
    return ref[0, k, spare : spare + 1, 0:1]


def ordered(info_ref, mine, theirs):
    one = info_ref[1] == 1

    def chip(at, k):
        here = one if at else jnp.logical_not(one)
        return jnp.where(here, mine[0, k], theirs[0, k])

    return [[chip(at, k) for k in (0, 1)] for at in (0, 1)]


def join_plane(info, mine, theirs, spare, deps=()):
    rows, _, n, m = mine.shape

    def kernel(info_ref, mine_r, theirs_r, up_o, down_o):
        (lead0, tail0), (lead1, tail1) = ordered(info_ref, mine_r, theirs_r)

        def tag(part):
            return part[spare : spare + 1, 0:1]

        is_sum = lax.broadcasted_iota(jnp.int32, (n, m), 0) < spare
        up_o[0] = tail1 + jnp.where(is_sum & (tag(tail0) == tag(tail1)), tail0, 0.0)
        down_o[0] = lead0 + jnp.where(is_sum & (tag(lead1) == tag(lead0)), lead1, 0.0)

    outs = [shaped(rows, n, m), shaped(rows, n, m)]
    return row_call(kernel, "join_plane", info, [mine, theirs], [per_row(mine)] * 2, outs, deps)


def split_plane(info, mine, theirs, ups, downs, spare):
    rows, _, n, m = mine.shape
    steps = len(ups)

    def kernel(info_ref, mine_r, theirs_r, *refs):
        give_o, own_o = refs[2 * steps :]
        (lead0, tail0), (lead1, tail1) = ordered(info_ref, mine_r, theirs_r)

        def tag(part):
            return part[spare : spare + 1, 0:1]

        before = jnp.zeros((n, m), F32)
        behind = jnp.zeros((n, m), F32)
        for k in range(steps):
            up, down = refs[k][0], refs[steps + k][0]
            before = before + jnp.where(tag(up) == tag(lead0), up, 0.0)
            behind = behind + jnp.where(tag(down) == tag(tail1), down, 0.0)
        behind0 = jnp.where(tag(tail0) == tag(lead1), lead1, 0.0) + jnp.where(
            tag(tail0) == tag(tail1), behind, 0.0
        )
        before1 = jnp.where(tag(lead1) == tag(tail0), tail0, 0.0) + jnp.where(
            tag(lead1) == tag(lead0), before, 0.0
        )
        one = info_ref[1] == 1
        give_o[0, 0] = jnp.where(one, before, before1)
        give_o[0, 1] = jnp.where(one, behind0, behind)
        own_o[0, 0] = jnp.where(one, before1, before)
        own_o[0, 1] = jnp.where(one, behind, behind0)

    inputs = [mine, theirs, *ups, *downs]
    outs = [shaped(rows, 2, n, m), shaped(rows, 2, n, m)]
    return row_call(kernel, "split_plane", info, inputs, [per_row(v) for v in inputs], outs)


def exchange(net, info, keep, send, ids_row, chip_len, spare, late=()):
    if not net.fast:
        first, last = jnp.min(ids_row, 2), jnp.max(ids_row, 2)
        pay = jnp.stack([keep, send], 1)
        up, down = pay[:, :, 1], pay[:, :, 0]
        before = jnp.zeros_like(up)
        behind = jnp.zeros_like(up)
        for _ in range(min(net.n_seq // 2 - 1, -(-SEG_MOST // chip_len))):
            up, down = net.shift(up, 1), net.shift(down, -1)
            reached = up[:, 0, spare, 0:1] == first
            before = before + jnp.where(reached[:, :, None, None], up, 0.0)
            reached = down[:, 0, spare, 0:1] == last
            behind = behind + jnp.where(reached[:, :, None, None], down, 0.0)
        return jnp.stack([before[:, 0], behind[:, 0]], 1), jnp.stack([before[:, 1], behind[:, 1]], 1)
    theirs = net.over_x(send)
    up, down = join_plane(info, keep, theirs, spare, late[0] if late else ())
    ups, downs = [], []
    for _ in range(min(net.nz - 1, -(-SEG_MOST // (2 * chip_len)))):
        up, down = net.z_up(up), net.z_down(down)
        ups.append(up)
        downs.append(down)
    if late:
        late[1].extend([ups[0], downs[0]])
    give, own = split_plane(info, keep, theirs, ups, downs, spare)
    if late:
        late[2].append(own)
    return own, net.over_x(give)


def body(
    tokens,
    segment_ids,
    features,
    query_weight,
    key_weight,
    value_weight,
    out_weight,
    up_weight,
    down_weight,
    first_gain,
    first_bias,
    second_gain,
    second_bias,
    cotangent,
):
    net = Net(lax.axis_size("dp"), lax.axis_size("seq"))
    rows, length, width = tokens.shape
    heads_all, head_dim, _ = features.shape
    heads = heads_all // 2
    mine = width // 2
    ff = up_weight.shape[1]
    ff_half = ff // 2
    core = net.core
    fast = net.fast
    chip_len = 2 * length
    count = rows * length
    spare = heads // 2 * head_dim + heads // 2
    side = net.x if fast else jnp.zeros_like(core)
    info = jnp.stack([core, side]).astype(jnp.int32)

    tokens_got = net.over_core(tokens.astype(F32))
    ids = segment_ids.astype(F32)
    ids_chip = jnp.concatenate([ids, net.over_core(ids)], 1)
    idr, idc = ids_chip[:, None, :], ids_chip[:, :, None]

    keys, values, fk, keep, send = keys_kernel(
        info, tokens, tokens_got, key_weight, value_weight, features, idc, idr
    )
    queries, fq, num, den = queries_kernel(
        info, tokens, tokens_got, query_weight, features, fk, values, idc, idr
    )
    own, got = exchange(net, info, keep, send, idr, chip_len, spare)
    att, den, att_here, att_send = attend_kernel(info, fq, num, den, own, got, idc, idr)
    att_got = net.over_core(att_send).reshape(count, mine)

    flat = tokens.reshape(count, width)
    first = jnp.stack([first_gain, first_bias])
    second = jnp.stack([second_gain, second_bias])
    (
        y1, y1_send, act, act_send, slope, result, dz, dz_send, dh2, unit, inv, sums_two
    ) = ffn_forward(
        info, flat, att_here.reshape(count, mine), att_got, out_weight, first,
        up_weight, down_weight, second, cotangent.reshape(count, width),
    )
    y1_got = net.over_core(y1_send)
    act_got = net.over_core(act_send)
    dz_got = net.over_core(dz_send)
    df, df_send = ffn_inner(info, dz, down_weight, slope)
    df_got = net.over_core(df_send)

    one = jnp.where(net.seq < 0, 0.5, 1.0).astype(F32)

    def rounded(wide):
        return (wide * one).astype(BF)

    def both(a, b):
        return jnp.concatenate([a, rounded(b)], 0)

    deps = ()
    if fast:
        bits_mine, bits_other = stage_bits(net, 0), stage_bits(net, 0, 1 - core)
        down_parts = (act, act_got, dz, dz_got)
        up_parts = (y1, y1_got, df, df_got)
        f_sends = down_products(1 - bits_mine, *down_parts, deps=[df])
        f_sends = up_products(1 - bits_mine, *up_parts, f_sends, 6)
        deps = f_sends[1:]
    else:
        grad_up = total(net, mm_tn(both(y1, y1_got), both(df, df_got)), 1)
        grad_down = total(net, mm_tn(both(act, act_got), both(dz, dz_got)), 0)

    dh1, go, go_send, sums_one = ffn_back(
        info, df, df_send, up_weight, dh2, unit, inv, first, deps
    )
    go_got = net.over_core(go_send)
    dn, dd, keep_d, send_d = grads_one_kernel(
        info, go.reshape(rows, length, width), go_got.reshape(rows, length, width), out_weight,
        att, den, fq, idc, idr,
    )
    late = []
    if fast:
        f_gots = moves(net, f_sends, 0)
        f_keeps = down_products(bits_mine, *down_parts, deps=[go])
        f_keeps = up_products(bits_mine, *up_parts, f_keeps, 1)
        f_sends, f_keeps = add_stage(net, f_keeps, f_gots, 1, [send_d])
        late = [[f_sends[1]], [], []]
    own_d, got_d = exchange(net, info, keep_d, send_d, idr, chip_len, spare, late)
    dq, dfk, dv = grads_two_kernel(
        info, fq, fk, queries, values, dn, dd, features, own, got, idc, idr, deps=late[2] if fast else ()
    )
    if fast:
        f_gots = [
            stage_move(net, f_sends[0], 0, 1), stage_move(net, tie(f_sends[1], *late[1]), 1, 1)
        ]
        f_sends, f_keeps = add_stage(net, f_keeps, f_gots, 2, [dq])
        f_gots = moves(net, f_sends, 2)
    dk, dv = grads_three_kernel(
        info, fk, keys, values, dfk, dv, features, own_d, got_d, idc, idr, deps=f_sends[1:] if fast else ()
    )

    chip_flat = (rows * chip_len, mine)
    if fast:
        sums = jnp.concatenate([sums_one[:2], sums_two[:2]])
        small = (sums + net.over_core(sums)).reshape(8, mine)
        attn_parts = (
            flat, tokens_got.reshape(count, width),
            dq.reshape(chip_flat), dk.reshape(chip_flat), dv.reshape(chip_flat),
            att.reshape(chip_flat), go, go_got, small,
        )

        def over_core(parts):
            return [net.over_core(part) for part in parts]

        a_sends = attn_products(1 - bits_mine, *attn_parts)
        a_gots = moves(net, a_sends, 0)
        a_keeps = attn_products(bits_mine, *attn_parts, deps=a_sends[1:])
        f_sends, f_keeps = add_stage(net, f_keeps, f_gots, 3, a_keeps[1:])
        f_gots = moves(net, f_sends, 3)
        f_own = last_add(f_keeps, f_gots)
        f_gots = moves(net, f_own, 3)
        a_sends, a_keeps = add_stage(net, a_keeps, a_gots, 1, f_own[1:])
        a_gots = moves(net, a_sends, 1)
        f_own = join_stage(net, f_own, f_gots, 3, a_sends[1:])
        f_gots = moves(net, f_own, 2)
        a_sends, a_keeps = add_stage(net, a_keeps, a_gots, 2, f_own[1:])
        a_gots = moves(net, a_sends, 2)
        f_one = join_stage(net, f_own, f_gots, 2, a_sends[1:])
        f_two = moves(net, f_one, 1)
        f_one_core = over_core(f_one)
        a_sends, a_keeps = add_stage(net, a_keeps, a_gots, 3, f_one[1:])
        a_gots = moves(net, a_sends, 3)
        a_own = last_add(a_keeps, a_gots)
        a_gots = moves(net, a_own, 3)
        shapes = [shaped(*w.shape) for w in (up_weight, down_weight)]
        copies = ffn_copies(width, ff_half)
        outs, done = place_pieces(
            net, [(f_one, 0, 0, 0), (f_one_core, 1, 0, 0)], shapes, copies, a_own[1:]
        )
        f_three = moves(net, [tie(part, a_own[1]) for part in f_one], 0)
        a_own = join_stage(net, a_own, a_gots, 3, done)
        a_gots = moves(net, a_own, 2)
        f_two_core = over_core(f_two)
        outs, done = place_pieces(
            net, [(f_two, 0, 0, 1), (f_two_core, 1, 0, 1)], outs, copies, a_own[1:]
        )
        f_four = moves(net, f_two, 0)
        a_one = join_stage(net, a_own, a_gots, 2, done)
        a_two = moves(net, a_one, 1)
        a_three = moves(net, a_one, 0)
        f_three_core = over_core(f_three)
        outs, done = place_pieces(
            net, [(f_three, 0, 1, 0), (f_three_core, 1, 1, 0)], outs, copies, a_one[1:]
        )
        here, share_send = shares_kernel(
            info, dq, dk, dv, query_weight, key_weight, value_weight, deps=done
        )
        a_four = moves(net, a_two, 0)
        f_four_core = over_core(f_four)
        a_one_core = over_core(a_one)
        (grad_up, grad_down), done = place_pieces(
            net, [(f_four, 0, 1, 1), (f_four_core, 1, 1, 1)], outs, copies, [share_send]
        )
        shapes = [shaped(width, width)] * 4
        copies = attn_copies(mine)
        a_two_core = over_core(a_two)
        outs, done = place_pieces(
            net,
            [(a_one, 0, 0, 0), (a_one_core, 1, 0, 0), (a_two, 0, 0, 1), (a_two_core, 1, 0, 1)],
            shapes, copies, done,
        )
        a_three_core = over_core(a_three)
        a_four = [tie(part, *done) for part in a_four]
        outs, done = place_pieces(
            net, [(a_three, 0, 1, 0), (a_three_core, 1, 1, 0), (a_four, 0, 1, 1)], outs, copies
        )
        (grad_query, grad_key, grad_value, grad_out), _ = place_pieces(
            net, [(over_core(a_four), 1, 1, 1)], outs, copies
        )
        rest_rows = mine // 3
        at = rest_rows - (rest_rows + SPARE_ROWS) // 2
        one, two = a_one[1][at : at + 8], a_two[1][at : at + 8]
        small = jnp.where(stage_bit(net, 1, 1, core) == 1, one, two).reshape(4, width)
    else:
        x_chip = jnp.concatenate([tokens, rounded(tokens_got)], 1).reshape(rows * chip_len, width)
        go_chip = jnp.concatenate(
            [go.reshape(rows, length, width), rounded(go_got).reshape(rows, length, width)], 1
        ).reshape(rows * chip_len, width)
        grad_query = total(net, mm_tn(x_chip, dq.reshape(chip_flat)), 1)
        grad_key = total(net, mm_tn(x_chip, dk.reshape(chip_flat)), 1)
        grad_value = total(net, mm_tn(x_chip, dv.reshape(chip_flat)), 1)
        grad_out = total(net, mm_tn(att.astype(BF).reshape(chip_flat), go_chip), 0)

        here, share_send = shares_kernel(info, dq, dk, dv, query_weight, key_weight, value_weight)
        small = lax.psum(jnp.concatenate([sums_one[:2], sums_two[:2]]), AXES)

    grad_input = dh1.reshape(rows, length, width) + here + net.over_core(share_send)
    return (
        result.reshape(rows, length, width),
        grad_input.astype(BF),
        grad_query,
        grad_key,
        grad_value,
        grad_out,
        grad_up,
        grad_down,
        small[0],
        small[1],
        small[2],
        small[3],
    )


def solution(mesh):
    split = P("dp", "seq", None)
    placed = (split, P("dp", "seq")) + (P(),) * 11 + (split,)
    return jax.shard_map(
        body,
        mesh=mesh,
        in_specs=placed,
        out_specs=(split, split) + (P(),) * 10,
        check_vma=False,
    )
```

```python
import jax
import jax.numpy as jnp
from jax import lax
from jax.experimental import pallas as pl
from jax.experimental.pallas import tpu as pltpu
from jax.sharding import PartitionSpec as P

SEG_MOST = 2048
SPARE_ROWS = 128
EPSILON = 1e-06
AXES = ("dp", "seq")
BF = jnp.bfloat16
F32 = jnp.float32
ANY = pl.BlockSpec(memory_space=pl.ANY)
HBM = pl.BlockSpec(memory_space=pltpu.HBM)
ROOM = 20 << 20
SMALL = 14 << 20


COSTS = {
    "tie": 0.1, "add_stage": 12, "last_add": 4.5, "join_stage": 9, "down_products": 12, "up_products 1": 6,
    "up_products 2": 1, "attn_products": 12, "place_pieces": 13.5, "ffn_forward": 15, "ffn_inner": 8,
    "ffn_back": 3, "keys": 10, "queries": 8, "attend": 6, "grads_one": 3, "grads_two": 12, "grads_three": 8,
    "shares": 9, "join_plane": 3, "split_plane": 3,
}
CALLS = {}


def cost(name):
    CALLS[name] = CALLS.get(name, 0) + 1
    us = COSTS.get(f"{name} {CALLS[name]}", COSTS.get(name))
    return pl.CostEstimate(flops=int(us * 1e9), bytes_accessed=1, transcendentals=0)


def shaped(*shape, dtype=F32):
    return jax.ShapeDtypeStruct(shape, dtype)


def mm(a, b):
    return jnp.dot(a, b, preferred_element_type=F32)


def mm_nt(a, b):
    return lax.dot_general(a, b, (((1,), (1,)), ((), ())), preferred_element_type=F32)


def mm_tn(a, b):
    return lax.dot_general(a, b, (((0,), (0,)), ((), ())), preferred_element_type=F32)


def dslice(a, start, size, axis=0):
    return lax.dynamic_slice_in_dim(a, start, size, axis)


class Net:
    def __init__(self, n_dp, n_seq):
        self.n_dp, self.n_seq = n_dp, n_seq
        self.nz = 4
        self.nx = n_seq // 8
        self.fast = n_dp == 2 and n_seq == 16
        seq = lax.axis_index("seq")
        self.y = lax.axis_index("dp")
        self.core = seq % 2
        self.x = (seq // 2) % self.nx
        self.z = seq // (2 * self.nx)
        self.seq = seq

    def perm(self, move):
        pairs = []
        for y in range(self.n_dp):
            for s in range(self.n_seq):
                target = move(y, s // (2 * self.nx), (s // 2) % self.nx, s % 2)
                if target is not None:
                    ty, tz, tx, tc = target
                    pairs.append((y * self.n_seq + s, ty * self.n_seq + (tz * self.nx + tx) * 2 + tc))
        return pairs

    def send(self, value, move):
        return lax.ppermute(value, AXES, self.perm(move))

    def over_core(self, value):
        return self.send(value, lambda y, z, x, c: (y, z, x, 1 - c))

    def over_x(self, value):
        return self.send(value, lambda y, z, x, c: (y, z, 1 - x, c))

    def z_up(self, value):
        return self.send(value, lambda y, z, x, c: (y, z + 1, x, c) if z < 3 else None)

    def z_down(self, value):
        return self.send(value, lambda y, z, x, c: (y, z - 1, x, c) if z > 0 else None)

    def shift(self, value, step):
        chips = self.n_seq // 2
        pairs = []
        for y in range(self.n_dp):
            for s in range(self.n_seq):
                if 0 <= s // 2 + step < chips:
                    pairs.append((y * self.n_seq + s, y * self.n_seq + s + 2 * step))
        return lax.ppermute(value, AXES, pairs)


ORDERS = ((("x", "y", "1", "2"), ("y", "x", "2", "1")), (("1", "2", "x", "y"), ("2", "1", "x", "y")))


def stage_move(net, value, stream, stage):
    def move(y, z, x, c):
        axis = ORDERS[stream][c][stage]
        return {
            "x": (y, z, 1 - x, c),
            "y": (1 - y, z, x, c),
            "1": (y, z ^ 1, x, c),
            "2": (y, z ^ 2, x, c),
        }[axis]

    return net.send(value, move)


def stage_bit(net, stream, stage, core):
    place = {"x": net.x, "y": net.y, "1": net.z % 2, "2": net.z // 2}
    zero, one = (place[ORDERS[stream][c][stage]] for c in (0, 1))
    return jnp.where(core == 0, zero, one)


def tie(value, *deps):
    def kernel(*refs):
        pass

    anywhere = pl.BlockSpec(memory_space=pl.ANY)
    return pl.pallas_call(
        kernel,
        in_specs=[anywhere] * (1 + len(deps)),
        out_specs=anywhere,
        out_shape=jax.ShapeDtypeStruct(value.shape, value.dtype),
        input_output_aliases={0: 0},
        compiler_params=pltpu.CompilerParams(vmem_limit_bytes=SMALL),
        cost_estimate=cost("tie"),
        name="tie",
    )(value, *deps)


def moves(net, parts, stage):
    return [stage_move(net, part, i, stage) for i, part in enumerate(parts)]


def stage_bits(net, stage, count=2):
    return jnp.stack([stage_bit(net, i, stage, net.core) for i in range(count)]).astype(jnp.int32)


def add_stage(net, keeps, gots, stage, deps=()):
    rows, count = keeps[0].shape[0], len(keeps)
    steps = 4 if rows >= 1152 else 2 if rows >= 512 else 1

    def kernel(bits_ref, *refs):
        outs = refs[4 * count + len(deps) :]
        for i in range(2 * count):
            outs[i][...] = refs[2 * i][...] + refs[2 * i + 1][...]

    in_specs, inputs, out_specs, shapes = [], [], [], []
    for side in (0, 1):
        for i, (keep, got) in enumerate(zip(keeps, gots)):
            half, width = keep.shape[0] // 2, keep.shape[1]
            block = (half // steps, width)
            spec = pl.BlockSpec(
                block,
                lambda r, bits, i=i, side=side: (
                    (bits[i] if side else 1 - bits[i]) * steps + r,
                    0,
                ),
            )
            in_specs += [spec, spec]
            inputs += [keep, got]
            out_specs.append(pl.BlockSpec(block, lambda r, bits: (r, 0)))
            shapes.append(shaped(half, width))
    in_specs += [ANY] * len(deps)
    outs = pl.pallas_call(
        kernel,
        grid_spec=pltpu.PrefetchScalarGridSpec(
            num_scalar_prefetch=1, grid=(steps,), in_specs=in_specs, out_specs=out_specs
        ),
        out_shape=shapes,
        compiler_params=pltpu.CompilerParams(vmem_limit_bytes=SMALL),
        cost_estimate=cost("add_stage"),
        name="add_stage",
    )(stage_bits(net, stage, count), *inputs, *deps)
    return outs[:count], outs[count:]


def last_add(keeps, gots, deps=()):
    count = len(keeps)

    def kernel(*refs):
        outs = refs[2 * count + len(deps) :]
        for i in range(count):
            outs[i][...] = refs[i][...] + refs[count + i][...]

    whole = pl.BlockSpec(memory_space=pltpu.VMEM)
    return pl.pallas_call(
        kernel,
        in_specs=[whole] * (2 * count) + [ANY] * len(deps),
        out_specs=[whole] * count,
        out_shape=[shaped(*k.shape) for k in keeps],
        compiler_params=pltpu.CompilerParams(vmem_limit_bytes=SMALL),
        cost_estimate=cost("last_add"),
        name="last_add",
    )(*keeps, *gots, *deps)


def join_stage(net, parts, gots, stage, deps=()):
    steps = max(1, parts[0].shape[0] // 144)
    count = len(parts)

    def kernel(bits_ref, *refs):
        outs = refs[2 * count + len(deps) :]
        for i in range(count):
            bit = bits_ref[i]
            outs[i][pl.ds(bit, 1)] = refs[2 * i][...][None]
            outs[i][pl.ds(1 - bit, 1)] = refs[2 * i + 1][...][None]

    in_specs, out_specs, shapes = [], [], []
    for part in parts:
        n, width = part.shape
        rows = n // steps
        in_specs += [pl.BlockSpec((rows, width), lambda r, bits: (r, 0))] * 2
        out_specs.append(pl.BlockSpec((2, rows, width), lambda r, bits: (0, r, 0)))
        shapes.append(shaped(2, n, width))
    outs = pl.pallas_call(
        kernel,
        grid_spec=pltpu.PrefetchScalarGridSpec(
            num_scalar_prefetch=1,
            grid=(steps,),
            in_specs=in_specs + [ANY] * len(deps),
            out_specs=out_specs,
        ),
        out_shape=shapes,
        compiler_params=pltpu.CompilerParams(vmem_limit_bytes=SMALL),
        cost_estimate=cost("join_stage"),
        name="join_stage",
    )(stage_bits(net, stage, count), *[v for pair in zip(parts, gots) for v in pair], *deps)
    return [out.reshape(2 * out.shape[1], out.shape[2]) for out in outs]


def tn(a, a_other, b, b_other):
    return mm_tn(a, b) + mm_tn(a_other.astype(BF), b_other.astype(BF))


def picked_columns(count, size, index):
    return pl.BlockSpec((count, size), lambda g, bits: (0, index(bits)))


def whole_of(array):
    return pl.BlockSpec(array.shape, lambda g, bits: (0,) * array.ndim)


def down_products(bits, act, act_other, gz, gz_other, deps=()):
    count, width = gz.shape
    unit = act.shape[1] // 12
    sizes = (5 * unit, unit)

    def kernel(bits_ref, a0, a0o, a1, a1o, gz_r, gzo_r, *rest):
        outs, scratch, sems = rest[len(deps) : -2], rest[-2], rest[-1]
        scratch[: sizes[0], :] = tn(a0[...], a0o[...], gz_r[...], gzo_r[...])
        scratch[sizes[0] :, :] = tn(a1[...], a1o[...], gz_r[...], gzo_r[...])
        copies = [
            pltpu.make_async_copy(
                scratch.at[: sizes[0]], outs[0].at[outs[0].shape[0] - sizes[0] :], sems.at[0]
            ),
            pltpu.make_async_copy(
                scratch.at[sizes[0] :], outs[1].at[outs[1].shape[0] - sizes[1] :], sems.at[1]
            ),
        ]
        for copy in copies:
            copy.start()
        for copy in copies:
            copy.wait()

    first = picked_columns(count, sizes[0], lambda bits: bits[0])
    second = picked_columns(count, sizes[1], lambda bits: 10 + bits[1])
    up_rows = act.shape[1] // width * (width // 6)
    return pl.pallas_call(
        kernel,
        grid_spec=pltpu.PrefetchScalarGridSpec(
            num_scalar_prefetch=1,
            grid=(1,),
            in_specs=[first, first, second, second, whole_of(gz), whole_of(gz_other)]
            + [ANY] * len(deps),
            out_specs=[ANY, ANY],
            scratch_shapes=[
                pltpu.VMEM((6 * unit, width), F32),
                pltpu.SemaphoreType.DMA((2,)),
            ],
        ),
        out_shape=[shaped(2 * up_rows + sizes[0], width), shaped(up_rows + sizes[1], width)],
        compiler_params=pltpu.CompilerParams(vmem_limit_bytes=ROOM),
        cost_estimate=cost("down_products"),
        name="down_products",
    )(bits, act, act_other, act, act_other, gz, gz_other, *deps)


def up_products(bits, y1, y1_other, gi, gi_other, outs):
    count, width = y1.shape
    u = width // 6
    parts = gi.shape[1] // width

    def kernel(bits_ref, y1_r, y1o_r, gi_r, gio_r, *rest):
        outs = rest[2:]

        def fill(out):
            y, yo = y1_r[...], y1o_r[...]
            for part in range(parts):
                cut = slice(part * width, (part + 1) * width)
                out[part * u : (part + 1) * u, :] = tn(y, yo, gi_r[:, cut], gio_r[:, cut])

        pl.when(pl.program_id(0) < 2)(lambda: fill(outs[0]))
        pl.when(pl.program_id(0) == 2)(lambda: fill(outs[1]))

    picked = pl.BlockSpec(
        (count, u), lambda i, bits: (0, jnp.where(i < 2, 2 * bits[0] + i, 4 + bits[1]))
    )
    return pl.pallas_call(
        kernel,
        grid_spec=pltpu.PrefetchScalarGridSpec(
            num_scalar_prefetch=1,
            grid=(3,),
            in_specs=[picked, picked, whole_of(gi), whole_of(gi_other), ANY, ANY],
            out_specs=[
                pl.BlockSpec((parts * u, width), lambda i, bits: (jnp.minimum(i, 1), 0)),
                pl.BlockSpec((parts * u, width), lambda i, bits: (0, 0)),
            ],
        ),
        out_shape=[shaped(*o.shape) for o in outs],
        input_output_aliases={5: 0, 6: 1},
        compiler_params=pltpu.CompilerParams(vmem_limit_bytes=ROOM),
        cost_estimate=cost("up_products"),
        name="up_products",
    )(bits, y1, y1_other, gi, gi_other, *outs)


def attn_products(bits, x, x_other, dq, dk, dv, attn, go, go_other, small, deps=()):
    count, width = x.shape
    mine = attn.shape[1]

    def kernel(bits_ref, x_r, xo_r, dq_r, dk_r, dv_r, attn_r, go_r, goo_r, small_r, *rest):
        (out,) = rest[len(deps) :]
        x, xo = x_r[...], xo_r[...].astype(BF)
        for k, grad in enumerate((dq_r, dk_r, dv_r)):
            out[k * mine : (k + 1) * mine, :] = tn(x, xo, grad[:count], grad[count:])
        part = attn_r[...].astype(BF)
        out[3 * mine : 4 * mine, :] = tn(part[:count], part[count:], go_r[...], goo_r[...])
        out[4 * mine :, :] = jnp.zeros((SPARE_ROWS, mine), F32)
        out[4 * mine : 4 * mine + 8, :] = small_r[...]

    half = picked_columns(count, mine, lambda bits: bits[0])
    rows = 4 * mine + SPARE_ROWS
    out = pl.pallas_call(
        kernel,
        grid_spec=pltpu.PrefetchScalarGridSpec(
            num_scalar_prefetch=1,
            grid=(1,),
            in_specs=[half, half]
            + [whole_of(v) for v in (dq, dk, dv, attn)]
            + [half, half, whole_of(small)]
            + [ANY] * len(deps),
            out_specs=pl.BlockSpec((rows, mine), lambda g, bits: (0, 0)),
        ),
        out_shape=shaped(rows, mine),
        compiler_params=pltpu.CompilerParams(vmem_limit_bytes=ROOM),
        cost_estimate=cost("attn_products"),
        name="attn_products",
    )(bits, x, x_other, dq, dk, dv, attn, go, go_other, small, *deps)
    return [out]


def place_pieces(net, pieces, outs, copies, deps=()):
    fresh = isinstance(outs[0], jax.ShapeDtypeStruct)
    n_out, m = len(outs), len(pieces[0][0])
    inputs = [part for piece in pieces for part in piece[0]]
    n = len(inputs)
    scalars = []
    for _, other_core, other_first, other_second in pieces:
        core = 1 - net.core if other_core else net.core
        scalars.append(core)
        for i in range(m):
            for stage, flip in ((0, other_first), (1, other_second)):
                bit = stage_bit(net, i, stage, core)
                scalars.append(1 - bit if flip else bit)
    where = jnp.stack(scalars).astype(jnp.int32)

    def kernel(where_ref, *refs):
        srcs = refs[: n]
        dests = refs[-(n + 3 + n_out) : -(n + 3)]
        refs[-(n + 3)][...] = jnp.zeros((8, 128), F32)
        held, (arrive, sems) = refs[-(n + 2) : -2], refs[-2:]
        loads = [pltpu.make_async_copy(srcs[j], held[j], arrive.at[j]) for j in range(n)]
        for load in loads:
            load.start()

        def each(j, act):
            piece, i = j // m, j % m
            core = where_ref[(1 + 2 * m) * piece]
            at = (1 + 2 * m) * piece + 1 + 2 * i
            first, second = where_ref[at], where_ref[at + 1]
            for quarter in (0, 1):

                @pl.when(second == quarter)
                def _():
                    for k, (src, dest) in enumerate(copies(i, quarter, core, first, held[j], dests)):
                        act(pltpu.make_async_copy(src, dest, sems.at[j, k]))

        for j in range(n):
            loads[j].wait()
            each(j, lambda copy: copy.start())
        for j in range(n):
            each(j, lambda copy: copy.wait())

    operands = inputs + ([] if fresh else list(outs)) + list(deps)
    *outs, done = pl.pallas_call(
        kernel,
        grid_spec=pltpu.PrefetchScalarGridSpec(
            num_scalar_prefetch=1,
            grid=(1,),
            in_specs=[ANY] * len(inputs) + [HBM] * (0 if fresh else n_out) + [ANY] * len(deps),
            out_specs=[HBM] * n_out + [pl.BlockSpec((8, 128), lambda g, where: (0, 0))],
            scratch_shapes=[pltpu.VMEM(part.shape, F32) for part in inputs] + [
                pltpu.SemaphoreType.DMA((n,)),
                pltpu.SemaphoreType.DMA((n, 6)),
            ],
        ),
        out_shape=[shaped(*o.shape) for o in outs] + [shaped(8, 128)],
        input_output_aliases={} if fresh else {1 + n + i: i for i in range(n_out)},
        compiler_params=pltpu.CompilerParams(vmem_limit_bytes=ROOM),
        cost_estimate=cost("place_pieces"),
        name="place_pieces",
    )(where, *operands)
    return outs, [done]


def rows_at(ref, start, size, step, lanes=None):
    start = pl.multiple_of(start, step)
    return ref.at[pl.ds(start, size)] if lanes is None else ref.at[pl.ds(start, size), lanes]


def spans(sizes, at, length):
    start = 0
    for k, size in enumerate(sizes):
        low, high = max(start, at), min(start + size, at + length)
        if low < high:
            yield k, low - start, low - at, high - low
        start += size


def ffn_copies(width, ff_half):
    u, unit = width // 6, ff_half // 12
    parts = ff_half // width

    def copies(i, quarter, c, b, src, dests):
        up, down = dests
        blocks = 1 if i else 2
        sizes = [u] * (parts * blocks) + [unit if i else 5 * unit]
        length = src.shape[0]
        for k, row, at, n in spans(sizes, quarter * length, length):
            if k < parts * blocks:
                block = 4 + b if i else 2 * b + k // parts
                lanes = pl.ds(pl.multiple_of(c * ff_half + k % parts * width, 128), width)
                dest = rows_at(up, block * u + row, n, 8, lanes)
            else:
                start = 10 * unit + b * unit if i else 5 * unit * b
                dest = rows_at(down, c * ff_half + start + row, n, 8)
            yield src.at[at : at + n], dest

    return copies


def attn_copies(mine):
    def copies(i, quarter, c, b, src, dests):
        own = pl.ds(pl.multiple_of(c * mine, 128), mine)
        half = pl.ds(pl.multiple_of(b * mine, 128), mine)
        length = src.shape[0]
        for k, row, at, n in spans([mine] * 4, quarter * length, length):
            if k < 3:
                dest = rows_at(dests[k], b * mine + row, n, 8, own)
            else:
                dest = rows_at(dests[3], c * mine + row, n, 8, half)
            yield src.at[at : at + n], dest

    return copies


def total(net, half, axis):
    size = half.shape[axis]
    shape = tuple(2 * n if i == axis else n for i, n in enumerate(half.shape))
    own = lax.dynamic_update_slice_in_dim(jnp.zeros(shape, F32), half, net.core * size, axis)
    return lax.psum(own, AXES)


def per_row(array):
    rest = array.shape[1:]
    return pl.BlockSpec((1, *rest), lambda r, info: (r, *(0 for _ in rest)))


def row_call(kernel, name, info, inputs, in_specs, outs, deps=(), flops=0):
    n_in = len(inputs)
    rows = outs[0].shape[0]

    def run(info_ref, *refs):
        kernel(info_ref, *refs[:n_in], *refs[n_in + len(deps) :])

    size = sum(v.size * v.dtype.itemsize for v in [*inputs, *outs])
    return pl.pallas_call(
        run,
        grid_spec=pltpu.PrefetchScalarGridSpec(
            num_scalar_prefetch=1,
            grid=(rows,),
            in_specs=list(in_specs) + [ANY] * len(deps),
            out_specs=[per_row(o) for o in outs],
        ),
        out_shape=outs,
        compiler_params=pltpu.CompilerParams(vmem_limit_bytes=ROOM),
        cost_estimate=cost(name),
        name=name,
    )(info, *inputs, *deps)


def edges(idc_ref, idr_ref):
    row = idr_ref[0]
    first = jnp.min(row, axis=1, keepdims=True)
    last = jnp.max(row, axis=1, keepdims=True)
    return idc_ref[0] == first, idc_ref[0] == last, first, last


def phi(part, feats):
    head_dim, feat_count = feats.shape
    wide = part.astype(F32)
    square = jnp.sum(wide * wide, -1, keepdims=True)
    inner = mm(part, feats) * head_dim ** (-0.25) - square * (0.5 * head_dim ** (-0.5))
    return (jnp.exp(inner) * feat_count ** (-0.5)).astype(BF)


def put_edges(info_ref, keep, send, h, heads, sums, lead_z, tail_z):
    half = heads // 2
    group, at = h // half, h % half
    e = sums.shape[0] // 2

    def put(ref):
        ref[0, 0, at * e : (at + 1) * e, :] = sums[:e]
        ref[0, 1, at * e : (at + 1) * e, :] = sums[e:]
        ref[0, 0, half * e + at : half * e + at + 1, :] = lead_z
        ref[0, 1, half * e + at : half * e + at + 1, :] = tail_z

    @pl.when(info_ref[1] == group)
    def _():
        put(keep)

    @pl.when(info_ref[1] != group)
    def _():
        put(send)


def put_tags(keep, send, spare, first, last):
    n, m = keep.shape[2:]
    for ref in (keep, send):
        ref[0, 0, spare:, :] = jnp.broadcast_to(first, (n - spare, m))
        ref[0, 1, spare:, :] = jnp.broadcast_to(last, (n - spare, m))


def weight_columns(weight, mine):
    return pl.BlockSpec((weight.shape[0], mine), lambda r, info: (0, info[0]))


def head_features(features, heads):
    return pl.BlockSpec((heads, *features.shape[1:]), lambda r, info: (info[0], 0, 0))


def keys_kernel(info, x, x_got, key_weight, value_weight, features, idc, idr):
    rows, length, width = x.shape
    mine, heads = width // 2, features.shape[0] // 2
    e, m = features.shape[1:]
    n = heads // 2 * e + 8
    spare = heads // 2 * e + heads // 2

    def kernel(info_ref, x_r, xg_r, wk_r, wv_r, f_r, idc_r, idr_r, k_o, v_o, fk_o, keep, send):
        chip = jnp.concatenate([x_r[0], xg_r[0].astype(BF)], 0)
        keys = mm(chip, wk_r[...]).astype(BF)
        values = mm(chip, wv_r[...]).astype(BF)
        k_o[0] = keys
        v_o[0] = values
        lead, tail, first, last = edges(idc_r, idr_r)
        masks = jnp.concatenate([lead.astype(F32), tail.astype(F32)], 1).astype(BF)
        lead_b, tail_b = masks[:, 0:1], masks[:, 1:2]
        for h in range(heads):
            cut = slice(h * e, (h + 1) * e)
            feat = phi(keys[:, cut], f_r[h])
            fk_o[0, h] = feat
            part = values[:, cut]
            sums = mm_tn(jnp.concatenate([part * lead_b, part * tail_b], 1), feat)
            zs = mm_tn(masks, feat)
            put_edges(info_ref, keep, send, h, heads, sums, zs[0:1], zs[1:2])
        put_tags(keep, send, spare, first, last)

    outs = [
        shaped(rows, 2 * length, mine, dtype=BF),
        shaped(rows, 2 * length, mine, dtype=BF),
        shaped(rows, heads, 2 * length, m, dtype=BF),
        shaped(rows, 2, n, m),
        shaped(rows, 2, n, m),
    ]
    specs = [
        per_row(x), per_row(x_got),
        weight_columns(key_weight, mine), weight_columns(value_weight, mine),
        head_features(features, heads), per_row(idc), per_row(idr),
    ]
    return row_call(
        kernel, "keys", info, [x, x_got, key_weight, value_weight, features, idc, idr], specs, outs,
        flops=rows * length * width * mine * 10,
    )


def queries_kernel(info, x, x_got, query_weight, features, fk, values, idc, idr, deps=()):
    rows, length, width = x.shape
    mine, heads = width // 2, features.shape[0] // 2
    e, m = features.shape[1:]

    def kernel(info_ref, x_r, xg_r, wq_r, f_r, fk_r, v_r, idc_r, idr_r, q_o, fq_o, num_o, den_o):
        chip = jnp.concatenate([x_r[0], xg_r[0].astype(BF)], 0)
        queries = mm(chip, wq_r[...]).astype(BF)
        q_o[0] = queries
        same = idc_r[0] == idr_r[0]
        lane = lax.broadcasted_iota(jnp.int32, (2 * length, 128), 1)
        dens = jnp.ones((2 * length, 128), F32)
        for h in range(heads):
            cut = slice(h * e, (h + 1) * e)
            feat = phi(queries[:, cut], f_r[h])
            fq_o[0, h] = feat
            scores = jnp.where(same, mm_nt(feat, fk_r[0, h]), 0.0)
            num_o[0, :, cut] = mm(scores.astype(BF), v_r[0, :, cut])
            dens = jnp.where(lane == h, jnp.sum(scores, -1, keepdims=True), dens)
        den_o[0] = dens

    outs = [
        shaped(rows, 2 * length, mine, dtype=BF),
        shaped(rows, heads, 2 * length, m, dtype=BF),
        shaped(rows, 2 * length, mine),
        shaped(rows, 2 * length, 128),
    ]
    specs = [
        per_row(x), per_row(x_got), weight_columns(query_weight, mine),
        head_features(features, heads), per_row(fk), per_row(values), per_row(idc), per_row(idr),
    ]
    return row_call(
        kernel, "queries", info,
        [x, x_got, query_weight, features, fk, values, idc, idr], specs, outs, deps,
        flops=rows * length * width * mine * 12,
    )


def carry_of(info_ref, own_r, got_r, h, heads, e):
    half = heads // 2
    group, at = h // half, h % half
    flag = info_ref[1] == group

    def picked(k, rows):
        return jnp.where(flag, own_r[0, k, rows, :], got_r[0, k, rows, :])

    kv = slice(at * e, (at + 1) * e)
    z = slice(half * e + at, half * e + at + 1)
    return picked(0, kv), picked(1, kv), picked(0, z), picked(1, z)


def attend_kernel(info, fq, num, den, own, got, idc, idr):
    rows, heads, chip_len, m = fq.shape
    mine = num.shape[2]
    e = mine // heads
    length = chip_len // 2

    def kernel(info_ref, fq_r, num_r, den_r, own_r, got_r, idc_r, idr_r, att_o, den_o, here_o, send_o):
        lead, tail, _, _ = edges(idc_r, idr_r)
        lead, tail = lead.astype(F32), tail.astype(F32)
        lane = lax.broadcasted_iota(jnp.int32, (chip_len, 128), 1)
        dens = den_r[0]
        for h in range(heads):
            cut = slice(h * e, (h + 1) * e)
            before, behind, zb, za = carry_of(info_ref, own_r, got_r, h, heads, e)
            feat = fq_r[0, h]
            more = mm_nt(feat, jnp.concatenate([before, behind], 0).astype(BF))
            numer = num_r[0, :, cut] + lead * more[:, :e] + tail * more[:, e:]
            extra = jnp.sum(feat.astype(F32) * (lead * zb + tail * za), -1, keepdims=True)
            denom = den_r[0, :, h : h + 1] + extra
            dens = jnp.where(lane == h, denom, dens)
            att = numer / denom
            att_o[0, :, cut] = att
            rounded = att.astype(BF)
            here_o[0, :, cut] = rounded[:length]
            send_o[0, :, cut] = rounded[length:].astype(F32)
        den_o[0] = dens

    outs = [
        shaped(rows, chip_len, mine),
        shaped(rows, chip_len, 128),
        shaped(rows, length, mine, dtype=BF),
        shaped(rows, length, mine),
    ]
    inputs = [fq, num, den, own, got, idc, idr]
    return row_call(
        kernel, "attend", info, inputs, [per_row(v) for v in inputs], outs,
        flops=rows * chip_len * mine * m * 6,
    )


def grads_one_kernel(info, go, go_got, out_weight, att, den, fq, idc, idr):
    rows, length, width = go.shape
    heads, m = fq.shape[1], fq.shape[3]
    mine = width // 2
    e = mine // heads
    n = heads // 2 * e + 8
    spare = heads // 2 * e + heads // 2

    def kernel(info_ref, go_r, gog_r, wo_r, att_r, den_r, fq_r, idc_r, idr_r, dn_o, dd_o, keep, send):
        chip = jnp.concatenate([go_r[0], gog_r[0].astype(BF)], 0)
        pulls = mm_nt(chip, wo_r[...])
        lead, tail, first, last = edges(idc_r, idr_r)
        lead, tail = lead.astype(F32), tail.astype(F32)
        lane = lax.broadcasted_iota(jnp.int32, (2 * length, 128), 1)
        dds = jnp.zeros((2 * length, 128), F32)
        for h in range(heads):
            cut = slice(h * e, (h + 1) * e)
            denom = den_r[0, :, h : h + 1]
            pull = pulls[:, cut]
            dn = (pull / denom).astype(BF)
            dn_o[0, :, cut] = dn
            dd = -jnp.sum(pull * att_r[0, :, cut], -1, keepdims=True) / denom
            dds = jnp.where(lane == h, dd, dds)
            wide = dn.astype(F32)
            sums = mm_tn(jnp.concatenate([wide * lead, wide * tail], 1).astype(BF), fq_r[0, h])
            high = dd.astype(BF).astype(F32)
            low = dd - high
            four = jnp.concatenate([high * lead, low * lead, high * tail, low * tail], 1)
            zs = mm_tn(four.astype(BF), fq_r[0, h])
            put_edges(info_ref, keep, send, h, heads, sums, zs[0:1] + zs[1:2], zs[2:3] + zs[3:4])
        dd_o[0] = dds
        put_tags(keep, send, spare, first, last)

    outs = [
        shaped(rows, 2 * length, mine, dtype=BF),
        shaped(rows, 2 * length, 128),
        shaped(rows, 2, n, m),
        shaped(rows, 2, n, m),
    ]
    specs = [
        per_row(go), per_row(go_got),
        pl.BlockSpec((mine, width), lambda r, info: (info[0], 0)),
        per_row(att), per_row(den), per_row(fq), per_row(idc), per_row(idr),
    ]
    return row_call(
        kernel, "grads_one", info, [go, go_got, out_weight, att, den, fq, idc, idr], specs, outs,
        flops=rows * length * width * mine * 6,
    )


def pulled_back(grad_feat, feat, part, feats):
    e = feats.shape[0]
    weighted = grad_feat * feat.astype(F32)
    inner = (weighted * e ** (-0.25)).astype(BF)
    folded = jnp.sum(weighted, -1, keepdims=True) * e ** (-0.5)
    return (mm_nt(inner, feats) - part.astype(F32) * folded).astype(BF)


def grads_two_kernel(info, fq, fk, queries, values, dn, dd, features, own, got, idc, idr, deps=()):
    rows, heads, chip_len, m = fq.shape
    mine = queries.shape[2]
    e = mine // heads

    def kernel(
        info_ref, fq_r, fk_r, q_r, v_r, dn_r, dd_r, f_r, own_r, got_r, idc_r, idr_r, dq_o, dfk_o, dv_o
    ):
        same = idc_r[0] == idr_r[0]
        lead, tail, _, _ = edges(idc_r, idr_r)
        lead, tail = lead.astype(F32), tail.astype(F32)
        for h in range(heads):
            cut = slice(h * e, (h + 1) * e)
            feat_q, feat_k = fq_r[0, h], fk_r[0, h]
            part, value = dn_r[0, :, cut], v_r[0, :, cut]
            denom = dd_r[0, :, h : h + 1]
            scores = jnp.where(same, mm_nt(feat_q, feat_k), 0.0).astype(BF)
            pulls = jnp.where(same, mm_nt(part, value) + denom, 0.0).astype(BF)
            dv_o[0, :, cut] = mm_tn(scores, part)
            dfk_o[0, h] = mm_tn(pulls, feat_q)
            before, behind, zb, za = carry_of(info_ref, own_r, got_r, h, heads, e)
            wide = part.astype(F32)
            both = jnp.concatenate([wide * lead, wide * tail], 1).astype(BF)
            grad = (
                mm(pulls, feat_k)
                + mm(both, jnp.concatenate([before, behind], 0).astype(BF))
                + denom * (lead * zb + tail * za)
            )
            dq_o[0, :, cut] = pulled_back(grad, feat_q, q_r[0, :, cut], f_r[h])

    outs = [
        shaped(rows, chip_len, mine, dtype=BF),
        shaped(rows, heads, chip_len, m),
        shaped(rows, chip_len, mine),
    ]
    inputs = [fq, fk, queries, values, dn, dd, features, own, got, idc, idr]
    specs = [per_row(v) for v in inputs]
    specs[6] = head_features(features, heads)
    return row_call(
        kernel, "grads_two", info, inputs, specs, outs, deps, flops=rows * chip_len * chip_len * mine * 30
    )


def grads_three_kernel(info, fk, keys, values, dfk, dv, features, own, got, idc, idr, deps=()):
    rows, heads, chip_len, m = fk.shape
    mine = keys.shape[2]
    e = mine // heads

    def kernel(
        info_ref, fk_r, k_r, v_r, dfk_r, dv_r, f_r, own_r, got_r, idc_r, idr_r, dk_o, dv_o
    ):
        lead, tail, _, _ = edges(idc_r, idr_r)
        lead, tail = lead.astype(F32), tail.astype(F32)
        for h in range(heads):
            cut = slice(h * e, (h + 1) * e)
            feat = fk_r[0, h]
            before, behind, zb, za = carry_of(info_ref, own_r, got_r, h, heads, e)
            kv = jnp.concatenate([before, behind], 0).astype(BF)
            wide = v_r[0, :, cut].astype(F32)
            both = jnp.concatenate([wide * lead, wide * tail], 1).astype(BF)
            grad = dfk_r[0, h] + mm(both, kv) + (lead * zb + tail * za)
            dk_o[0, :, cut] = pulled_back(grad, feat, k_r[0, :, cut], f_r[h])
            more = mm_nt(feat, kv)
            total_v = dv_r[0, :, cut] + lead * more[:, :e] + tail * more[:, e:]
            dv_o[0, :, cut] = total_v.astype(BF)

    outs = [shaped(rows, chip_len, mine, dtype=BF), shaped(rows, chip_len, mine, dtype=BF)]
    inputs = [fk, keys, values, dfk, dv, features, own, got, idc, idr]
    specs = [per_row(v) for v in inputs]
    specs[5] = head_features(features, heads)
    return row_call(
        kernel, "grads_three", info, inputs, specs, outs, deps, flops=rows * chip_len * m * mine * 8
    )


def shares_kernel(info, dq, dk, dv, query_weight, key_weight, value_weight, deps=()):
    rows, chip_len, mine = dq.shape
    width = query_weight.shape[0]
    length = chip_len // 2

    def kernel(info_ref, dq_r, dk_r, dv_r, wq_r, wk_r, wv_r, here_o, send_o):
        total_x = (
            mm_nt(dq_r[0], wq_r[...]) + mm_nt(dk_r[0], wk_r[...]) + mm_nt(dv_r[0], wv_r[...])
        )
        here_o[0] = total_x[:length]
        send_o[0] = total_x[length:]

    outs = [shaped(rows, length, width), shaped(rows, length, width)]
    specs = [per_row(dq), per_row(dk), per_row(dv)] + [
        weight_columns(w, mine) for w in (query_weight, key_weight, value_weight)
    ]
    return row_call(
        kernel, "shares", info, [dq, dk, dv, query_weight, key_weight, value_weight], specs, outs, deps,
        flops=rows * chip_len * mine * width * 6,
    )


def norm(hidden):
    mean = jnp.mean(hidden, -1, keepdims=True)
    centered = hidden - mean
    variance = jnp.mean(centered * centered, -1, keepdims=True)
    inv_std = lax.rsqrt(variance + EPSILON)
    return centered * inv_std, inv_std


def norm_back(upstream, normed, inv_std, gain):
    scaled = upstream * gain
    return inv_std * (
        scaled
        - jnp.mean(scaled, -1, keepdims=True)
        - normed * jnp.mean(scaled * normed, -1, keepdims=True)
    )


def put_sums(ref, upstream, normed):
    ref[...] = jnp.zeros_like(ref)
    ref[0:1, :] = jnp.sum(upstream * normed, 0, keepdims=True)
    ref[1:2, :] = jnp.sum(upstream, 0, keepdims=True)


def ffn_chunk(j, info, chunks):
    return lax.rem(j + (1 - info[0]) * (chunks // 2), chunks)


def ffn_forward(info, x, att, att_got, out_weight, first, up, down, second, cot, chunks=2):
    count, width = x.shape
    mine = att.shape[1]
    ff = up.shape[1]
    size = ff // chunks
    half = chunks // 2

    def kernel(
        info_ref, x_r, att_r, attg_r, wo_r, wog_r, first_r, up_r, down_r, second_r, cot_r,
        y_o, ys_o, here_o, send_o, slope_o, out_o, dz_o, dzs_o, dh_o, unit_o, inv_o, sums_o, y_s, acc,
    ):
        j = pl.program_id(0)

        @pl.when(j == 0)
        def _():
            hidden = (
                x_r[...].astype(F32)
                + mm(att_r[...], wo_r[...])
                + mm(attg_r[...].astype(BF), wog_r[...])
            )
            normed, inv_std = norm(hidden)
            unit_o[...] = normed
            inv_o[...] = jnp.broadcast_to(inv_std, inv_o.shape)
            y = normed * first_r[0:1, :] + first_r[1:2, :]
            acc[...] = y
            y_s[...] = y.astype(BF)
            y_o[...] = y_s[...]
            ys_o[...] = y_s[...].astype(F32)

        inner = mm(y_s[...], up_r[...])
        bell = 0.5 * (1.0 + lax.erf(inner * 0.7071067811865476))
        slope_o[...] = bell + inner * (jnp.exp(-0.5 * inner * inner) * 0.3989422804014327)
        act = (inner * bell).astype(BF)

        @pl.when(j < half)
        def _():
            send_o[...] = act.astype(F32)

        @pl.when(j >= half)
        def _():
            here_o[...] = act

        acc[...] += mm(act, down_r[...])

        @pl.when(j == chunks - 1)
        def _():
            normed, inv_std = norm(acc[...])
            gain = second_r[0:1, :]
            out_o[...] = (normed * gain + second_r[1:2, :]).astype(BF)
            upstream = cot_r[...].astype(F32)
            put_sums(sums_o, upstream, normed)
            grad = norm_back(upstream, normed, inv_std, gain)
            dh_o[...] = grad
            dz_o[...] = grad.astype(BF)
            dzs_o[...] = grad.astype(BF).astype(F32)

    def whole(array):
        return pl.BlockSpec(array.shape, lambda j, info: (0, 0))

    flat = pl.BlockSpec((count, width), lambda j, info: (0, 0))
    outs = [
        (shaped(count, width, dtype=BF), flat),
        (shaped(count, width), flat),
        (shaped(count, ff // 2, dtype=BF), pl.BlockSpec((count, size), lambda j, info: (0, jnp.maximum(j - half, 0)))),
        (shaped(count, ff // 2), pl.BlockSpec((count, size), lambda j, info: (0, jnp.minimum(j, half - 1)))),
        (shaped(count, ff), pl.BlockSpec((count, size), lambda j, info: (0, j))),
        (shaped(count, width, dtype=BF), flat),
        (shaped(count, width, dtype=BF), flat),
        (shaped(count, width), flat),
        (shaped(count, width), flat),
        (shaped(count, width), flat),
        (shaped(count, 128), pl.BlockSpec((count, 128), lambda j, info: (0, 0))),
        (shaped(8, width), pl.BlockSpec((8, width), lambda j, info: (0, 0))),
    ]
    return pl.pallas_call(
        kernel,
        grid_spec=pltpu.PrefetchScalarGridSpec(
            num_scalar_prefetch=1,
            grid=(chunks,),
            in_specs=[
                whole(x), whole(att), whole(att_got),
                pl.BlockSpec((mine, width), lambda j, info: (info[0], 0)),
                pl.BlockSpec((mine, width), lambda j, info: (1 - info[0], 0)),
                whole(first),
                pl.BlockSpec((width, size), lambda j, info: (0, ffn_chunk(j, info, chunks))),
                pl.BlockSpec((size, width), lambda j, info: (ffn_chunk(j, info, chunks), 0)),
                whole(second), whole(cot),
            ],
            out_specs=[spec for _, spec in outs],
            scratch_shapes=[pltpu.VMEM((count, width), BF), pltpu.VMEM((count, width), F32)],
        ),
        out_shape=[shape for shape, _ in outs],
        compiler_params=pltpu.CompilerParams(vmem_limit_bytes=ROOM),
        cost_estimate=cost("ffn_forward"),
        name="ffn_forward",
    )(info, x, att, att_got, out_weight, out_weight, first, up, down, second, cot)


def ffn_inner(info, dz, down, slope, chunks=2):
    count, width = dz.shape
    ff = down.shape[0]
    size = ff // chunks
    half = chunks // 2

    def kernel(info_ref, dz_r, down_r, slope_r, here_o, send_o):
        j = pl.program_id(0)
        grad = (mm_nt(dz_r[...], down_r[...]) * slope_r[...]).astype(BF)

        @pl.when(j < half)
        def _():
            send_o[...] = grad.astype(F32)

        @pl.when(j >= half)
        def _():
            here_o[...] = grad

    return pl.pallas_call(
        kernel,
        grid_spec=pltpu.PrefetchScalarGridSpec(
            num_scalar_prefetch=1,
            grid=(chunks,),
            in_specs=[
                pl.BlockSpec((count, width), lambda j, info: (0, 0)),
                pl.BlockSpec((size, width), lambda j, info: (ffn_chunk(j, info, chunks), 0)),
                pl.BlockSpec((count, size), lambda j, info: (0, j)),
            ],
            out_specs=[
                pl.BlockSpec((count, size), lambda j, info: (0, jnp.maximum(j - half, 0))),
                pl.BlockSpec((count, size), lambda j, info: (0, jnp.minimum(j, half - 1))),
            ],
        ),
        out_shape=[shaped(count, ff // 2, dtype=BF), shaped(count, ff // 2)],
        compiler_params=pltpu.CompilerParams(vmem_limit_bytes=ROOM),
        cost_estimate=cost("ffn_inner"),
        name="ffn_inner",
    )(info, dz, down, slope)


def ffn_back(info, here, send, up, dh, unit, inv, first, deps=(), chunks=2):
    count, width = dh.shape
    ff = up.shape[1]
    size = ff // chunks
    half = chunks // 2

    def kernel(info_ref, here_r, send_r, up_r, dh_r, unit_r, inv_r, first_r, *rest):
        dh_o, go_o, gos_o, sums_o, acc = rest[len(deps) :]
        j = pl.program_id(0)

        @pl.when(j == 0)
        def _():
            acc[...] = dh_r[...]

        @pl.when(j < half)
        def _():
            acc[...] += mm_nt(send_r[...].astype(BF), up_r[...])

        @pl.when(j >= half)
        def _():
            acc[...] += mm_nt(here_r[...], up_r[...])

        @pl.when(j == chunks - 1)
        def _():
            upstream, normed = acc[...], unit_r[...]
            put_sums(sums_o, upstream, normed)
            grad = norm_back(upstream, normed, inv_r[:, 0:1], first_r[0:1, :])
            dh_o[...] = grad
            go_o[...] = grad.astype(BF)
            gos_o[...] = grad.astype(BF).astype(F32)

    def whole(array):
        return pl.BlockSpec(array.shape, lambda j, info: (0, 0))

    flat = pl.BlockSpec((count, width), lambda j, info: (0, 0))
    return pl.pallas_call(
        kernel,
        grid_spec=pltpu.PrefetchScalarGridSpec(
            num_scalar_prefetch=1,
            grid=(chunks,),
            in_specs=[
                pl.BlockSpec((count, size), lambda j, info: (0, jnp.maximum(j - half, 0))),
                pl.BlockSpec((count, size), lambda j, info: (0, jnp.minimum(j, half - 1))),
                pl.BlockSpec((width, size), lambda j, info: (0, ffn_chunk(j, info, chunks))),
                whole(dh), whole(unit), whole(inv), whole(first),
            ] + [ANY] * len(deps),
            out_specs=[flat, flat, flat, pl.BlockSpec((8, width), lambda j, info: (0, 0))],
            scratch_shapes=[pltpu.VMEM((count, width), F32)],
        ),
        out_shape=[
            shaped(count, width), shaped(count, width, dtype=BF), shaped(count, width), shaped(8, width)
        ],
        compiler_params=pltpu.CompilerParams(vmem_limit_bytes=ROOM),
        cost_estimate=cost("ffn_back"),
        name="ffn_back",
    )(info, here, send, up, dh, unit, inv, first, *deps)


def tag_of(ref, k, spare):
    return ref[0, k, spare : spare + 1, 0:1]


def ordered(info_ref, mine, theirs):
    one = info_ref[1] == 1

    def chip(at, k):
        here = one if at else jnp.logical_not(one)
        return jnp.where(here, mine[0, k], theirs[0, k])

    return [[chip(at, k) for k in (0, 1)] for at in (0, 1)]


def join_plane(info, mine, theirs, spare, deps=()):
    rows, _, n, m = mine.shape

    def kernel(info_ref, mine_r, theirs_r, up_o, down_o):
        (lead0, tail0), (lead1, tail1) = ordered(info_ref, mine_r, theirs_r)

        def tag(part):
            return part[spare : spare + 1, 0:1]

        is_sum = lax.broadcasted_iota(jnp.int32, (n, m), 0) < spare
        up_o[0] = tail1 + jnp.where(is_sum & (tag(tail0) == tag(tail1)), tail0, 0.0)
        down_o[0] = lead0 + jnp.where(is_sum & (tag(lead1) == tag(lead0)), lead1, 0.0)

    outs = [shaped(rows, n, m), shaped(rows, n, m)]
    return row_call(kernel, "join_plane", info, [mine, theirs], [per_row(mine)] * 2, outs, deps)


def split_plane(info, mine, theirs, ups, downs, spare):
    rows, _, n, m = mine.shape
    steps = len(ups)

    def kernel(info_ref, mine_r, theirs_r, *refs):
        give_o, own_o = refs[2 * steps :]
        (lead0, tail0), (lead1, tail1) = ordered(info_ref, mine_r, theirs_r)

        def tag(part):
            return part[spare : spare + 1, 0:1]

        before = jnp.zeros((n, m), F32)
        behind = jnp.zeros((n, m), F32)
        for k in range(steps):
            up, down = refs[k][0], refs[steps + k][0]
            before = before + jnp.where(tag(up) == tag(lead0), up, 0.0)
            behind = behind + jnp.where(tag(down) == tag(tail1), down, 0.0)
        behind0 = jnp.where(tag(tail0) == tag(lead1), lead1, 0.0) + jnp.where(
            tag(tail0) == tag(tail1), behind, 0.0
        )
        before1 = jnp.where(tag(lead1) == tag(tail0), tail0, 0.0) + jnp.where(
            tag(lead1) == tag(lead0), before, 0.0
        )
        one = info_ref[1] == 1
        give_o[0, 0] = jnp.where(one, before, before1)
        give_o[0, 1] = jnp.where(one, behind0, behind)
        own_o[0, 0] = jnp.where(one, before1, before)
        own_o[0, 1] = jnp.where(one, behind, behind0)

    inputs = [mine, theirs, *ups, *downs]
    outs = [shaped(rows, 2, n, m), shaped(rows, 2, n, m)]
    return row_call(kernel, "split_plane", info, inputs, [per_row(v) for v in inputs], outs)


def exchange(net, info, keep, send, ids_row, chip_len, spare, late=()):
    if not net.fast:
        first, last = jnp.min(ids_row, 2), jnp.max(ids_row, 2)
        pay = jnp.stack([keep, send], 1)
        up, down = pay[:, :, 1], pay[:, :, 0]
        before = jnp.zeros_like(up)
        behind = jnp.zeros_like(up)
        for _ in range(min(net.n_seq // 2 - 1, -(-SEG_MOST // chip_len))):
            up, down = net.shift(up, 1), net.shift(down, -1)
            reached = up[:, 0, spare, 0:1] == first
            before = before + jnp.where(reached[:, :, None, None], up, 0.0)
            reached = down[:, 0, spare, 0:1] == last
            behind = behind + jnp.where(reached[:, :, None, None], down, 0.0)
        return jnp.stack([before[:, 0], behind[:, 0]], 1), jnp.stack([before[:, 1], behind[:, 1]], 1)
    theirs = net.over_x(send)
    up, down = join_plane(info, keep, theirs, spare, late[0] if late else ())
    ups, downs = [], []
    for _ in range(min(net.nz - 1, -(-SEG_MOST // (2 * chip_len)))):
        up, down = net.z_up(up), net.z_down(down)
        ups.append(up)
        downs.append(down)
    if late:
        late[1].extend([ups[0], downs[0]])
    give, own = split_plane(info, keep, theirs, ups, downs, spare)
    if late:
        late[2].append(own)
    return own, net.over_x(give)


def body(
    tokens,
    segment_ids,
    features,
    query_weight,
    key_weight,
    value_weight,
    out_weight,
    up_weight,
    down_weight,
    first_gain,
    first_bias,
    second_gain,
    second_bias,
    cotangent,
):
    CALLS.clear()
    net = Net(lax.axis_size("dp"), lax.axis_size("seq"))
    rows, length, width = tokens.shape
    heads_all, head_dim, _ = features.shape
    heads = heads_all // 2
    mine = width // 2
    ff = up_weight.shape[1]
    ff_half = ff // 2
    core = net.core
    fast = net.fast
    chip_len = 2 * length
    count = rows * length
    spare = heads // 2 * head_dim + heads // 2
    side = net.x if fast else jnp.zeros_like(core)
    info = jnp.stack([core, side]).astype(jnp.int32)

    tokens_got = net.over_core(tokens.astype(F32))
    ids = segment_ids.astype(F32)
    ids_chip = jnp.concatenate([ids, net.over_core(ids)], 1)
    idr, idc = ids_chip[:, None, :], ids_chip[:, :, None]

    keys, values, fk, keep, send = keys_kernel(
        info, tokens, tokens_got, key_weight, value_weight, features, idc, idr
    )
    queries, fq, num, den = queries_kernel(
        info, tokens, tokens_got, query_weight, features, fk, values, idc, idr
    )
    own, got = exchange(net, info, keep, send, idr, chip_len, spare)
    att, den, att_here, att_send = attend_kernel(info, fq, num, den, own, got, idc, idr)
    att_got = net.over_core(att_send).reshape(count, mine)

    flat = tokens.reshape(count, width)
    first = jnp.stack([first_gain, first_bias])
    second = jnp.stack([second_gain, second_bias])
    (
        y1, y1_send, act, act_send, slope, result, dz, dz_send, dh2, unit, inv, sums_two
    ) = ffn_forward(
        info, flat, att_here.reshape(count, mine), att_got, out_weight, first,
        up_weight, down_weight, second, cotangent.reshape(count, width),
    )
    y1_got = net.over_core(y1_send)
    act_got = net.over_core(act_send)
    dz_got = net.over_core(dz_send)
    df, df_send = ffn_inner(info, dz, down_weight, slope)
    df_got = net.over_core(df_send)

    one = jnp.where(net.seq < 0, 0.5, 1.0).astype(F32)

    def rounded(wide):
        return (wide * one).astype(BF)

    def both(a, b):
        return jnp.concatenate([a, rounded(b)], 0)

    deps = ()
    if fast:
        bits_mine = stage_bits(net, 0)
        down_parts = (act, act_got, dz, dz_got)
        up_parts = (y1, y1_got, df, df_got)
        f_sends = down_products(1 - bits_mine, *down_parts, deps=[df])
        f_sends = up_products(1 - bits_mine, *up_parts, f_sends)
        deps = f_sends[1:]
    else:
        grad_up = total(net, mm_tn(both(y1, y1_got), both(df, df_got)), 1)
        grad_down = total(net, mm_tn(both(act, act_got), both(dz, dz_got)), 0)

    dh1, go, go_send, sums_one = ffn_back(
        info, df, df_send, up_weight, dh2, unit, inv, first, deps
    )
    go_got = net.over_core(go_send)
    dn, dd, keep_d, send_d = grads_one_kernel(
        info, go.reshape(rows, length, width), go_got.reshape(rows, length, width), out_weight,
        att, den, fq, idc, idr,
    )
    late = []
    if fast:
        f_gots = moves(net, f_sends, 0)
        f_keeps = down_products(bits_mine, *down_parts, deps=[go])
        f_keeps = up_products(bits_mine, *up_parts, f_keeps)
        f_sends, f_keeps = add_stage(net, f_keeps, f_gots, 1, [send_d])
        late = [[f_sends[1]], [], []]
    own_d, got_d = exchange(net, info, keep_d, send_d, idr, chip_len, spare, late)
    dq, dfk, dv = grads_two_kernel(
        info, fq, fk, queries, values, dn, dd, features, own, got, idc, idr, deps=late[2] if fast else ()
    )
    if fast:
        f_gots = [
            stage_move(net, f_sends[0], 0, 1), stage_move(net, tie(f_sends[1], *late[1]), 1, 1)
        ]
        f_sends, f_keeps = add_stage(net, f_keeps, f_gots, 2, [dq])
        f_gots = moves(net, f_sends, 2)
    dk, dv = grads_three_kernel(
        info, fk, keys, values, dfk, dv, features, own_d, got_d, idc, idr, deps=f_sends[1:] if fast else ()
    )

    chip_flat = (rows * chip_len, mine)
    if fast:
        sums = jnp.concatenate([sums_one[:2], sums_two[:2]])
        small = (sums + net.over_core(sums)).reshape(8, mine)
        attn_parts = (
            flat, tokens_got.reshape(count, width),
            dq.reshape(chip_flat), dk.reshape(chip_flat), dv.reshape(chip_flat),
            att.reshape(chip_flat), go, go_got, small,
        )

        def over_core(parts):
            return [net.over_core(part) for part in parts]

        a_sends = attn_products(1 - bits_mine, *attn_parts)
        a_gots = moves(net, a_sends, 0)
        a_keeps = attn_products(bits_mine, *attn_parts, deps=a_sends)
        f_sends, f_keeps = add_stage(net, f_keeps, f_gots, 3, a_keeps)
        f_gots = moves(net, f_sends, 3)
        f_own = last_add(f_keeps, f_gots)
        f_gots = moves(net, f_own, 3)
        f_own = join_stage(net, f_own, f_gots, 3)
        f_gots = moves(net, f_own, 2)
        a_sends, a_keeps = add_stage(net, a_keeps, a_gots, 1, f_own[1:])
        a_gots = moves(net, a_sends, 1)
        a_sends, a_keeps = add_stage(net, a_keeps, a_gots, 2)
        a_gots = moves(net, a_sends, 2)
        f_one = join_stage(net, f_own, f_gots, 2, a_sends)
        f_two = moves(net, f_one, 1)
        a_sends, a_keeps = add_stage(net, a_keeps, a_gots, 3, f_one[1:])
        a_gots = moves(net, a_sends, 3)
        f_one_core = over_core([tie(part, *a_sends) for part in f_one])
        shapes = [shaped(*w.shape) for w in (up_weight, down_weight)]
        copies = ffn_copies(width, ff_half)
        outs, done = place_pieces(
            net, [(f_one, 0, 0, 0), (f_one_core, 1, 0, 0)], shapes, copies, a_sends
        )
        a_keeps = [tie(a_keeps[0], *f_two)]
        a_own = last_add(a_keeps, a_gots, done)
        a_gots = moves(net, a_own, 3)
        f_three = moves(net, f_one, 0)
        a_own = join_stage(net, a_own, a_gots, 3, done)
        a_gots = moves(net, a_own, 2)
        f_two_core = over_core(f_two)
        outs, done = place_pieces(
            net, [(f_two, 0, 0, 1), (f_two_core, 1, 0, 1)], outs, copies, a_own
        )
        f_four = moves(net, f_two, 0)
        a_one = join_stage(net, a_own, a_gots, 2, done)
        a_two = moves(net, a_one, 1)
        a_three = moves(net, a_one, 0)
        f_three_core = over_core(f_three)
        outs, done = place_pieces(
            net, [(f_three, 0, 1, 0), (f_three_core, 1, 1, 0)], outs, copies, a_one
        )
        here, share_send = shares_kernel(
            info, dq, dk, dv, query_weight, key_weight, value_weight, deps=done
        )
        a_four = moves(net, a_two, 0)
        f_four_core = over_core(f_four)
        a_one_core = over_core(a_one)
        (grad_up, grad_down), done = place_pieces(
            net, [(f_four, 0, 1, 1), (f_four_core, 1, 1, 1)], outs, copies, [share_send]
        )
        shapes = [shaped(width, width)] * 4
        copies = attn_copies(mine)
        a_two_core = over_core(a_two)
        outs, done = place_pieces(
            net,
            [(a_one, 0, 0, 0), (a_one_core, 1, 0, 0), (a_two, 0, 0, 1), (a_two_core, 1, 0, 1)],
            shapes, copies, done,
        )
        a_three_core = over_core(a_three)
        outs, done = place_pieces(
            net, [(a_three, 0, 1, 0), (a_three_core, 1, 1, 0)], outs, copies, done
        )
        a_four = [tie(part, *done) for part in a_four]
        outs, done = place_pieces(net, [(a_four, 0, 1, 1)], outs, copies)
        (grad_query, grad_key, grad_value, grad_out), _ = place_pieces(
            net, [(over_core(a_four), 1, 1, 1)], outs, copies
        )
        at = 4 * mine - (4 * mine + SPARE_ROWS) // 2
        one, two = a_one[0][at : at + 8], a_two[0][at : at + 8]
        small = jnp.where(stage_bit(net, 0, 1, core) == 1, one, two).reshape(4, width)
    else:
        x_chip = jnp.concatenate([tokens, rounded(tokens_got)], 1).reshape(rows * chip_len, width)
        go_chip = jnp.concatenate(
            [go.reshape(rows, length, width), rounded(go_got).reshape(rows, length, width)], 1
        ).reshape(rows * chip_len, width)
        grad_query = total(net, mm_tn(x_chip, dq.reshape(chip_flat)), 1)
        grad_key = total(net, mm_tn(x_chip, dk.reshape(chip_flat)), 1)
        grad_value = total(net, mm_tn(x_chip, dv.reshape(chip_flat)), 1)
        grad_out = total(net, mm_tn(att.astype(BF).reshape(chip_flat), go_chip), 0)

        here, share_send = shares_kernel(info, dq, dk, dv, query_weight, key_weight, value_weight)
        small = lax.psum(jnp.concatenate([sums_one[:2], sums_two[:2]]), AXES)

    grad_input = dh1.reshape(rows, length, width) + here + net.over_core(share_send)
    return (
        result.reshape(rows, length, width),
        grad_input.astype(BF),
        grad_query,
        grad_key,
        grad_value,
        grad_out,
        grad_up,
        grad_down,
        small[0],
        small[1],
        small[2],
        small[3],
    )


def solution(mesh):
    split = P("dp", "seq", None)
    placed = (split, P("dp", "seq")) + (P(),) * 11 + (split,)
    return jax.shard_map(
        body,
        mesh=mesh,
        in_specs=placed,
        out_specs=(split, split) + (P(),) * 10,
        check_vma=False,
    )
```

```python
import jax
import jax.numpy as jnp
from jax import lax
from jax.experimental import pallas as pl
from jax.experimental.pallas import tpu as pltpu
from jax.sharding import PartitionSpec as P

SEG_MOST = 2048
SPARE_ROWS = 128
EPSILON = 1e-06
AXES = ("dp", "seq")
BF = jnp.bfloat16
F32 = jnp.float32
ANY = pl.BlockSpec(memory_space=pl.ANY)
HBM = pl.BlockSpec(memory_space=pltpu.HBM)
ROOM = 20 << 20
SMALL = 14 << 20


COSTS = {
    "tie": 0.1, "add_stage": 12, "last_add": 4.5, "join_stage": 9, "down_products": 12, "up_products 1": 6,
    "up_products 2": 1, "attn_products": 12, "place_pieces": 13.5, "ffn_forward": 15, "ffn_inner": 8,
    "ffn_back": 3, "keys": 10, "queries": 8, "attend": 6, "grads_one": 3, "grads_two": 12, "grads_three": 8,
    "shares": 9, "join_plane": 3, "split_plane": 3,
    "join_stage 2": 3,
    "add_stage 5": 6,
}
CALLS = {}


def cost(name):
    CALLS[name] = CALLS.get(name, 0) + 1
    us = COSTS.get(f"{name} {CALLS[name]}", COSTS.get(name))
    return pl.CostEstimate(flops=int(us * 1e9), bytes_accessed=1, transcendentals=0)


def shaped(*shape, dtype=F32):
    return jax.ShapeDtypeStruct(shape, dtype)


def mm(a, b):
    return jnp.dot(a, b, preferred_element_type=F32)


def mm_nt(a, b):
    return lax.dot_general(a, b, (((1,), (1,)), ((), ())), preferred_element_type=F32)


def mm_tn(a, b):
    return lax.dot_general(a, b, (((0,), (0,)), ((), ())), preferred_element_type=F32)


def dslice(a, start, size, axis=0):
    return lax.dynamic_slice_in_dim(a, start, size, axis)


class Net:
    def __init__(self, n_dp, n_seq):
        self.n_dp, self.n_seq = n_dp, n_seq
        self.nz = 4
        self.nx = n_seq // 8
        self.fast = n_dp == 2 and n_seq == 16
        seq = lax.axis_index("seq")
        self.y = lax.axis_index("dp")
        self.core = seq % 2
        self.x = (seq // 2) % self.nx
        self.z = seq // (2 * self.nx)
        self.seq = seq

    def perm(self, move):
        pairs = []
        for y in range(self.n_dp):
            for s in range(self.n_seq):
                target = move(y, s // (2 * self.nx), (s // 2) % self.nx, s % 2)
                if target is not None:
                    ty, tz, tx, tc = target
                    pairs.append((y * self.n_seq + s, ty * self.n_seq + (tz * self.nx + tx) * 2 + tc))
        return pairs

    def send(self, value, move):
        return lax.ppermute(value, AXES, self.perm(move))

    def over_core(self, value):
        return self.send(value, lambda y, z, x, c: (y, z, x, 1 - c))

    def over_x(self, value):
        return self.send(value, lambda y, z, x, c: (y, z, 1 - x, c))

    def z_up(self, value):
        return self.send(value, lambda y, z, x, c: (y, z + 1, x, c) if z < 3 else None)

    def z_down(self, value):
        return self.send(value, lambda y, z, x, c: (y, z - 1, x, c) if z > 0 else None)

    def shift(self, value, step):
        chips = self.n_seq // 2
        pairs = []
        for y in range(self.n_dp):
            for s in range(self.n_seq):
                if 0 <= s // 2 + step < chips:
                    pairs.append((y * self.n_seq + s, y * self.n_seq + s + 2 * step))
        return lax.ppermute(value, AXES, pairs)


ORDERS = ((("x", "y", "1", "2"), ("y", "x", "2", "1")), (("1", "2", "x", "y"), ("2", "1", "x", "y")))


def stage_move(net, value, stream, stage):
    def move(y, z, x, c):
        axis = ORDERS[stream][c][stage]
        return {
            "x": (y, z, 1 - x, c),
            "y": (1 - y, z, x, c),
            "1": (y, z ^ 1, x, c),
            "2": (y, z ^ 2, x, c),
        }[axis]

    return net.send(value, move)


def stage_bit(net, stream, stage, core):
    place = {"x": net.x, "y": net.y, "1": net.z % 2, "2": net.z // 2}
    zero, one = (place[ORDERS[stream][c][stage]] for c in (0, 1))
    return jnp.where(core == 0, zero, one)


def tie(value, *deps):
    def kernel(*refs):
        pass

    anywhere = pl.BlockSpec(memory_space=pl.ANY)
    return pl.pallas_call(
        kernel,
        in_specs=[anywhere] * (1 + len(deps)),
        out_specs=anywhere,
        out_shape=jax.ShapeDtypeStruct(value.shape, value.dtype),
        input_output_aliases={0: 0},
        compiler_params=pltpu.CompilerParams(vmem_limit_bytes=SMALL),
        cost_estimate=cost("tie"),
        name="tie",
    )(value, *deps)


def moves(net, parts, stage):
    return [stage_move(net, part, i, stage) for i, part in enumerate(parts)]


def stage_bits(net, stage, count=2):
    return jnp.stack([stage_bit(net, i, stage, net.core) for i in range(count)]).astype(jnp.int32)


def add_stage(net, keeps, gots, stage, deps=()):
    rows, count = keeps[0].shape[0], len(keeps)
    steps = 4 if rows >= 1152 else 2 if rows >= 512 else 1

    def kernel(bits_ref, *refs):
        outs = refs[4 * count + len(deps) :]
        for i in range(2 * count):
            outs[i][...] = refs[2 * i][...] + refs[2 * i + 1][...]

    in_specs, inputs, out_specs, shapes = [], [], [], []
    for side in (0, 1):
        for i, (keep, got) in enumerate(zip(keeps, gots)):
            half, width = keep.shape[0] // 2, keep.shape[1]
            block = (half // steps, width)
            spec = pl.BlockSpec(
                block,
                lambda r, bits, i=i, side=side: (
                    (bits[i] if side else 1 - bits[i]) * steps + r,
                    0,
                ),
            )
            in_specs += [spec, spec]
            inputs += [keep, got]
            out_specs.append(pl.BlockSpec(block, lambda r, bits: (r, 0)))
            shapes.append(shaped(half, width))
    in_specs += [ANY] * len(deps)
    outs = pl.pallas_call(
        kernel,
        grid_spec=pltpu.PrefetchScalarGridSpec(
            num_scalar_prefetch=1, grid=(steps,), in_specs=in_specs, out_specs=out_specs
        ),
        out_shape=shapes,
        compiler_params=pltpu.CompilerParams(vmem_limit_bytes=SMALL),
        cost_estimate=cost("add_stage"),
        name="add_stage",
    )(stage_bits(net, stage, count), *inputs, *deps)
    return outs[:count], outs[count:]


def last_add(keeps, gots, deps=()):
    count = len(keeps)

    def kernel(*refs):
        outs = refs[2 * count + len(deps) :]
        for i in range(count):
            outs[i][...] = refs[i][...] + refs[count + i][...]

    whole = pl.BlockSpec(memory_space=pltpu.VMEM)
    return pl.pallas_call(
        kernel,
        in_specs=[whole] * (2 * count) + [ANY] * len(deps),
        out_specs=[whole] * count,
        out_shape=[shaped(*k.shape) for k in keeps],
        compiler_params=pltpu.CompilerParams(vmem_limit_bytes=SMALL),
        cost_estimate=cost("last_add"),
        name="last_add",
    )(*keeps, *gots, *deps)


def join_stage(net, parts, gots, stage, deps=()):
    steps = max(1, parts[0].shape[0] // 144)
    count = len(parts)

    def kernel(bits_ref, *refs):
        outs = refs[2 * count + len(deps) :]
        for i in range(count):
            bit = bits_ref[i]
            outs[i][pl.ds(bit, 1)] = refs[2 * i][...][None]
            outs[i][pl.ds(1 - bit, 1)] = refs[2 * i + 1][...][None]

    in_specs, out_specs, shapes = [], [], []
    for part in parts:
        n, width = part.shape
        rows = n // steps
        in_specs += [pl.BlockSpec((rows, width), lambda r, bits: (r, 0))] * 2
        out_specs.append(pl.BlockSpec((2, rows, width), lambda r, bits: (0, r, 0)))
        shapes.append(shaped(2, n, width))
    outs = pl.pallas_call(
        kernel,
        grid_spec=pltpu.PrefetchScalarGridSpec(
            num_scalar_prefetch=1,
            grid=(steps,),
            in_specs=in_specs + [ANY] * len(deps),
            out_specs=out_specs,
        ),
        out_shape=shapes,
        compiler_params=pltpu.CompilerParams(vmem_limit_bytes=SMALL),
        cost_estimate=cost("join_stage"),
        name="join_stage",
    )(stage_bits(net, stage, count), *[v for pair in zip(parts, gots) for v in pair], *deps)
    return [out.reshape(2 * out.shape[1], out.shape[2]) for out in outs]


def tn(a, a_other, b, b_other):
    return mm_tn(a, b) + mm_tn(a_other.astype(BF), b_other.astype(BF))


def picked_columns(count, size, index):
    return pl.BlockSpec((count, size), lambda g, bits: (0, index(bits)))


def whole_of(array):
    return pl.BlockSpec(array.shape, lambda g, bits: (0,) * array.ndim)


def down_products(bits, act, act_other, gz, gz_other, deps=()):
    count, width = gz.shape
    unit = act.shape[1] // 12
    sizes = (5 * unit, unit)

    def kernel(bits_ref, a0, a0o, a1, a1o, gz_r, gzo_r, *rest):
        outs, scratch, sems = rest[len(deps) : -2], rest[-2], rest[-1]
        scratch[: sizes[0], :] = tn(a0[...], a0o[...], gz_r[...], gzo_r[...])
        scratch[sizes[0] :, :] = tn(a1[...], a1o[...], gz_r[...], gzo_r[...])
        copies = [
            pltpu.make_async_copy(
                scratch.at[: sizes[0]], outs[0].at[outs[0].shape[0] - sizes[0] :], sems.at[0]
            ),
            pltpu.make_async_copy(
                scratch.at[sizes[0] :], outs[1].at[outs[1].shape[0] - sizes[1] :], sems.at[1]
            ),
        ]
        for copy in copies:
            copy.start()
        for copy in copies:
            copy.wait()

    first = picked_columns(count, sizes[0], lambda bits: bits[0])
    second = picked_columns(count, sizes[1], lambda bits: 10 + bits[1])
    up_rows = act.shape[1] // width * (width // 6)
    return pl.pallas_call(
        kernel,
        grid_spec=pltpu.PrefetchScalarGridSpec(
            num_scalar_prefetch=1,
            grid=(1,),
            in_specs=[first, first, second, second, whole_of(gz), whole_of(gz_other)]
            + [ANY] * len(deps),
            out_specs=[ANY, ANY],
            scratch_shapes=[
                pltpu.VMEM((6 * unit, width), F32),
                pltpu.SemaphoreType.DMA((2,)),
            ],
        ),
        out_shape=[shaped(2 * up_rows + sizes[0], width), shaped(up_rows + sizes[1], width)],
        compiler_params=pltpu.CompilerParams(vmem_limit_bytes=ROOM),
        cost_estimate=cost("down_products"),
        name="down_products",
    )(bits, act, act_other, act, act_other, gz, gz_other, *deps)


def up_products(bits, y1, y1_other, gi, gi_other, outs):
    count, width = y1.shape
    u = width // 6
    parts = gi.shape[1] // width

    def kernel(bits_ref, y1_r, y1o_r, gi_r, gio_r, *rest):
        outs = rest[2:]

        def fill(out):
            y, yo = y1_r[...], y1o_r[...]
            for part in range(parts):
                cut = slice(part * width, (part + 1) * width)
                out[part * u : (part + 1) * u, :] = tn(y, yo, gi_r[:, cut], gio_r[:, cut])

        pl.when(pl.program_id(0) < 2)(lambda: fill(outs[0]))
        pl.when(pl.program_id(0) == 2)(lambda: fill(outs[1]))

    picked = pl.BlockSpec(
        (count, u), lambda i, bits: (0, jnp.where(i < 2, 2 * bits[0] + i, 4 + bits[1]))
    )
    return pl.pallas_call(
        kernel,
        grid_spec=pltpu.PrefetchScalarGridSpec(
            num_scalar_prefetch=1,
            grid=(3,),
            in_specs=[picked, picked, whole_of(gi), whole_of(gi_other), ANY, ANY],
            out_specs=[
                pl.BlockSpec((parts * u, width), lambda i, bits: (jnp.minimum(i, 1), 0)),
                pl.BlockSpec((parts * u, width), lambda i, bits: (0, 0)),
            ],
        ),
        out_shape=[shaped(*o.shape) for o in outs],
        input_output_aliases={5: 0, 6: 1},
        compiler_params=pltpu.CompilerParams(vmem_limit_bytes=ROOM),
        cost_estimate=cost("up_products"),
        name="up_products",
    )(bits, y1, y1_other, gi, gi_other, *outs)


def attn_products(bits, x, x_other, dq, dk, dv, attn, go, go_other, small, deps=()):
    count, width = x.shape
    mine = attn.shape[1]

    def kernel(bits_ref, x_r, xo_r, dq_r, dk_r, dv_r, attn_r, go_r, goo_r, small_r, *rest):
        (out,) = rest[len(deps) :]
        x, xo = x_r[...], xo_r[...].astype(BF)
        for k, grad in enumerate((dq_r, dk_r, dv_r)):
            out[k * mine : (k + 1) * mine, :] = tn(x, xo, grad[:count], grad[count:])
        part = attn_r[...].astype(BF)
        out[3 * mine : 4 * mine, :] = tn(part[:count], part[count:], go_r[...], goo_r[...])
        out[4 * mine :, :] = jnp.zeros((SPARE_ROWS, mine), F32)
        out[4 * mine : 4 * mine + 8, :] = small_r[...]

    half = picked_columns(count, mine, lambda bits: bits[0])
    rows = 4 * mine + SPARE_ROWS
    out = pl.pallas_call(
        kernel,
        grid_spec=pltpu.PrefetchScalarGridSpec(
            num_scalar_prefetch=1,
            grid=(1,),
            in_specs=[half, half]
            + [whole_of(v) for v in (dq, dk, dv, attn)]
            + [half, half, whole_of(small)]
            + [ANY] * len(deps),
            out_specs=pl.BlockSpec((rows, mine), lambda g, bits: (0, 0)),
        ),
        out_shape=shaped(rows, mine),
        compiler_params=pltpu.CompilerParams(vmem_limit_bytes=ROOM),
        cost_estimate=cost("attn_products"),
        name="attn_products",
    )(bits, x, x_other, dq, dk, dv, attn, go, go_other, small, *deps)
    return [out]


def place_pieces(net, pieces, outs, copies, deps=()):
    fresh = isinstance(outs[0], jax.ShapeDtypeStruct)
    n_out, m = len(outs), len(pieces[0][0])
    inputs = [part for piece in pieces for part in piece[0]]
    n = len(inputs)
    scalars = []
    for _, other_core, other_first, other_second in pieces:
        core = 1 - net.core if other_core else net.core
        scalars.append(core)
        for i in range(m):
            for stage, flip in ((0, other_first), (1, other_second)):
                bit = stage_bit(net, i, stage, core)
                scalars.append(1 - bit if flip else bit)
    where = jnp.stack(scalars).astype(jnp.int32)

    def kernel(where_ref, *refs):
        srcs = refs[: n]
        dests = refs[-(n + 3 + n_out) : -(n + 3)]
        refs[-(n + 3)][...] = jnp.zeros((8, 128), F32)
        held, (arrive, sems) = refs[-(n + 2) : -2], refs[-2:]
        loads = [pltpu.make_async_copy(srcs[j], held[j], arrive.at[j]) for j in range(n)]
        for load in loads:
            load.start()

        def each(j, act):
            piece, i = j // m, j % m
            core = where_ref[(1 + 2 * m) * piece]
            at = (1 + 2 * m) * piece + 1 + 2 * i
            first, second = where_ref[at], where_ref[at + 1]
            for quarter in (0, 1):

                @pl.when(second == quarter)
                def _():
                    for k, (src, dest) in enumerate(copies(i, quarter, core, first, held[j], dests)):
                        act(pltpu.make_async_copy(src, dest, sems.at[j, k]))

        for j in range(n):
            loads[j].wait()
            each(j, lambda copy: copy.start())
        for j in range(n):
            each(j, lambda copy: copy.wait())

    operands = inputs + ([] if fresh else list(outs)) + list(deps)
    *outs, done = pl.pallas_call(
        kernel,
        grid_spec=pltpu.PrefetchScalarGridSpec(
            num_scalar_prefetch=1,
            grid=(1,),
            in_specs=[ANY] * len(inputs) + [HBM] * (0 if fresh else n_out) + [ANY] * len(deps),
            out_specs=[HBM] * n_out + [pl.BlockSpec((8, 128), lambda g, where: (0, 0))],
            scratch_shapes=[pltpu.VMEM(part.shape, F32) for part in inputs] + [
                pltpu.SemaphoreType.DMA((n,)),
                pltpu.SemaphoreType.DMA((n, 6)),
            ],
        ),
        out_shape=[shaped(*o.shape) for o in outs] + [shaped(8, 128)],
        input_output_aliases={} if fresh else {1 + n + i: i for i in range(n_out)},
        compiler_params=pltpu.CompilerParams(vmem_limit_bytes=ROOM),
        cost_estimate=cost("place_pieces"),
        name="place_pieces",
    )(where, *operands)
    return outs, [done]


def rows_at(ref, start, size, step, lanes=None):
    start = pl.multiple_of(start, step)
    return ref.at[pl.ds(start, size)] if lanes is None else ref.at[pl.ds(start, size), lanes]


def spans(sizes, at, length):
    start = 0
    for k, size in enumerate(sizes):
        low, high = max(start, at), min(start + size, at + length)
        if low < high:
            yield k, low - start, low - at, high - low
        start += size


def ffn_copies(width, ff_half):
    u, unit = width // 6, ff_half // 12
    parts = ff_half // width

    def copies(i, quarter, c, b, src, dests):
        up, down = dests
        blocks = 1 if i else 2
        sizes = [u] * (parts * blocks) + [unit if i else 5 * unit]
        length = src.shape[0]
        for k, row, at, n in spans(sizes, quarter * length, length):
            if k < parts * blocks:
                block = 4 + b if i else 2 * b + k // parts
                lanes = pl.ds(pl.multiple_of(c * ff_half + k % parts * width, 128), width)
                dest = rows_at(up, block * u + row, n, 8, lanes)
            else:
                start = 10 * unit + b * unit if i else 5 * unit * b
                dest = rows_at(down, c * ff_half + start + row, n, 8)
            yield src.at[at : at + n], dest

    return copies


def attn_copies(mine):
    def copies(i, quarter, c, b, src, dests):
        own = pl.ds(pl.multiple_of(c * mine, 128), mine)
        half = pl.ds(pl.multiple_of(b * mine, 128), mine)
        length = src.shape[0]
        for k, row, at, n in spans([mine] * 4, quarter * length, length):
            if k < 3:
                dest = rows_at(dests[k], b * mine + row, n, 8, own)
            else:
                dest = rows_at(dests[3], c * mine + row, n, 8, half)
            yield src.at[at : at + n], dest

    return copies


def total(net, half, axis):
    size = half.shape[axis]
    shape = tuple(2 * n if i == axis else n for i, n in enumerate(half.shape))
    own = lax.dynamic_update_slice_in_dim(jnp.zeros(shape, F32), half, net.core * size, axis)
    return lax.psum(own, AXES)


def per_row(array):
    rest = array.shape[1:]
    return pl.BlockSpec((1, *rest), lambda r, info: (r, *(0 for _ in rest)))


def row_call(kernel, name, info, inputs, in_specs, outs, deps=(), flops=0):
    n_in = len(inputs)
    rows = outs[0].shape[0]

    def run(info_ref, *refs):
        kernel(info_ref, *refs[:n_in], *refs[n_in + len(deps) :])

    size = sum(v.size * v.dtype.itemsize for v in [*inputs, *outs])
    return pl.pallas_call(
        run,
        grid_spec=pltpu.PrefetchScalarGridSpec(
            num_scalar_prefetch=1,
            grid=(rows,),
            in_specs=list(in_specs) + [ANY] * len(deps),
            out_specs=[per_row(o) for o in outs],
        ),
        out_shape=outs,
        compiler_params=pltpu.CompilerParams(vmem_limit_bytes=ROOM),
        cost_estimate=cost(name),
        name=name,
    )(info, *inputs, *deps)


def edges(idc_ref, idr_ref):
    row = idr_ref[0]
    first = jnp.min(row, axis=1, keepdims=True)
    last = jnp.max(row, axis=1, keepdims=True)
    return idc_ref[0] == first, idc_ref[0] == last, first, last


def phi(part, feats):
    head_dim, feat_count = feats.shape
    wide = part.astype(F32)
    square = jnp.sum(wide * wide, -1, keepdims=True)
    inner = mm(part, feats) * head_dim ** (-0.25) - square * (0.5 * head_dim ** (-0.5))
    return (jnp.exp(inner) * feat_count ** (-0.5)).astype(BF)


def put_edges(info_ref, keep, send, h, heads, sums, lead_z, tail_z):
    half = heads // 2
    group, at = h // half, h % half
    e = sums.shape[0] // 2

    def put(ref):
        ref[0, 0, at * e : (at + 1) * e, :] = sums[:e]
        ref[0, 1, at * e : (at + 1) * e, :] = sums[e:]
        ref[0, 0, half * e + at : half * e + at + 1, :] = lead_z
        ref[0, 1, half * e + at : half * e + at + 1, :] = tail_z

    @pl.when(info_ref[1] == group)
    def _():
        put(keep)

    @pl.when(info_ref[1] != group)
    def _():
        put(send)


def put_tags(keep, send, spare, first, last):
    n, m = keep.shape[2:]
    for ref in (keep, send):
        ref[0, 0, spare:, :] = jnp.broadcast_to(first, (n - spare, m))
        ref[0, 1, spare:, :] = jnp.broadcast_to(last, (n - spare, m))


def weight_columns(weight, mine):
    return pl.BlockSpec((weight.shape[0], mine), lambda r, info: (0, info[0]))


def head_features(features, heads):
    return pl.BlockSpec((heads, *features.shape[1:]), lambda r, info: (info[0], 0, 0))


def keys_kernel(info, x, x_got, key_weight, value_weight, features, idc, idr):
    rows, length, width = x.shape
    mine, heads = width // 2, features.shape[0] // 2
    e, m = features.shape[1:]
    n = heads // 2 * e + 8
    spare = heads // 2 * e + heads // 2

    def kernel(info_ref, x_r, xg_r, wk_r, wv_r, f_r, idc_r, idr_r, k_o, v_o, fk_o, keep, send):
        chip = jnp.concatenate([x_r[0], xg_r[0].astype(BF)], 0)
        keys = mm(chip, wk_r[...]).astype(BF)
        values = mm(chip, wv_r[...]).astype(BF)
        k_o[0] = keys
        v_o[0] = values
        lead, tail, first, last = edges(idc_r, idr_r)
        masks = jnp.concatenate([lead.astype(F32), tail.astype(F32)], 1).astype(BF)
        lead_b, tail_b = masks[:, 0:1], masks[:, 1:2]
        for h in range(heads):
            cut = slice(h * e, (h + 1) * e)
            feat = phi(keys[:, cut], f_r[h])
            fk_o[0, h] = feat
            part = values[:, cut]
            sums = mm_tn(jnp.concatenate([part * lead_b, part * tail_b], 1), feat)
            zs = mm_tn(masks, feat)
            put_edges(info_ref, keep, send, h, heads, sums, zs[0:1], zs[1:2])
        put_tags(keep, send, spare, first, last)

    outs = [
        shaped(rows, 2 * length, mine, dtype=BF),
        shaped(rows, 2 * length, mine, dtype=BF),
        shaped(rows, heads, 2 * length, m, dtype=BF),
        shaped(rows, 2, n, m),
        shaped(rows, 2, n, m),
    ]
    specs = [
        per_row(x), per_row(x_got),
        weight_columns(key_weight, mine), weight_columns(value_weight, mine),
        head_features(features, heads), per_row(idc), per_row(idr),
    ]
    return row_call(
        kernel, "keys", info, [x, x_got, key_weight, value_weight, features, idc, idr], specs, outs,
        flops=rows * length * width * mine * 10,
    )


def queries_kernel(info, x, x_got, query_weight, features, fk, values, idc, idr, deps=()):
    rows, length, width = x.shape
    mine, heads = width // 2, features.shape[0] // 2
    e, m = features.shape[1:]

    def kernel(info_ref, x_r, xg_r, wq_r, f_r, fk_r, v_r, idc_r, idr_r, q_o, fq_o, num_o, den_o):
        chip = jnp.concatenate([x_r[0], xg_r[0].astype(BF)], 0)
        queries = mm(chip, wq_r[...]).astype(BF)
        q_o[0] = queries
        same = idc_r[0] == idr_r[0]
        lane = lax.broadcasted_iota(jnp.int32, (2 * length, 128), 1)
        dens = jnp.ones((2 * length, 128), F32)
        for h in range(heads):
            cut = slice(h * e, (h + 1) * e)
            feat = phi(queries[:, cut], f_r[h])
            fq_o[0, h] = feat
            scores = jnp.where(same, mm_nt(feat, fk_r[0, h]), 0.0)
            num_o[0, :, cut] = mm(scores.astype(BF), v_r[0, :, cut])
            dens = jnp.where(lane == h, jnp.sum(scores, -1, keepdims=True), dens)
        den_o[0] = dens

    outs = [
        shaped(rows, 2 * length, mine, dtype=BF),
        shaped(rows, heads, 2 * length, m, dtype=BF),
        shaped(rows, 2 * length, mine),
        shaped(rows, 2 * length, 128),
    ]
    specs = [
        per_row(x), per_row(x_got), weight_columns(query_weight, mine),
        head_features(features, heads), per_row(fk), per_row(values), per_row(idc), per_row(idr),
    ]
    return row_call(
        kernel, "queries", info,
        [x, x_got, query_weight, features, fk, values, idc, idr], specs, outs, deps,
        flops=rows * length * width * mine * 12,
    )


def carry_of(info_ref, own_r, got_r, h, heads, e):
    half = heads // 2
    group, at = h // half, h % half
    flag = info_ref[1] == group

    def picked(k, rows):
        return jnp.where(flag, own_r[0, k, rows, :], got_r[0, k, rows, :])

    kv = slice(at * e, (at + 1) * e)
    z = slice(half * e + at, half * e + at + 1)
    return picked(0, kv), picked(1, kv), picked(0, z), picked(1, z)


def attend_kernel(info, fq, num, den, own, got, idc, idr):
    rows, heads, chip_len, m = fq.shape
    mine = num.shape[2]
    e = mine // heads
    length = chip_len // 2

    def kernel(info_ref, fq_r, num_r, den_r, own_r, got_r, idc_r, idr_r, att_o, den_o, here_o, send_o):
        lead, tail, _, _ = edges(idc_r, idr_r)
        lead, tail = lead.astype(F32), tail.astype(F32)
        lane = lax.broadcasted_iota(jnp.int32, (chip_len, 128), 1)
        dens = den_r[0]
        for h in range(heads):
            cut = slice(h * e, (h + 1) * e)
            before, behind, zb, za = carry_of(info_ref, own_r, got_r, h, heads, e)
            feat = fq_r[0, h]
            more = mm_nt(feat, jnp.concatenate([before, behind], 0).astype(BF))
            numer = num_r[0, :, cut] + lead * more[:, :e] + tail * more[:, e:]
            extra = jnp.sum(feat.astype(F32) * (lead * zb + tail * za), -1, keepdims=True)
            denom = den_r[0, :, h : h + 1] + extra
            dens = jnp.where(lane == h, denom, dens)
            att = numer / denom
            att_o[0, :, cut] = att
            rounded = att.astype(BF)
            here_o[0, :, cut] = rounded[:length]
            send_o[0, :, cut] = rounded[length:].astype(F32)
        den_o[0] = dens

    outs = [
        shaped(rows, chip_len, mine),
        shaped(rows, chip_len, 128),
        shaped(rows, length, mine, dtype=BF),
        shaped(rows, length, mine),
    ]
    inputs = [fq, num, den, own, got, idc, idr]
    return row_call(
        kernel, "attend", info, inputs, [per_row(v) for v in inputs], outs,
        flops=rows * chip_len * mine * m * 6,
    )


def grads_one_kernel(info, go, go_got, out_weight, att, den, fq, idc, idr):
    rows, length, width = go.shape
    heads, m = fq.shape[1], fq.shape[3]
    mine = width // 2
    e = mine // heads
    n = heads // 2 * e + 8
    spare = heads // 2 * e + heads // 2

    def kernel(info_ref, go_r, gog_r, wo_r, att_r, den_r, fq_r, idc_r, idr_r, dn_o, dd_o, keep, send):
        chip = jnp.concatenate([go_r[0], gog_r[0].astype(BF)], 0)
        pulls = mm_nt(chip, wo_r[...])
        lead, tail, first, last = edges(idc_r, idr_r)
        lead, tail = lead.astype(F32), tail.astype(F32)
        lane = lax.broadcasted_iota(jnp.int32, (2 * length, 128), 1)
        dds = jnp.zeros((2 * length, 128), F32)
        for h in range(heads):
            cut = slice(h * e, (h + 1) * e)
            denom = den_r[0, :, h : h + 1]
            pull = pulls[:, cut]
            dn = (pull / denom).astype(BF)
            dn_o[0, :, cut] = dn
            dd = -jnp.sum(pull * att_r[0, :, cut], -1, keepdims=True) / denom
            dds = jnp.where(lane == h, dd, dds)
            wide = dn.astype(F32)
            sums = mm_tn(jnp.concatenate([wide * lead, wide * tail], 1).astype(BF), fq_r[0, h])
            high = dd.astype(BF).astype(F32)
            low = dd - high
            four = jnp.concatenate([high * lead, low * lead, high * tail, low * tail], 1)
            zs = mm_tn(four.astype(BF), fq_r[0, h])
            put_edges(info_ref, keep, send, h, heads, sums, zs[0:1] + zs[1:2], zs[2:3] + zs[3:4])
        dd_o[0] = dds
        put_tags(keep, send, spare, first, last)

    outs = [
        shaped(rows, 2 * length, mine, dtype=BF),
        shaped(rows, 2 * length, 128),
        shaped(rows, 2, n, m),
        shaped(rows, 2, n, m),
    ]
    specs = [
        per_row(go), per_row(go_got),
        pl.BlockSpec((mine, width), lambda r, info: (info[0], 0)),
        per_row(att), per_row(den), per_row(fq), per_row(idc), per_row(idr),
    ]
    return row_call(
        kernel, "grads_one", info, [go, go_got, out_weight, att, den, fq, idc, idr], specs, outs,
        flops=rows * length * width * mine * 6,
    )


def pulled_back(grad_feat, feat, part, feats):
    e = feats.shape[0]
    weighted = grad_feat * feat.astype(F32)
    inner = (weighted * e ** (-0.25)).astype(BF)
    folded = jnp.sum(weighted, -1, keepdims=True) * e ** (-0.5)
    return (mm_nt(inner, feats) - part.astype(F32) * folded).astype(BF)


def grads_two_kernel(info, fq, fk, queries, values, dn, dd, features, own, got, idc, idr, deps=()):
    rows, heads, chip_len, m = fq.shape
    mine = queries.shape[2]
    e = mine // heads

    def kernel(
        info_ref, fq_r, fk_r, q_r, v_r, dn_r, dd_r, f_r, own_r, got_r, idc_r, idr_r, dq_o, dfk_o, dv_o
    ):
        same = idc_r[0] == idr_r[0]
        lead, tail, _, _ = edges(idc_r, idr_r)
        lead, tail = lead.astype(F32), tail.astype(F32)
        for h in range(heads):
            cut = slice(h * e, (h + 1) * e)
            feat_q, feat_k = fq_r[0, h], fk_r[0, h]
            part, value = dn_r[0, :, cut], v_r[0, :, cut]
            denom = dd_r[0, :, h : h + 1]
            scores = jnp.where(same, mm_nt(feat_q, feat_k), 0.0).astype(BF)
            pulls = jnp.where(same, mm_nt(part, value) + denom, 0.0).astype(BF)
            dv_o[0, :, cut] = mm_tn(scores, part)
            dfk_o[0, h] = mm_tn(pulls, feat_q)
            before, behind, zb, za = carry_of(info_ref, own_r, got_r, h, heads, e)
            wide = part.astype(F32)
            both = jnp.concatenate([wide * lead, wide * tail], 1).astype(BF)
            grad = (
                mm(pulls, feat_k)
                + mm(both, jnp.concatenate([before, behind], 0).astype(BF))
                + denom * (lead * zb + tail * za)
            )
            dq_o[0, :, cut] = pulled_back(grad, feat_q, q_r[0, :, cut], f_r[h])

    outs = [
        shaped(rows, chip_len, mine, dtype=BF),
        shaped(rows, heads, chip_len, m),
        shaped(rows, chip_len, mine),
    ]
    inputs = [fq, fk, queries, values, dn, dd, features, own, got, idc, idr]
    specs = [per_row(v) for v in inputs]
    specs[6] = head_features(features, heads)
    return row_call(
        kernel, "grads_two", info, inputs, specs, outs, deps, flops=rows * chip_len * chip_len * mine * 30
    )


def grads_three_kernel(info, fk, keys, values, dfk, dv, features, own, got, idc, idr, deps=()):
    rows, heads, chip_len, m = fk.shape
    mine = keys.shape[2]
    e = mine // heads

    def kernel(
        info_ref, fk_r, k_r, v_r, dfk_r, dv_r, f_r, own_r, got_r, idc_r, idr_r, dk_o, dv_o
    ):
        lead, tail, _, _ = edges(idc_r, idr_r)
        lead, tail = lead.astype(F32), tail.astype(F32)
        for h in range(heads):
            cut = slice(h * e, (h + 1) * e)
            feat = fk_r[0, h]
            before, behind, zb, za = carry_of(info_ref, own_r, got_r, h, heads, e)
            kv = jnp.concatenate([before, behind], 0).astype(BF)
            wide = v_r[0, :, cut].astype(F32)
            both = jnp.concatenate([wide * lead, wide * tail], 1).astype(BF)
            grad = dfk_r[0, h] + mm(both, kv) + (lead * zb + tail * za)
            dk_o[0, :, cut] = pulled_back(grad, feat, k_r[0, :, cut], f_r[h])
            more = mm_nt(feat, kv)
            total_v = dv_r[0, :, cut] + lead * more[:, :e] + tail * more[:, e:]
            dv_o[0, :, cut] = total_v.astype(BF)

    outs = [shaped(rows, chip_len, mine, dtype=BF), shaped(rows, chip_len, mine, dtype=BF)]
    inputs = [fk, keys, values, dfk, dv, features, own, got, idc, idr]
    specs = [per_row(v) for v in inputs]
    specs[5] = head_features(features, heads)
    return row_call(
        kernel, "grads_three", info, inputs, specs, outs, deps, flops=rows * chip_len * m * mine * 8
    )


def shares_kernel(info, dq, dk, dv, query_weight, key_weight, value_weight, deps=()):
    rows, chip_len, mine = dq.shape
    width = query_weight.shape[0]
    length = chip_len // 2

    def kernel(info_ref, dq_r, dk_r, dv_r, wq_r, wk_r, wv_r, here_o, send_o):
        total_x = (
            mm_nt(dq_r[0], wq_r[...]) + mm_nt(dk_r[0], wk_r[...]) + mm_nt(dv_r[0], wv_r[...])
        )
        here_o[0] = total_x[:length]
        send_o[0] = total_x[length:]

    outs = [shaped(rows, length, width), shaped(rows, length, width)]
    specs = [per_row(dq), per_row(dk), per_row(dv)] + [
        weight_columns(w, mine) for w in (query_weight, key_weight, value_weight)
    ]
    return row_call(
        kernel, "shares", info, [dq, dk, dv, query_weight, key_weight, value_weight], specs, outs, deps,
        flops=rows * chip_len * mine * width * 6,
    )


def norm(hidden):
    mean = jnp.mean(hidden, -1, keepdims=True)
    centered = hidden - mean
    variance = jnp.mean(centered * centered, -1, keepdims=True)
    inv_std = lax.rsqrt(variance + EPSILON)
    return centered * inv_std, inv_std


def norm_back(upstream, normed, inv_std, gain):
    scaled = upstream * gain
    return inv_std * (
        scaled
        - jnp.mean(scaled, -1, keepdims=True)
        - normed * jnp.mean(scaled * normed, -1, keepdims=True)
    )


def put_sums(ref, upstream, normed):
    ref[...] = jnp.zeros_like(ref)
    ref[0:1, :] = jnp.sum(upstream * normed, 0, keepdims=True)
    ref[1:2, :] = jnp.sum(upstream, 0, keepdims=True)


def ffn_chunk(j, info, chunks):
    return lax.rem(j + (1 - info[0]) * (chunks // 2), chunks)


def ffn_forward(info, x, att, att_got, out_weight, first, up, down, second, cot, chunks=2):
    count, width = x.shape
    mine = att.shape[1]
    ff = up.shape[1]
    size = ff // chunks
    half = chunks // 2

    def kernel(
        info_ref, x_r, att_r, attg_r, wo_r, wog_r, first_r, up_r, down_r, second_r, cot_r,
        y_o, ys_o, here_o, send_o, slope_o, out_o, dz_o, dzs_o, dh_o, unit_o, inv_o, sums_o, y_s, acc,
    ):
        j = pl.program_id(0)

        @pl.when(j == 0)
        def _():
            hidden = (
                x_r[...].astype(F32)
                + mm(att_r[...], wo_r[...])
                + mm(attg_r[...].astype(BF), wog_r[...])
            )
            normed, inv_std = norm(hidden)
            unit_o[...] = normed
            inv_o[...] = jnp.broadcast_to(inv_std, inv_o.shape)
            y = normed * first_r[0:1, :] + first_r[1:2, :]
            acc[...] = y
            y_s[...] = y.astype(BF)
            y_o[...] = y_s[...]
            ys_o[...] = y_s[...].astype(F32)

        inner = mm(y_s[...], up_r[...])
        bell = 0.5 * (1.0 + lax.erf(inner * 0.7071067811865476))
        slope_o[...] = bell + inner * (jnp.exp(-0.5 * inner * inner) * 0.3989422804014327)
        act = (inner * bell).astype(BF)

        @pl.when(j < half)
        def _():
            send_o[...] = act.astype(F32)

        @pl.when(j >= half)
        def _():
            here_o[...] = act

        acc[...] += mm(act, down_r[...])

        @pl.when(j == chunks - 1)
        def _():
            normed, inv_std = norm(acc[...])
            gain = second_r[0:1, :]
            out_o[...] = (normed * gain + second_r[1:2, :]).astype(BF)
            upstream = cot_r[...].astype(F32)
            put_sums(sums_o, upstream, normed)
            grad = norm_back(upstream, normed, inv_std, gain)
            dh_o[...] = grad
            dz_o[...] = grad.astype(BF)
            dzs_o[...] = grad.astype(BF).astype(F32)

    def whole(array):
        return pl.BlockSpec(array.shape, lambda j, info: (0, 0))

    flat = pl.BlockSpec((count, width), lambda j, info: (0, 0))
    outs = [
        (shaped(count, width, dtype=BF), flat),
        (shaped(count, width), flat),
        (shaped(count, ff // 2, dtype=BF), pl.BlockSpec((count, size), lambda j, info: (0, jnp.maximum(j - half, 0)))),
        (shaped(count, ff // 2), pl.BlockSpec((count, size), lambda j, info: (0, jnp.minimum(j, half - 1)))),
        (shaped(count, ff), pl.BlockSpec((count, size), lambda j, info: (0, j))),
        (shaped(count, width, dtype=BF), flat),
        (shaped(count, width, dtype=BF), flat),
        (shaped(count, width), flat),
        (shaped(count, width), flat),
        (shaped(count, width), flat),
        (shaped(count, 128), pl.BlockSpec((count, 128), lambda j, info: (0, 0))),
        (shaped(8, width), pl.BlockSpec((8, width), lambda j, info: (0, 0))),
    ]
    return pl.pallas_call(
        kernel,
        grid_spec=pltpu.PrefetchScalarGridSpec(
            num_scalar_prefetch=1,
            grid=(chunks,),
            in_specs=[
                whole(x), whole(att), whole(att_got),
                pl.BlockSpec((mine, width), lambda j, info: (info[0], 0)),
                pl.BlockSpec((mine, width), lambda j, info: (1 - info[0], 0)),
                whole(first),
                pl.BlockSpec((width, size), lambda j, info: (0, ffn_chunk(j, info, chunks))),
                pl.BlockSpec((size, width), lambda j, info: (ffn_chunk(j, info, chunks), 0)),
                whole(second), whole(cot),
            ],
            out_specs=[spec for _, spec in outs],
            scratch_shapes=[pltpu.VMEM((count, width), BF), pltpu.VMEM((count, width), F32)],
        ),
        out_shape=[shape for shape, _ in outs],
        compiler_params=pltpu.CompilerParams(vmem_limit_bytes=ROOM),
        cost_estimate=cost("ffn_forward"),
        name="ffn_forward",
    )(info, x, att, att_got, out_weight, out_weight, first, up, down, second, cot)


def ffn_inner(info, dz, down, slope, chunks=2):
    count, width = dz.shape
    ff = down.shape[0]
    size = ff // chunks
    half = chunks // 2

    def kernel(info_ref, dz_r, down_r, slope_r, here_o, send_o):
        j = pl.program_id(0)
        grad = (mm_nt(dz_r[...], down_r[...]) * slope_r[...]).astype(BF)

        @pl.when(j < half)
        def _():
            send_o[...] = grad.astype(F32)

        @pl.when(j >= half)
        def _():
            here_o[...] = grad

    return pl.pallas_call(
        kernel,
        grid_spec=pltpu.PrefetchScalarGridSpec(
            num_scalar_prefetch=1,
            grid=(chunks,),
            in_specs=[
                pl.BlockSpec((count, width), lambda j, info: (0, 0)),
                pl.BlockSpec((size, width), lambda j, info: (ffn_chunk(j, info, chunks), 0)),
                pl.BlockSpec((count, size), lambda j, info: (0, j)),
            ],
            out_specs=[
                pl.BlockSpec((count, size), lambda j, info: (0, jnp.maximum(j - half, 0))),
                pl.BlockSpec((count, size), lambda j, info: (0, jnp.minimum(j, half - 1))),
            ],
        ),
        out_shape=[shaped(count, ff // 2, dtype=BF), shaped(count, ff // 2)],
        compiler_params=pltpu.CompilerParams(vmem_limit_bytes=ROOM),
        cost_estimate=cost("ffn_inner"),
        name="ffn_inner",
    )(info, dz, down, slope)


def ffn_back(info, here, send, up, dh, unit, inv, first, deps=(), chunks=2):
    count, width = dh.shape
    ff = up.shape[1]
    size = ff // chunks
    half = chunks // 2

    def kernel(info_ref, here_r, send_r, up_r, dh_r, unit_r, inv_r, first_r, *rest):
        dh_o, go_o, gos_o, sums_o, acc = rest[len(deps) :]
        j = pl.program_id(0)

        @pl.when(j == 0)
        def _():
            acc[...] = dh_r[...]

        @pl.when(j < half)
        def _():
            acc[...] += mm_nt(send_r[...].astype(BF), up_r[...])

        @pl.when(j >= half)
        def _():
            acc[...] += mm_nt(here_r[...], up_r[...])

        @pl.when(j == chunks - 1)
        def _():
            upstream, normed = acc[...], unit_r[...]
            put_sums(sums_o, upstream, normed)
            grad = norm_back(upstream, normed, inv_r[:, 0:1], first_r[0:1, :])
            dh_o[...] = grad
            go_o[...] = grad.astype(BF)
            gos_o[...] = grad.astype(BF).astype(F32)

    def whole(array):
        return pl.BlockSpec(array.shape, lambda j, info: (0, 0))

    flat = pl.BlockSpec((count, width), lambda j, info: (0, 0))
    return pl.pallas_call(
        kernel,
        grid_spec=pltpu.PrefetchScalarGridSpec(
            num_scalar_prefetch=1,
            grid=(chunks,),
            in_specs=[
                pl.BlockSpec((count, size), lambda j, info: (0, jnp.maximum(j - half, 0))),
                pl.BlockSpec((count, size), lambda j, info: (0, jnp.minimum(j, half - 1))),
                pl.BlockSpec((width, size), lambda j, info: (0, ffn_chunk(j, info, chunks))),
                whole(dh), whole(unit), whole(inv), whole(first),
            ] + [ANY] * len(deps),
            out_specs=[flat, flat, flat, pl.BlockSpec((8, width), lambda j, info: (0, 0))],
            scratch_shapes=[pltpu.VMEM((count, width), F32)],
        ),
        out_shape=[
            shaped(count, width), shaped(count, width, dtype=BF), shaped(count, width), shaped(8, width)
        ],
        compiler_params=pltpu.CompilerParams(vmem_limit_bytes=ROOM),
        cost_estimate=cost("ffn_back"),
        name="ffn_back",
    )(info, here, send, up, dh, unit, inv, first, *deps)


def tag_of(ref, k, spare):
    return ref[0, k, spare : spare + 1, 0:1]


def ordered(info_ref, mine, theirs):
    one = info_ref[1] == 1

    def chip(at, k):
        here = one if at else jnp.logical_not(one)
        return jnp.where(here, mine[0, k], theirs[0, k])

    return [[chip(at, k) for k in (0, 1)] for at in (0, 1)]


def join_plane(info, mine, theirs, spare, deps=()):
    rows, _, n, m = mine.shape

    def kernel(info_ref, mine_r, theirs_r, up_o, down_o):
        (lead0, tail0), (lead1, tail1) = ordered(info_ref, mine_r, theirs_r)

        def tag(part):
            return part[spare : spare + 1, 0:1]

        is_sum = lax.broadcasted_iota(jnp.int32, (n, m), 0) < spare
        up_o[0] = tail1 + jnp.where(is_sum & (tag(tail0) == tag(tail1)), tail0, 0.0)
        down_o[0] = lead0 + jnp.where(is_sum & (tag(lead1) == tag(lead0)), lead1, 0.0)

    outs = [shaped(rows, n, m), shaped(rows, n, m)]
    return row_call(kernel, "join_plane", info, [mine, theirs], [per_row(mine)] * 2, outs, deps)


def split_plane(info, mine, theirs, ups, downs, spare):
    rows, _, n, m = mine.shape
    steps = len(ups)

    def kernel(info_ref, mine_r, theirs_r, *refs):
        give_o, own_o = refs[2 * steps :]
        (lead0, tail0), (lead1, tail1) = ordered(info_ref, mine_r, theirs_r)

        def tag(part):
            return part[spare : spare + 1, 0:1]

        before = jnp.zeros((n, m), F32)
        behind = jnp.zeros((n, m), F32)
        for k in range(steps):
            up, down = refs[k][0], refs[steps + k][0]
            before = before + jnp.where(tag(up) == tag(lead0), up, 0.0)
            behind = behind + jnp.where(tag(down) == tag(tail1), down, 0.0)
        behind0 = jnp.where(tag(tail0) == tag(lead1), lead1, 0.0) + jnp.where(
            tag(tail0) == tag(tail1), behind, 0.0
        )
        before1 = jnp.where(tag(lead1) == tag(tail0), tail0, 0.0) + jnp.where(
            tag(lead1) == tag(lead0), before, 0.0
        )
        one = info_ref[1] == 1
        give_o[0, 0] = jnp.where(one, before, before1)
        give_o[0, 1] = jnp.where(one, behind0, behind)
        own_o[0, 0] = jnp.where(one, before1, before)
        own_o[0, 1] = jnp.where(one, behind, behind0)

    inputs = [mine, theirs, *ups, *downs]
    outs = [shaped(rows, 2, n, m), shaped(rows, 2, n, m)]
    return row_call(kernel, "split_plane", info, inputs, [per_row(v) for v in inputs], outs)


def exchange(net, info, keep, send, ids_row, chip_len, spare, late=()):
    if not net.fast:
        first, last = jnp.min(ids_row, 2), jnp.max(ids_row, 2)
        pay = jnp.stack([keep, send], 1)
        up, down = pay[:, :, 1], pay[:, :, 0]
        before = jnp.zeros_like(up)
        behind = jnp.zeros_like(up)
        for _ in range(min(net.n_seq // 2 - 1, -(-SEG_MOST // chip_len))):
            up, down = net.shift(up, 1), net.shift(down, -1)
            reached = up[:, 0, spare, 0:1] == first
            before = before + jnp.where(reached[:, :, None, None], up, 0.0)
            reached = down[:, 0, spare, 0:1] == last
            behind = behind + jnp.where(reached[:, :, None, None], down, 0.0)
        return jnp.stack([before[:, 0], behind[:, 0]], 1), jnp.stack([before[:, 1], behind[:, 1]], 1)
    theirs = net.over_x(send)
    up, down = join_plane(info, keep, theirs, spare, late[0] if late else ())
    ups, downs = [], []
    for _ in range(min(net.nz - 1, -(-SEG_MOST // (2 * chip_len)))):
        up, down = net.z_up(up), net.z_down(down)
        ups.append(up)
        downs.append(down)
    if late:
        late[1].extend([ups[0], downs[0]])
    give, own = split_plane(info, keep, theirs, ups, downs, spare)
    if late:
        late[2].append(own)
    return own, net.over_x(give)


def body(
    tokens,
    segment_ids,
    features,
    query_weight,
    key_weight,
    value_weight,
    out_weight,
    up_weight,
    down_weight,
    first_gain,
    first_bias,
    second_gain,
    second_bias,
    cotangent,
):
    CALLS.clear()
    net = Net(lax.axis_size("dp"), lax.axis_size("seq"))
    rows, length, width = tokens.shape
    heads_all, head_dim, _ = features.shape
    heads = heads_all // 2
    mine = width // 2
    ff = up_weight.shape[1]
    ff_half = ff // 2
    core = net.core
    fast = net.fast
    chip_len = 2 * length
    count = rows * length
    spare = heads // 2 * head_dim + heads // 2
    side = net.x if fast else jnp.zeros_like(core)
    info = jnp.stack([core, side]).astype(jnp.int32)

    tokens_got = net.over_core(tokens.astype(F32))
    ids = segment_ids.astype(F32)
    ids_chip = jnp.concatenate([ids, net.over_core(ids)], 1)
    idr, idc = ids_chip[:, None, :], ids_chip[:, :, None]

    keys, values, fk, keep, send = keys_kernel(
        info, tokens, tokens_got, key_weight, value_weight, features, idc, idr
    )
    queries, fq, num, den = queries_kernel(
        info, tokens, tokens_got, query_weight, features, fk, values, idc, idr
    )
    own, got = exchange(net, info, keep, send, idr, chip_len, spare)
    att, den, att_here, att_send = attend_kernel(info, fq, num, den, own, got, idc, idr)
    att_got = net.over_core(att_send).reshape(count, mine)

    flat = tokens.reshape(count, width)
    first = jnp.stack([first_gain, first_bias])
    second = jnp.stack([second_gain, second_bias])
    (
        y1, y1_send, act, act_send, slope, result, dz, dz_send, dh2, unit, inv, sums_two
    ) = ffn_forward(
        info, flat, att_here.reshape(count, mine), att_got, out_weight, first,
        up_weight, down_weight, second, cotangent.reshape(count, width),
    )
    y1_got = net.over_core(y1_send)
    act_got = net.over_core(act_send)
    dz_got = net.over_core(dz_send)
    df, df_send = ffn_inner(info, dz, down_weight, slope)
    df_got = net.over_core(df_send)

    one = jnp.where(net.seq < 0, 0.5, 1.0).astype(F32)

    def rounded(wide):
        return (wide * one).astype(BF)

    def both(a, b):
        return jnp.concatenate([a, rounded(b)], 0)

    deps = ()
    if fast:
        bits_mine = stage_bits(net, 0)
        down_parts = (act, act_got, dz, dz_got)
        up_parts = (y1, y1_got, df, df_got)
        f_sends = down_products(1 - bits_mine, *down_parts, deps=[df])
        f_sends = up_products(1 - bits_mine, *up_parts, f_sends)
        deps = f_sends[1:]
    else:
        grad_up = total(net, mm_tn(both(y1, y1_got), both(df, df_got)), 1)
        grad_down = total(net, mm_tn(both(act, act_got), both(dz, dz_got)), 0)

    dh1, go, go_send, sums_one = ffn_back(
        info, df, df_send, up_weight, dh2, unit, inv, first, deps
    )
    go_got = net.over_core(go_send)
    dn, dd, keep_d, send_d = grads_one_kernel(
        info, go.reshape(rows, length, width), go_got.reshape(rows, length, width), out_weight,
        att, den, fq, idc, idr,
    )
    late = []
    if fast:
        f_gots = moves(net, f_sends, 0)
        f_keeps = down_products(bits_mine, *down_parts, deps=[go])
        f_keeps = up_products(bits_mine, *up_parts, f_keeps)
        f_sends, f_keeps = add_stage(net, f_keeps, f_gots, 1, [send_d])
        late = [[f_sends[1]], [], []]
    own_d, got_d = exchange(net, info, keep_d, send_d, idr, chip_len, spare, late)
    dq, dfk, dv = grads_two_kernel(
        info, fq, fk, queries, values, dn, dd, features, own, got, idc, idr, deps=late[2] if fast else ()
    )
    if fast:
        f_gots = [
            stage_move(net, f_sends[0], 0, 1), stage_move(net, tie(f_sends[1], *late[1]), 1, 1)
        ]
        f_sends, f_keeps = add_stage(net, f_keeps, f_gots, 2, [dq])
        f_gots = moves(net, f_sends, 2)
    dk, dv = grads_three_kernel(
        info, fk, keys, values, dfk, dv, features, own_d, got_d, idc, idr, deps=f_sends[1:] if fast else ()
    )

    chip_flat = (rows * chip_len, mine)
    if fast:
        sums = jnp.concatenate([sums_one[:2], sums_two[:2]])
        small = (sums + net.over_core(sums)).reshape(8, mine)
        attn_parts = (
            flat, tokens_got.reshape(count, width),
            dq.reshape(chip_flat), dk.reshape(chip_flat), dv.reshape(chip_flat),
            att.reshape(chip_flat), go, go_got, small,
        )

        def over_core(parts):
            return [net.over_core(part) for part in parts]

        a_sends = attn_products(1 - bits_mine, *attn_parts)
        a_gots = moves(net, a_sends, 0)
        a_keeps = attn_products(bits_mine, *attn_parts, deps=a_sends)
        f_sends, f_keeps = add_stage(net, f_keeps, f_gots, 3, a_keeps)
        f_gots = moves(net, f_sends, 3)
        f_own = last_add(f_keeps, f_gots)
        f_gots = moves(net, f_own, 3)
        f_own = join_stage(net, f_own, f_gots, 3)
        f_gots = moves(net, f_own, 2)
        a_sends, a_keeps = add_stage(net, a_keeps, a_gots, 1, f_own[1:])
        a_gots = moves(net, a_sends, 1)
        a_sends, a_keeps = add_stage(net, a_keeps, a_gots, 2)
        a_gots = moves(net, a_sends, 2)
        f_one = join_stage(net, f_own, f_gots, 2, a_sends)
        f_two = moves(net, f_one, 1)
        a_sends, a_keeps = add_stage(net, a_keeps, a_gots, 3, f_one[1:])
        a_gots = moves(net, a_sends, 3)
        f_one_core = over_core([tie(part, *a_sends) for part in f_one])
        shapes = [shaped(*w.shape) for w in (up_weight, down_weight)]
        copies = ffn_copies(width, ff_half)
        outs, done = place_pieces(
            net, [(f_one, 0, 0, 0), (f_one_core, 1, 0, 0)], shapes, copies, a_sends
        )
        a_keeps = [tie(a_keeps[0], *f_two)]
        a_own = last_add(a_keeps, a_gots, done)
        a_gots = moves(net, a_own, 3)
        f_three = moves(net, f_one, 0)
        a_own = join_stage(net, a_own, a_gots, 3, done)
        a_gots = moves(net, a_own, 2)
        f_two_core = over_core(f_two)
        outs, done = place_pieces(
            net, [(f_two, 0, 0, 1), (f_two_core, 1, 0, 1)], outs, copies, a_own
        )
        f_four = moves(net, f_two, 0)
        a_one = join_stage(net, a_own, a_gots, 2, done)
        a_two = moves(net, a_one, 1)
        a_three = moves(net, a_one, 0)
        f_three_core = over_core(f_three)
        outs, done = place_pieces(
            net, [(f_three, 0, 1, 0), (f_three_core, 1, 1, 0)], outs, copies, a_one
        )
        here, share_send = shares_kernel(
            info, dq, dk, dv, query_weight, key_weight, value_weight, deps=done
        )
        a_four = moves(net, a_two, 0)
        f_four_core = over_core(f_four)
        a_one_core = over_core(a_one)
        (grad_up, grad_down), done = place_pieces(
            net, [(f_four, 0, 1, 1), (f_four_core, 1, 1, 1)], outs, copies, [share_send]
        )
        shapes = [shaped(width, width)] * 4
        copies = attn_copies(mine)
        a_two_core = over_core(a_two)
        outs, done = place_pieces(
            net,
            [(a_one, 0, 0, 0), (a_one_core, 1, 0, 0), (a_two, 0, 0, 1), (a_two_core, 1, 0, 1)],
            shapes, copies, done,
        )
        a_three_core = over_core(a_three)
        outs, done = place_pieces(
            net, [(a_three, 0, 1, 0), (a_three_core, 1, 1, 0)], outs, copies, done
        )
        a_four = [tie(part, *done) for part in a_four]
        outs, done = place_pieces(net, [(a_four, 0, 1, 1)], outs, copies)
        (grad_query, grad_key, grad_value, grad_out), _ = place_pieces(
            net, [(over_core(a_four), 1, 1, 1)], outs, copies
        )
        at = 4 * mine - (4 * mine + SPARE_ROWS) // 2
        one, two = a_one[0][at : at + 8], a_two[0][at : at + 8]
        small = jnp.where(stage_bit(net, 0, 1, core) == 1, one, two).reshape(4, width)
    else:
        x_chip = jnp.concatenate([tokens, rounded(tokens_got)], 1).reshape(rows * chip_len, width)
        go_chip = jnp.concatenate(
            [go.reshape(rows, length, width), rounded(go_got).reshape(rows, length, width)], 1
        ).reshape(rows * chip_len, width)
        grad_query = total(net, mm_tn(x_chip, dq.reshape(chip_flat)), 1)
        grad_key = total(net, mm_tn(x_chip, dk.reshape(chip_flat)), 1)
        grad_value = total(net, mm_tn(x_chip, dv.reshape(chip_flat)), 1)
        grad_out = total(net, mm_tn(att.astype(BF).reshape(chip_flat), go_chip), 0)

        here, share_send = shares_kernel(info, dq, dk, dv, query_weight, key_weight, value_weight)
        small = lax.psum(jnp.concatenate([sums_one[:2], sums_two[:2]]), AXES)

    grad_input = dh1.reshape(rows, length, width) + here + net.over_core(share_send)
    return (
        result.reshape(rows, length, width),
        grad_input.astype(BF),
        grad_query,
        grad_key,
        grad_value,
        grad_out,
        grad_up,
        grad_down,
        small[0],
        small[1],
        small[2],
        small[3],
    )


def solution(mesh):
    split = P("dp", "seq", None)
    placed = (split, P("dp", "seq")) + (P(),) * 11 + (split,)
    return jax.shard_map(
        body,
        mesh=mesh,
        in_specs=placed,
        out_specs=(split, split) + (P(),) * 10,
        check_vma=False,
    )
```
